256 devices in a mesh: dp: 32 (over z, y), ha: 2 (over x_lo), wa: 4 (over x_hi, core).
Axes of the slice: x: 4 (x_hi: 2, x_lo: 2; x = x_hi * 2 + x_lo), y: 4, z: 8, core: 2. Of those that a mesh axis runs over, the one named last changes fastest.
Arguments:
- activations: bfloat16 [32, 4, 24, 64, 256], P('dp', None, 'ha', 'wa'), may hold values from -6 to 6
- saved_hidden: bfloat16 [32, 4, 24, 64, 256], P('dp', None, 'ha', 'wa'), may hold values from -6 to 6
- cotangent: bfloat16 [32, 4, 24, 64, 256], P('dp', None, 'ha', 'wa'), may hold values from -6 to 6
- conv_one: bfloat16 [256, 3, 3, 3, 256], replicated, may hold values from -0.078125 to 0.078125
- conv_two: bfloat16 [256, 3, 3, 3, 256], replicated, may hold values from -0.078125 to 0.078125
- film_table: float32 [1000, 512], replicated, may hold values from -3 to 3
- timesteps: int32 [32], P('dp'), may hold values from 0 to 999
Outputs:
- grad_input: bfloat16 [32, 4, 24, 64, 256], P('dp', None, 'ha', 'wa')
- grad_conv_one: float32 [256, 3, 3, 3, 256], P(('ha', 'wa'), None, None, None, 'dp')
- grad_conv_two: float32 [256, 3, 3, 3, 256], P(('ha', 'wa'), None, None, None, 'dp')
The draws below stay inside these ranges and needn't reach their ends.
All inputs are finite; a program needn't handle non-finite values.
Results may differ from the reference program's by a relative error of at most 0.003.
Values may be sent and summed in bfloat16 or wider, within the bound.
No kernel may reach another device: no remote copies, remote signals or barrier semaphores. Data moves between devices by JAX's collectives and lax.ppermute only.
A program may use at most 320 MiB of HBM per device.

```python
import jax
import jax.numpy as jnp
from jax import lax

C = 256
FRAMES = 4
TSTEPS = 1000
CLIPS = 32
HEIGHT = 24
WIDTH = 64


def plant(values, key, smallest, largest):
    longest = values.shape.index(max(values.shape))
    spots = []
    for shift in (0, 1):
        where = [jax.random.randint(jax.random.fold_in(key, axis), (), 0, length) for axis, length in enumerate(values.shape)]
        where[longest] = (where[longest] + shift) % values.shape[longest]
        spots.append(tuple(where))
    return values.at[spots[0]].set(smallest).at[spots[1]].set(largest)


def raised(array, stream_key, source, target, blocks, factor):
    owner, partner = [(jnp.arange(array.shape[position]) // (array.shape[position] // blocks)).reshape([-1 if axis == position else 1 for axis in range(array.ndim)]) for position in (source, target)]
    chosen = jax.random.permutation(stream_key, blocks)[partner]
    strong = (owner == chosen) | (owner == (partner + blocks // 2) % blocks)
    return jnp.where(strong, factor * array, array)


def shard_levels(key, dims, cuts, smallest, high):
    def one(position, parts):
        draws = jax.random.uniform(jax.random.fold_in(jax.random.fold_in(key, 6), position), (parts,), jnp.float32, smallest / len(cuts), high / len(cuts))
        return jnp.repeat(jnp.exp(draws), dims[position] // parts).reshape((-1,) + (1,) * (len(dims) - position - 1))

    gain = one(*cuts[0])
    for cut in cuts[1:]:
        gain = gain * one(*cut)
    return gain


def normal_values(own_key, extent, deviation, limit, split=(), held_as=jnp.bfloat16):
    array = jax.random.normal(own_key, extent, jnp.float32) * deviation
    if len(split) > 0:
        array = shard_levels(own_key, extent, split, -0.22, 0.18) * array
    return jnp.clip(array, min=-limit, max=limit).astype(held_as)


def noise_with(rng, extent, deviation, reach, pieces, heavy, dtype=jnp.bfloat16):
    entries = deviation * jax.random.normal(rng, extent, jnp.float32)
    if pieces:
        entries = entries * shard_levels(rng, extent, pieces, -0.22, 0.18)
    return jnp.clip(raised(entries, jax.random.fold_in(rng, 3), *heavy), -reach, reach).astype(dtype)


def setup_inputs(seed: int = 0) -> dict:
    key_list = jax.random.split(jax.random.key(seed), 8)
    return {
        "activations": normal_values(key_list[0], (CLIPS, FRAMES, HEIGHT, WIDTH, C), 1.0, 6.0, ((0, 32), (2, 2), (3, 4))),
        "saved_hidden": normal_values(key_list[1], (CLIPS, FRAMES, HEIGHT, WIDTH, C), 1.0, 6.0, ((0, 32), (2, 2), (3, 4))),
        "cotangent": noise_with(key_list[2], (CLIPS, FRAMES, HEIGHT, WIDTH, C), 1.0, 6.0, ((0, 32), (2, 2), (3, 4)), (0, 4, 32, 2.75)),
        "conv_one": normal_values(key_list[3], (C, 3, 3, 3, C), (27 * C) ** -0.5, 0.078125),
        "conv_two": normal_values(key_list[4], (C, 3, 3, 3, C), (27 * C) ** -0.5, 0.078125),
        "film_table": normal_values(key_list[5], (TSTEPS, 2 * C), 0.5, 3.0, (), jnp.float32),
        "timesteps": plant(jax.random.randint(key_list[6], (CLIPS,), 0, TSTEPS), jax.random.fold_in(key_list[6], 1), 0, TSTEPS - 1).astype(jnp.int32),
    }


def weight_grad(padded_in, cotan_in):
    num_frames, num_rows, num_cols, outs_count = cotan_in.shape
    cot_rows = cotan_in.reshape(-1, outs_count)
    blocks_list = []
    for offset in range(27):
        tshift, hshift, wshift = (offset // 9, offset // 3 % 3, offset % 3)
        window = padded_in[tshift:tshift + num_frames, hshift:hshift + num_rows, wshift:wshift + num_cols]
        window = window.reshape(-1, padded_in.shape[-1])
        blocks_list.append(lax.dot_general(window, cot_rows, (((0,), (0,)), ((), ())), preferred_element_type=jnp.float32))
    return jnp.stack(blocks_list, 1).reshape(padded_in.shape[-1], 3, 3, 3, outs_count)

def conv_transpose(padded_cot, weight):
    num_frames = padded_cot.shape[0] - 2
    num_rows = padded_cot.shape[1] - 2
    num_cols = padded_cot.shape[2] - 2
    accum_sum = jnp.zeros((num_frames * num_rows * num_cols, weight.shape[0]), jnp.float32)
    for offset in range(27):
        tshift, hshift, wshift = (offset // 9, offset // 3 % 3, offset % 3)
        window = padded_cot[2 - tshift:2 - tshift + num_frames, 2 - hshift:2 - hshift + num_rows, 2 - wshift:2 - wshift + num_cols]
        window = window.reshape(-1, padded_cot.shape[-1])
        accum_sum = accum_sum + lax.dot_general(window, weight[:, tshift, hshift, wshift, :], (((1,), (1,)), ((), ())), preferred_element_type=jnp.float32)
    return accum_sum.reshape(num_frames, num_rows, num_cols, weight.shape[0])

def reference(activations, saved_hidden, cotangent, conv_one, conv_two, film_table, timesteps):
    one_hot = (lax.broadcasted_iota(jnp.int32, (CLIPS, TSTEPS), 1) == timesteps[:, None]).astype(jnp.float32)
    film_rows = jnp.dot(one_hot, film_table, precision=lax.Precision.HIGHEST, preferred_element_type=jnp.float32)

    def one_clip(running, clip_args):
        inputs, hidden_pre, upstream, film_row = clip_args
        film_scale = 1.0 + film_row[:C]
        film_shift = film_row[C:]
        shifted = hidden_pre.astype(jnp.float32) * film_scale + film_shift
        sigma = jax.nn.sigmoid(shifted)
        activated = (shifted * sigma).astype(jnp.bfloat16)
        cot_pad = jnp.pad(upstream, ((0, 2), (1, 1), (1, 1), (0, 0)))
        grad_act = conv_transpose(cot_pad, conv_two)
        grad_hidden = (grad_act * film_scale * sigma * (1.0 + shifted * (1.0 - sigma))).astype(jnp.bfloat16)
        hid_pad = jnp.pad(grad_hidden, ((0, 2), (1, 1), (1, 1), (0, 0)))
        grad_input = (upstream.astype(jnp.float32) + conv_transpose(hid_pad, conv_one)).astype(jnp.bfloat16)
        act_pad = jnp.pad(activated, ((2, 0), (1, 1), (1, 1), (0, 0)))
        inp_pad = jnp.pad(inputs, ((2, 0), (1, 1), (1, 1), (0, 0)))
        sum_two = running[1] + weight_grad(act_pad, upstream)
        sum_one = running[0] + weight_grad(inp_pad, grad_hidden)
        return ((sum_one, sum_two), grad_input)
    zeros_grad = jnp.zeros((C, 3, 3, 3, C), jnp.float32)
    sums, grad_input = lax.scan(one_clip, (zeros_grad, zeros_grad), (activations, saved_hidden, cotangent, film_rows))
    factor = float(CLIPS * FRAMES * HEIGHT * WIDTH) ** (-0.5)
    return (grad_input, sums[0] * factor, sums[1] * factor)
```

```python
import functools

import jax
import jax.numpy as jnp
from jax import lax
from jax.experimental import pallas as pl
from jax.experimental.pallas import tpu as pltpu
from jax.sharding import Mesh
from jax.sharding import PartitionSpec as P

BF = jnp.bfloat16
F32 = jnp.float32
AX = ("z", "y", "ha", "xh", "core")
SIZES = (8, 4, 2, 2, 2)
PARAMS = pltpu.CompilerParams(vmem_limit_bytes=56 * 2**20)
VM = pl.BlockSpec(memory_space=pltpu.VMEM)
SM = pl.BlockSpec(memory_space=pltpu.SMEM)
HB = pl.BlockSpec(memory_space=pl.ANY)
NT = (((1,), (1,)), ((), ()))
TN = (((0,), (0,)), ((), ()))
SDS = jax.ShapeDtypeStruct


def split_index(i):
    core, xh, ha, y, z = i % 2, i // 2 % 2, i // 4 % 2, i // 8 % 4, i // 32
    return z, y, xh * 2 + ha, core


def join_index(z, y, x, core):
    return (((z % 8) * 4 + y % 4) * 4 + (x % 2) * 2 + x % 4 // 2) * 2 + core


def ring_pairs(dx=0, dy=0, dc=0):
    pairs = []
    for i in range(256):
        z, y, x, core = split_index(i)
        pairs.append((i, join_index(z, y + dy, x + dx, core ^ dc)))
    return pairs


def block_pairs(dh, dw):
    pairs = []
    for i in range(256):
        ha, wa, dp = i // 4 % 2, i % 4, i // 8
        if 0 <= wa + dw < 4:
            pairs.append((i, dp * 8 + (ha ^ dh) * 4 + wa + dw))
    return pairs


def send(value, pairs):
    return lax.ppermute(value, AX, pairs)


def halo(block, ha):
    near = lax.dynamic_index_in_dim(block, 11 * (1 - ha), 1, keepdims=False)
    row = send(near, block_pairs(1, 0))
    left = send(block[:, :, 15, :], block_pairs(0, 1))
    right = send(block[:, :, 0, :], block_pairs(0, -1))
    corner_left = send(near[:, 15, :], block_pairs(1, 1))
    corner_right = send(near[:, 0, :], block_pairs(1, -1))
    return row, left, right, corner_left, corner_right


def build_shifted(wide, block, row, left, right, corner_left, corner_right, ha):
    col = lax.broadcasted_iota(jnp.int32, (16, 256), 0)
    is_top, is_low = (ha == 1).astype(F32), (ha == 0).astype(F32)
    for f in range(4):
        edge = row[f].astype(F32)
        lefts, rights = left[f].astype(F32), right[f].astype(F32)
        cl, cr = corner_left[f : f + 1].astype(F32), corner_right[f : f + 1].astype(F32)
        for r in range(14):
            if r in (0, 13):
                keep = is_top if r == 0 else is_low
                cells, lo, hi = edge * keep, cl * keep, cr * keep
                wide[f, r, :, 256:512] = cells.astype(BF)
            else:
                cells = block[f, r - 1].astype(F32)
                lo, hi = lefts[r - 1 : r], rights[r - 1 : r]
                wide[f, r, :, 256:512] = block[f, r - 1]
            wide[f, r, :, 512:768] = jnp.where(col == 0, lo, pltpu.roll(cells, 1, 0)).astype(BF)
            wide[f, r, :, 0:256] = jnp.where(col == 15, hi, pltpu.roll(cells, 15, 0)).astype(BF)


def weight_copies(weight, held, sem):
    return [
        pltpu.make_async_copy(weight.at[pl.ds(a * 9, 9)], held.at[pl.ds(a * 9, 9)], sem.at[a])
        for a in range(3)
    ]


def conv_sum(wide, held, copies, total):
    for a in (2, 1, 0):
        frames = a + 2
        copies[a].wait()
        for b in range(3):
            window = wide[2 - a : 4, 2 - b : 14 - b].reshape(frames * 192, 768)
            part = None
            for e in range(3):
                one = lax.dot_general(
                    window[:, e * 256 : (e + 1) * 256],
                    held[(a * 3 + b) * 3 + e],
                    NT,
                    preferred_element_type=F32,
                )
                part = one if part is None else part + one
            if a == 2 and b == 0:
                total[...] = part
            else:
                total[0 : frames * 192] += part


def first_kernel(
    place, block, row, left, right, cl, cr, hidden, inputs, film, weight,
    act_out, inp_out, wide, hid_out, held, total, sem,
):
    copies = weight_copies(weight, held, sem)
    for a in (2, 1, 0):
        copies[a].start()
    x, core, ha = place[0], place[2], place[3]
    lane = lax.broadcasted_iota(jnp.int32, (256, 256), 1)
    goal = (x + ((lane >> 5) & 3)) & 3
    kept = core ^ (lane >> 7)
    source = ((goal & 1) << 7) + ((goal >> 1) << 6) + (kept << 5) + (lane & 31)
    order = (lax.broadcasted_iota(jnp.int32, (256, 256), 0) == source).astype(BF)
    inp_out[...] = jnp.dot(
        inputs[...].reshape(768, 256), order, preferred_element_type=F32
    ).astype(BF)
    scale, shift = 1.0 + film[0:1, 0:256], film[0:1, 256:512]
    shifted = hidden[...].reshape(768, 256).astype(F32) * scale + shift
    sigma = jax.nn.sigmoid(shifted)
    activated = (shifted * sigma).astype(BF)
    act_out[...] = jnp.dot(activated, order, preferred_element_type=F32).astype(BF)
    build_shifted(wide, block, row, left, right, cl, cr, ha)
    conv_sum(wide, held, copies, total)
    shifted = hidden[...].reshape(768, 256).astype(F32) * scale + shift
    sigma = jax.nn.sigmoid(shifted)
    grad = total[...] * scale * sigma * (1.0 + shifted * (1.0 - sigma))
    hid_out[...] = grad.astype(BF).reshape(4, 12, 16, 256)


def second_grad_kernel(wide, act, own, pair):
    b = pl.program_id(0)
    for a in range(3):
        rows = (a + 2) * 192
        window = wide[2 - a : 4, pl.ds(2 - b, 12)].reshape(rows, 768)
        grad = lax.dot_general(act[0:rows], window, TN, preferred_element_type=F32)
        own[a, 0] = grad[0:128]
        pair[a, 0] = grad[128:256]


def second_pair_kernel(own, pair, keep, one, two, three):
    for a in range(3):
        total = own[a, 0] + pair[a, 0]
        keep[a, 0] = total[0:32]
        one[a, 0] = total[32:64].astype(BF)
        two[a, 0] = total[64:96].astype(BF)
        three[a, 0] = total[96:128].astype(BF)


def second_x_kernel(place, own, got1, got2, got3, keep, one, two, three, held):
    y = place[1]
    outs = (keep, one, two, three)

    def tap(t):
        ab, lanes = t // 3, slice(t % 3 * 256, t % 3 * 256 + 256)
        at = (ab // 3, ab % 3, slice(None), lanes)
        return own[at] + got1[at].astype(F32) + got2[at].astype(F32) + got3[at].astype(F32)

    for g in range(7):
        parts = [tap(t) if t < 27 else jnp.zeros((32, 256), F32) for t in range(4 * g, 4 * g + 4)]
        held[...] = jnp.concatenate(parts, axis=0).T.reshape(8, 4, 8, 128)
        for q in range(4):
            piece = held[:, (y + q) & 3].reshape(64, 128)
            outs[q][g] = piece.astype(outs[q].dtype)


def first_grad_kernel(
    place, block, row, left, right, cl, cr, inp, wide, own, pair, held
):
    b = pl.program_id(0)
    y = place[1]

    @pl.when(b == 0)
    def _():
        build_shifted(wide, block, row, left, right, cl, cr, place[3])

    for a in range(3):
        rows = (a + 2) * 192
        window = wide[2 - a : 4, pl.ds(2 - b, 12)].reshape(rows, 768)
        grad = lax.dot_general(window, inp[0:rows], TN, preferred_element_type=F32)
        held[...] = grad.reshape(3, 8, 4, 8, 256)
        for q in range(4):
            piece = held[:, :, (y + q) & 3].reshape(3, 64, 256)
            own[q, a, 0] = piece[:, :, 0:128]
            pair[q, a, 0] = piece[:, :, 128:256]


def first_pair_kernel(own, pair, keep, one, two, three):
    for q, out in enumerate((keep, one, two, three)):
        out[...] = (own[q] + pair[q]).astype(out.dtype)


def first_y_kernel(own, got1, got2, got3, keep, one, two, three):
    outs = (keep, one, two, three)

    def tap(t):
        at = (t // 9, t // 3 % 3, t % 3)
        return own[at] + got1[at].astype(F32) + got2[at].astype(F32) + got3[at].astype(F32)

    for g in range(7):
        taps = [tap(t) if t < 27 else jnp.zeros((64, 128), F32) for t in range(4 * g, 4 * g + 4)]
        for q in range(4):
            piece = jnp.concatenate([v[:, q * 32 : q * 32 + 32] for v in taps], axis=1)
            outs[q][g] = piece.astype(outs[q].dtype)


def last_stage_kernel(a0, a1, a2, a3, b0, b1, b2, b3, out):
    sums = []
    for own, got in ((a0, (a1, a2, a3)), (b0, (b1, b2, b3))):
        total = own[...]
        for ref in got:
            total = total + ref[...].astype(F32)
        sums.append(total)
    for z in range(8):
        parts = [total[:, z * 8 : z * 8 + 8].reshape(56, 128) for total in sums]
        out[z] = jnp.concatenate(parts, axis=0).astype(BF)


def final_kernel(factor, got, one, two):
    total = got[0].astype(F32)
    for z in range(1, 8):
        total = total + got[z].astype(F32)
    total = (total * factor).reshape(2, 7, 8, 128)
    for out, which in ((two, 0), (one, 1)):
        for t in range(27):
            out[t] = total[which, t // 4, :, t % 4 * 32 : t % 4 * 32 + 32]


def input_conv_kernel(wide, block, weight, out, held, total, sem):
    copies = weight_copies(weight, held, sem)
    for a in (2, 1, 0):
        copies[a].start()
    conv_sum(wide, held, copies, total)
    grad = block[...].reshape(768, 256).astype(F32) + total[...]
    out[...] = grad.astype(BF).reshape(4, 12, 16, 256)


def shards(activations, saved_hidden, cotangent, conv_one, conv_two, film_table, timesteps):
    inputs, hidden, block = activations[0], saved_hidden[0], cotangent[0]
    ha, xh = lax.axis_index("ha"), lax.axis_index("xh")
    y, core = lax.axis_index("y"), lax.axis_index("core")
    place = jnp.stack([xh * 2 + ha, y, core, ha]).astype(jnp.int32)
    film = lax.dynamic_slice(film_table, (timesteps[0], 0), (1, 512))
    taps_one = conv_one.transpose(1, 2, 3, 0, 4).reshape(27, 256, 256)
    taps_two = conv_two.transpose(1, 2, 3, 0, 4).reshape(27, 256, 256)
    conv_scratch = [
        pltpu.VMEM((27, 256, 256), BF),
        pltpu.VMEM((768, 256), F32),
        pltpu.SemaphoreType.DMA((3,)),
    ]
    whole = lambda shape: pl.BlockSpec(shape, lambda b: (0,) * len(shape))

    cot_halo = halo(block, ha)
    act, inp, wide_cot, grad_hidden = pl.pallas_call(
        first_kernel,
        out_shape=(
            SDS((768, 256), BF),
            SDS((768, 256), BF),
            SDS((4, 14, 16, 768), BF),
            SDS((4, 12, 16, 256), BF),
        ),
        in_specs=[SM] + [VM] * 9 + [HB],
        out_specs=[VM] * 4,
        scratch_shapes=conv_scratch,
        compiler_params=PARAMS,
        name="conv_two_back",
    )(place, block, *cot_halo, hidden, inputs, film, taps_two)

    hid_halo = halo(grad_hidden, ha)

    tall = pl.BlockSpec((3, 1, 128, 768), lambda b: (0, b, 0, 0))
    low = pl.BlockSpec((3, 1, 32, 768), lambda b: (0, b, 0, 0))
    own, pair = pl.pallas_call(
        second_grad_kernel,
        grid=(3,),
        out_shape=(SDS((3, 3, 128, 768), F32),) * 2,
        in_specs=[whole((4, 14, 16, 768)), whole((768, 256))],
        out_specs=[tall, tall],
        compiler_params=PARAMS,
        name="grad_two",
    )(wide_cot, act)
    pair = send(pair, ring_pairs(dc=1))
    pieces = pl.pallas_call(
        second_pair_kernel,
        grid=(3,),
        out_shape=(SDS((3, 3, 32, 768), F32),) + (SDS((3, 3, 32, 768), BF),) * 3,
        in_specs=[tall, tall],
        out_specs=[low] * 4,
        compiler_params=PARAMS,
        name="grad_two_pair",
    )(own, pair)
    got = [send(pieces[d], ring_pairs(dx=d)) for d in (2, 1, 3)]
    quads = (SDS((7, 64, 128), F32),) + (SDS((7, 64, 128), BF),) * 3
    pieces = pl.pallas_call(
        second_x_kernel,
        out_shape=quads,
        in_specs=[SM] + [VM] * 4,
        out_specs=[VM] * 4,
        scratch_shapes=[pltpu.VMEM((8, 4, 8, 128), F32)],
        compiler_params=PARAMS,
        name="grad_two_x",
    )(place, pieces[0], *got)
    parts_two = [pieces[0]] + [send(pieces[d], ring_pairs(dy=d)) for d in (2, 1, 3)]

    wide_spec = whole((4, 14, 16, 768))
    split = pl.BlockSpec((4, 3, 1, 3, 64, 128), lambda b: (0, 0, b, 0, 0, 0))
    part = pl.BlockSpec((3, 1, 3, 64, 128), lambda b: (0, b, 0, 0, 0))
    wide_hid, own, pair = pl.pallas_call(
        first_grad_kernel,
        grid=(3,),
        out_shape=(SDS((4, 14, 16, 768), BF),) + (SDS((4, 3, 3, 3, 64, 128), F32),) * 2,
        in_specs=[
            SM,
            whole((4, 12, 16, 256)),
            whole((4, 16, 256)),
            whole((4, 12, 256)),
            whole((4, 12, 256)),
            whole((4, 256)),
            whole((4, 256)),
            whole((768, 256)),
        ],
        out_specs=[wide_spec, split, split],
        scratch_shapes=[pltpu.VMEM((3, 8, 4, 8, 256), F32)],
        compiler_params=PARAMS,
        name="grad_one",
    )(place, grad_hidden, *hid_halo, inp)
    pair = send(pair, ring_pairs(dc=1))
    pieces = pl.pallas_call(
        first_pair_kernel,
        grid=(3,),
        out_shape=(SDS((3, 3, 3, 64, 128), F32),) + (SDS((3, 3, 3, 64, 128), BF),) * 3,
        in_specs=[split, split],
        out_specs=[part] * 4,
        compiler_params=PARAMS,
        name="grad_one_pair",
    )(own, pair)
    got = [send(pieces[d], ring_pairs(dy=d)) for d in (2, 1, 3)]
    pieces = pl.pallas_call(
        first_y_kernel,
        out_shape=quads,
        in_specs=[VM] * 4,
        out_specs=[VM] * 4,
        compiler_params=PARAMS,
        name="grad_one_y",
    )(pieces[0], *got)
    parts_one = [pieces[0]] + [send(pieces[d], ring_pairs(dx=d)) for d in (2, 1, 3)]

    grad_input = pl.pallas_call(
        input_conv_kernel,
        out_shape=SDS((4, 12, 16, 256), BF),
        in_specs=[VM, VM, HB],
        out_specs=VM,
        scratch_shapes=conv_scratch,
        compiler_params=PARAMS,
        name="conv_one_back",
    )(wide_hid, block, taps_one)

    planes = pl.pallas_call(
        last_stage_kernel,
        out_shape=SDS((8, 112, 128), BF),
        in_specs=[VM] * 8,
        out_specs=VM,
        compiler_params=PARAMS,
        name="last_stage",
    )(*parts_two, *parts_one)
    planes = lax.all_to_all(planes, "z", 0, 0, tiled=True)
    factor = float(256 * 768) ** (-0.5)
    grad_one, grad_two = pl.pallas_call(
        functools.partial(final_kernel, factor),
        out_shape=(SDS((27, 8, 32), F32),) * 2,
        in_specs=[VM],
        out_specs=[VM] * 2,
        compiler_params=PARAMS,
        name="final_sum",
    )(planes)
    shape = lambda g: g.transpose(2, 0, 1).reshape(32, 3, 3, 3, 8)
    return grad_input[None], shape(grad_one), shape(grad_two)


def solution(mesh):
    fine = Mesh(mesh.devices.reshape(SIZES), AX)
    clip = ("z", "y")
    placed = P(clip, None, "ha", ("xh", "core"), None)
    weight = P(("ha", "xh", "core"), None, None, None, clip)
    return jax.shard_map(
        shards,
        mesh=fine,
        in_specs=(placed, placed, placed, P(), P(), P(), P(clip)),
        out_specs=(placed, weight, weight),
        check_vma=False,
    )
```

```python
import functools

import jax
import jax.numpy as jnp
from jax import lax
from jax.experimental import pallas as pl
from jax.experimental.pallas import tpu as pltpu
from jax.sharding import Mesh
from jax.sharding import PartitionSpec as P

BF = jnp.bfloat16
F32 = jnp.float32
AX = ("z", "y", "ha", "xh", "core")
SIZES = (8, 4, 2, 2, 2)
VM = pl.BlockSpec(memory_space=pltpu.VMEM)
HB = pl.BlockSpec(memory_space=pl.ANY)
SM = pl.BlockSpec(memory_space=pltpu.SMEM)
NT = (((1,), (1,)), ((), ()))
TN = (((0,), (0,)), ((), ()))


def core_pairs():
    return [(i, i ^ 1) for i in range(256)]


def block_pairs(dh, dw):
    pairs = []
    for i in range(256):
        ha, wa, dp = i // 4 % 2, i % 4, i // 8
        if 0 <= wa + dw < 4:
            pairs.append((i, dp * 8 + (ha ^ dh) * 4 + wa + dw))
    return pairs


def send(value, pairs):
    return lax.ppermute(value, AX, pairs)


def call(kernel, name, args, spaces, outs, scratch=(), limit=16):
    args = [
        pltpu.with_memory_space_constraint(a, pltpu.VMEM) if s == "v" else a
        for a, s in zip(args, spaces)
    ]
    specs = {"v": VM, "c": VM, "h": HB, "s": SM}
    return pl.pallas_call(
        kernel,
        out_shape=tuple(outs),
        in_specs=[specs[s] for s in spaces],
        out_specs=tuple(VM for _ in outs),
        scratch_shapes=list(scratch),
        compiler_params=pltpu.CompilerParams(vmem_limit_bytes=limit * 2**20),
        name=name,
    )(*args)


def pack_kernel(count, *refs):
    blocks, (row, hi, lo, corner_hi, corner_lo, wide) = refs[:count], refs[count:]
    ha = lax.axis_index("ha")
    edge = 11 * (1 - ha)
    for n, block in enumerate(blocks):
        flat = block[...].reshape(768, 256).astype(F32)
        wide[0] = flat[:, 0:128]
        wide[1] = flat[:, 128:256]
        for f in range(4):
            row[n, f] = block[f, edge]
            for j, out, corner in ((15, hi, corner_hi), (0, lo, corner_lo)):
                for h in range(2):
                    lanes = slice(h * 128, h * 128 + 128)
                    cells = wide[h, pl.ds(f * 192 + j, 12, stride=16), :]
                    cells = jnp.concatenate([cells, jnp.zeros((4, 128), F32)], axis=0)
                    out[n, f, :, lanes] = cells.astype(BF)
                    cell = wide[h, pl.ds(f * 192 + edge * 16 + j, 1), :]
                    corner[n, f, :, lanes] = jnp.broadcast_to(cell, (16, 128)).astype(BF)


def halo(name, blocks, space):
    n = len(blocks)
    side = pltpu.VMEM((n, 4, 16, 256), BF)
    row, hi, lo, corner_hi, corner_lo = call(
        functools.partial(pack_kernel, n),
        name,
        blocks,
        space * n,
        [side] * 5,
        [pltpu.VMEM((2, 768, 128), F32)],
    )
    return (
        send(row, block_pairs(1, 0)),
        send(hi, block_pairs(0, 1)),
        send(lo, block_pairs(0, -1)),
        send(corner_hi, block_pairs(1, 1)),
        send(corner_lo, block_pairs(1, -1)),
    )


def build_shifted(wide, block, row, left, right, corner_left, corner_right, ha, from_left):
    col = lax.broadcasted_iota(jnp.int32, (16, 256), 0)
    is_top, is_low = (ha == 1).astype(F32), (ha == 0).astype(F32)
    at_left, at_right = (0, 512) if from_left else (512, 0)
    for f in range(4):
        edge = row(f).astype(F32)
        lefts, rights = left(f).astype(F32), right(f).astype(F32)
        cl, cr = corner_left(f).astype(F32), corner_right(f).astype(F32)
        for r in range(14):
            if r in (0, 13):
                keep = is_top if r == 0 else is_low
                cells, lo, hi = edge * keep, cl * keep, cr * keep
            else:
                cells = block(f, r - 1).astype(F32)
                lo, hi = lefts[r - 1 : r], rights[r - 1 : r]
            wide[f, r, :, 256:512] = cells.astype(BF)
            shifted = jnp.where(col == 0, lo, pltpu.roll(cells, 1, 0))
            wide[f, r, :, at_left : at_left + 256] = shifted.astype(BF)
            shifted = jnp.where(col == 15, hi, pltpu.roll(cells, 15, 0))
            wide[f, r, :, at_right : at_right + 256] = shifted.astype(BF)


def weight_copies(weight, held, sem):
    return [
        pltpu.make_async_copy(weight.at[pl.ds(a * 9, 9)], held.at[pl.ds(a * 9, 9)], sem.at[a])
        for a in range(3)
    ]


def conv_sum(wide, held, copies, total):
    for a in (2, 1, 0):
        frames = a + 2
        copies[a].wait()
        for b in range(3):
            window = wide[2 - a : 4, 2 - b : 14 - b].reshape(frames * 192, 768)
            part = None
            for e in range(3):
                one = lax.dot_general(
                    window[:, e * 256 : (e + 1) * 256],
                    held[(a * 3 + b) * 3 + e],
                    NT,
                    preferred_element_type=F32,
                )
                part = one if part is None else part + one
            if a == 2 and b == 0:
                total[...] = part
            else:
                total[0 : frames * 192] += part


CONV_SCRATCH = [
    pltpu.VMEM((27, 256, 256), BF),
    pltpu.VMEM((768, 256), F32),
    pltpu.SemaphoreType.DMA((4,)),
]


def first_kernel(
    step, block, inputs, hidden, row, left, right, corner_left, corner_right, table, weight,
    act_out, wide_in, wide, hid_out, held, total, sem, film, side,
):
    start = step[0]
    whole = pl.multiple_of(start // 8 * 8, 8)
    film_copy = pltpu.make_async_copy(table.at[pl.ds(whole, 8)], film, sem.at[3])
    film_copy.start()
    copies = weight_copies(weight, held, sem)
    for a in (2, 1, 0):
        copies[a].start()
    ha, core = lax.axis_index("ha"), lax.axis_index("core")

    lane = lax.broadcasted_iota(jnp.int32, (256, 256), 1)
    goal = (lane >> 5) & 3
    source = ((goal & 1) << 7) + ((goal >> 1) << 6) + ((core ^ (lane >> 7)) << 5) + (lane & 31)
    order = (lax.broadcasted_iota(jnp.int32, (256, 256), 0) == source).astype(BF)

    def sort(value):
        return jnp.dot(value, order, preferred_element_type=F32)

    build_shifted(
        wide,
        lambda f, r: block[f, r],
        lambda f: row[0, f],
        lambda f: left[0, f],
        lambda f: right[0, f],
        lambda f: corner_left[0, f],
        lambda f: corner_right[0, f],
        ha,
        False,
    )
    film_copy.wait()
    line = film[pl.ds(start - whole, 1), :]
    scale, shift = 1.0 + line[:, 0:256], line[:, 256:512]
    shifted = hidden[...].reshape(768, 256).astype(F32) * scale + shift
    sigma = jax.nn.sigmoid(shifted)
    act_out[...] = sort((shifted * sigma).astype(BF)).astype(BF)
    total[...] = sort(inputs[...].reshape(768, 256))
    for n, ref in enumerate((row, left, right, corner_left, corner_right)):
        side[n] = sort(ref[1].reshape(64, 256)).reshape(4, 16, 256)
    build_shifted(
        wide_in,
        lambda f, r: total[(f * 12 + r) * 16 : (f * 12 + r) * 16 + 16],
        lambda f: side[0, f],
        lambda f: side[1, f],
        lambda f: side[2, f],
        lambda f: side[3, f],
        lambda f: side[4, f],
        ha,
        True,
    )
    conv_sum(wide, held, copies, total)
    shifted = hidden[...].reshape(768, 256).astype(F32) * scale + shift
    sigma = jax.nn.sigmoid(shifted)
    grad = total[...] * scale * sigma * (1.0 + shifted * (1.0 - sigma))
    hid_out[...] = grad.astype(BF).reshape(4, 12, 16, 256)


def input_conv_kernel(
    hid, block, row, left, right, corner_left, corner_right, weight,
    out, held, total, sem, wide,
):
    copies = weight_copies(weight, held, sem)
    for a in (2, 1, 0):
        copies[a].start()
    build_shifted(
        wide,
        lambda f, r: hid[f, r],
        lambda f: row[0, f],
        lambda f: left[0, f],
        lambda f: right[0, f],
        lambda f: corner_left[0, f],
        lambda f: corner_right[0, f],
        lax.axis_index("ha"),
        False,
    )
    conv_sum(wide, held, copies, total)
    grad = block[...].reshape(768, 256).astype(F32) + total[...]
    out[...] = grad.astype(BF).reshape(4, 12, 16, 256)


def second_grad_kernel(wide, act, own, pair):
    for a in range(3):
        rows = (a + 2) * 192
        for b in range(3):
            window = wide[2 - a : 4, 2 - b : 14 - b].reshape(rows, 768)
            grad = lax.dot_general(act[0:rows], window, TN, preferred_element_type=F32)
            own[a * 3 + b] = grad[0:128]
            pair[a * 3 + b] = grad[128:256]


def second_pair_kernel(own, pair, out, keep):
    x = lax.axis_index("xh") * 2 + lax.axis_index("ha")
    mine = pl.ds(pl.multiple_of(x * 32, 32), 32)
    for ab in range(9):
        for q in range(4):
            rows = slice(q * 32, q * 32 + 32)
            out[q, ab] = (own[ab, rows] + pair[ab, rows]).astype(BF)
        keep[ab] = own[ab, mine] + pair[ab, mine]


def second_x_kernel(got, own, out, keep, held):
    x = lax.axis_index("xh") * 2 + lax.axis_index("ha")
    y = lax.axis_index("y")

    def tap(t):
        ab, lanes = t // 3, slice(t % 3 * 256, t % 3 * 256 + 256)
        total = own[ab, :, lanes]
        for d in range(1, 4):
            total = total + got[(x + d) & 3, ab, :, lanes].astype(F32)
        return total

    for g in range(7):
        parts = [tap(t) if t < 27 else jnp.zeros((32, 256), F32) for t in range(4 * g, 4 * g + 4)]
        held[...] = jnp.concatenate(parts, axis=0).T.reshape(8, 4, 8, 128)
        for q in range(4):
            out[q, g] = held[:, q].reshape(64, 128).astype(BF)
        keep[g] = held[:, y].reshape(64, 128)


def first_grad_kernel(hid, wide, own, pair):
    for a in range(3):
        rows = (a + 2) * 192
        left = hid[2 - a : 4].reshape(rows, 256)
        for b in range(3):
            window = wide[0 : a + 2, b : b + 12].reshape(rows, 768)
            grad = lax.dot_general(left, window, TN, preferred_element_type=F32)
            grad = grad.reshape(8, 4, 8, 768)
            for q in range(4):
                piece = grad[:, q].reshape(64, 768)
                for e in range(3):
                    t = (a * 3 + b) * 3 + e
                    own[q, t] = piece[:, e * 256 : e * 256 + 128]
                    pair[q, t] = piece[:, e * 256 + 128 : e * 256 + 256]


def first_pair_kernel(own, pair, out, keep):
    y = lax.axis_index("y")
    for q in range(4):
        out[q] = (own[q] + pair[q]).astype(BF)
    keep[...] = own[y] + pair[y]


def first_y_kernel(got, own, out, keep, held):
    y = lax.axis_index("y")
    x = lax.axis_index("xh") * 2 + lax.axis_index("ha")

    def tap(t):
        total = own[t]
        for d in range(1, 4):
            total = total + got[(y + d) & 3, t].astype(F32)
        return total

    for g in range(7):
        taps = [tap(t) if t < 27 else jnp.zeros((64, 128), F32) for t in range(4 * g, 4 * g + 4)]
        for q in range(4):
            piece = jnp.concatenate([v[:, q * 32 : q * 32 + 32] for v in taps], axis=1)
            held[q] = piece
            out[q, g] = piece.astype(BF)
        keep[g] = held[x]


def last_kernel(got_two, own_two, got_one, own_one, out, keep, held):
    x = lax.axis_index("xh") * 2 + lax.axis_index("ha")
    y, z = lax.axis_index("y"), lax.axis_index("z")
    for n, (own, got, me) in enumerate(((own_two, got_two, y), (own_one, got_one, x))):
        total = own[...]
        for d in range(1, 4):
            total = total + got[(me + d) & 3].astype(F32)
        held[n] = total.reshape(7, 8, 8, 128)

    def plane(z):
        return jnp.concatenate([held[n, :, z].reshape(56, 128) for n in range(2)], axis=0)

    for q in range(8):
        out[q] = plane(q).astype(BF)
    keep[...] = plane(z)


def final_kernel(factor, got, own, one, two):
    z = lax.axis_index("z")
    total = own[...]
    for d in range(1, 8):
        total = total + got[(z + d) & 7].astype(F32)
    total = (total * factor).reshape(2, 7, 8, 128)
    for out, which in ((two, 0), (one, 1)):
        for t in range(27):
            out[t] = total[which, t // 4, :, t % 4 * 32 : t % 4 * 32 + 32]


def shards(activations, saved_hidden, cotangent, conv_one, conv_two, film_table, timesteps):
    inputs, hidden, block = activations[0], saved_hidden[0], cotangent[0]
    taps_one = conv_one.transpose(1, 2, 3, 0, 4).reshape(27, 256, 256)
    taps_two = conv_two.transpose(1, 2, 3, 0, 4).reshape(27, 256, 256)
    to_x = lambda v: lax.all_to_all(v, ("xh", "ha"), 0, 0, tiled=True)
    to_y = lambda v: lax.all_to_all(v, "y", 0, 0, tiled=True)
    wide = pltpu.VMEM((4, 14, 16, 768), BF)
    quads = [pltpu.VMEM((4, 7, 64, 128), BF), pltpu.VMEM((7, 64, 128), F32)]

    sides = halo("pack_first", [block, inputs], "c")
    act, wide_in, wide_cot, grad_hidden = call(
        first_kernel,
        "conv_two_back",
        (timesteps, block, inputs, hidden, *sides, film_table, taps_two),
        "sccc" + "v" * 5 + "hh",
        [pltpu.VMEM((768, 256), BF), wide, wide, pltpu.VMEM((4, 12, 16, 256), BF)],
        [*CONV_SCRATCH, pltpu.VMEM((8, 512), F32), pltpu.VMEM((5, 4, 16, 256), F32)],
    )

    tall = pltpu.VMEM((9, 128, 768), F32)
    own, pair = call(second_grad_kernel, "grad_two", (wide_cot, act), "vv", [tall, tall])
    pair = send(pair, core_pairs())
    out, own_two = call(
        second_pair_kernel,
        "grad_two_pair",
        (own, pair),
        "vv",
        [pltpu.VMEM((4, 9, 32, 768), BF), pltpu.VMEM((9, 32, 768), F32)],
    )
    got_two = to_x(out)

    split = pltpu.VMEM((4, 27, 64, 128), F32)
    own, pair = call(first_grad_kernel, "grad_one", (grad_hidden, wide_in), "vv", [split, split])
    pair = send(pair, core_pairs())
    out, own_one = call(
        first_pair_kernel,
        "grad_one_pair",
        (own, pair),
        "vv",
        [pltpu.VMEM((4, 27, 64, 128), BF), pltpu.VMEM((27, 64, 128), F32)],
    )
    got_one = to_y(out)

    sides = halo("pack_second", [grad_hidden], "v")
    (grad_input,) = call(
        input_conv_kernel,
        "conv_one_back",
        (grad_hidden, block, *sides, taps_one),
        "vc" + "v" * 5 + "h",
        [jax.ShapeDtypeStruct((4, 12, 16, 256), BF)],
        [*CONV_SCRATCH, pltpu.VMEM((4, 14, 16, 768), BF)],
    )

    out, own_two = call(
        second_x_kernel, "grad_two_x", (got_two, own_two), "vv", quads,
        [pltpu.VMEM((8, 4, 8, 128), F32)],
    )
    got_two = to_y(out)
    out, own_one = call(
        first_y_kernel, "grad_one_y", (got_one, own_one), "vv", quads,
        [pltpu.VMEM((4, 64, 128), F32)],
    )
    got_one = to_x(out)

    out, own = call(
        last_kernel,
        "last_stage",
        (got_two, own_two, got_one, own_one),
        "vvvv",
        [pltpu.VMEM((8, 112, 128), BF), pltpu.VMEM((112, 128), F32)],
        [pltpu.VMEM((2, 7, 8, 8, 128), F32)],
    )
    planes = lax.all_to_all(out, "z", 0, 0, tiled=True)
    factor = float(256 * 768) ** (-0.5)
    result = jax.ShapeDtypeStruct((27, 8, 32), F32)
    grad_one, grad_two = call(
        functools.partial(final_kernel, factor),
        "final_sum",
        (planes, own),
        "vv",
        [result, result],
    )
    shape = lambda g: g.transpose(2, 0, 1).reshape(32, 3, 3, 3, 8)
    return grad_input[None], shape(grad_one), shape(grad_two)


def solution(mesh):
    fine = Mesh(mesh.devices.reshape(SIZES), AX)
    clip = ("z", "y")
    placed = P(clip, None, "ha", ("xh", "core"), None)
    weight = P(("ha", "xh", "core"), None, None, None, clip)
    return jax.shard_map(
        shards,
        mesh=fine,
        in_specs=(placed, placed, placed, P(), P(), P(), P(clip)),
        out_specs=(placed, weight, weight),
        check_vma=False,
    )
```

```python
import functools

import jax
import jax.numpy as jnp
from jax import lax
from jax.experimental import pallas as pl
from jax.experimental.pallas import tpu as pltpu
from jax.sharding import Mesh
from jax.sharding import PartitionSpec as P

BF = jnp.bfloat16
F32 = jnp.float32
AX = ("z", "y", "ha", "xh", "core")
SIZES = (8, 4, 2, 2, 2)
VM = pl.BlockSpec(memory_space=pltpu.VMEM)
HB = pl.BlockSpec(memory_space=pl.ANY)
SM = pl.BlockSpec(memory_space=pltpu.SMEM)
NT = (((1,), (1,)), ((), ()))
TN = (((0,), (0,)), ((), ()))


def core_pairs():
    return [(i, i ^ 1) for i in range(256)]


def block_pairs(dh, dw):
    return [(i, i // 8 * 8 + (i // 4 % 2 ^ dh) * 4 + (i + dw) % 4) for i in range(256)]


def ring_pairs(dx, dy):
    pairs = []
    for i in range(256):
        core, xh, ha, y, z = i % 2, i // 2 % 2, i // 4 % 2, i // 8 % 4, i // 32
        x = (xh * 2 + ha + dx) % 4
        pairs.append((i, ((z * 4 + (y + dy) % 4) * 2 + x % 2) * 4 + x // 2 * 2 + core))
    return pairs


def send(value, pairs):
    return lax.ppermute(value, AX, pairs)


def call(kernel, name, args, spaces, outs, scratch=(), limit=16):
    where = {"v": pltpu.VMEM, "p": pltpu.HBM, "h": pltpu.HBM}
    args = [
        pltpu.with_memory_space_constraint(a, where[s]) if s in where else a
        for a, s in zip(args, spaces)
    ]
    specs = {"v": VM, "p": VM, "h": HB, "s": SM}
    return pl.pallas_call(
        kernel,
        out_shape=tuple(o for o, _ in outs),
        in_specs=[specs[s] for s in spaces],
        out_specs=tuple(specs[s] for _, s in outs),
        scratch_shapes=list(scratch),
        compiler_params=pltpu.CompilerParams(vmem_limit_bytes=limit * 2**20),
        name=name,
    )(*args)


def near(shape, dtype):
    return pltpu.VMEM(shape, dtype), "v"


def far(shape, dtype):
    return pltpu.HBM(shape, dtype), "h"


def x_place():
    return lax.axis_index("xh") * 2 + lax.axis_index("ha")


def column(wide, lanes_half, f, j):
    cells = wide[lanes_half, pl.ds(f * 192 + j, 12, stride=16), :]
    return jnp.concatenate([cells, jnp.zeros((4, 128), F32)], axis=0).astype(BF)


def spread(wide, block):
    flat = block[...].reshape(768, 256).astype(F32)
    wide[0] = flat[:, 0:128]
    wide[1] = flat[:, 128:256]


def pack_kernel(one, two, row, hi, lo, corner_hi, corner_lo, wide):
    edge = 11 * (1 - lax.axis_index("ha"))
    for n, block in enumerate((one, two)):
        spread(wide, block)
        for f in range(4):
            row[n, f] = block[f, edge]
            for j, out, corner in ((15, hi, corner_hi), (0, lo, corner_lo)):
                for h in range(2):
                    lanes = slice(h * 128, h * 128 + 128)
                    out[n, f, :, lanes] = column(wide, h, f, j)
                    cell = wide[h, pl.ds(f * 192 + edge * 16 + j, 1), :]
                    corner[n, f, :, lanes] = jnp.broadcast_to(cell, (16, 128)).astype(BF)


def pack_columns_kernel(block, after, hi, lo, wide):
    del after
    spread(wide, block)
    for f in range(4):
        for j, out in ((15, hi), (0, lo)):
            for h in range(2):
                out[f, :, h * 128 : h * 128 + 128] = column(wide, h, f, j)


def pack_rows_kernel(block, left, right, row):
    edge = 11 * (1 - lax.axis_index("ha"))
    for f in range(4):
        row[0, f] = block[f, edge]
        for n, side in ((1, left), (2, right)):
            cells = side[f].astype(F32)
            cell = jnp.where(edge == 0, cells[0:1], cells[11:12])
            row[n, f] = jnp.broadcast_to(cell, (16, 256)).astype(BF)


def build_shifted(put, cell_row, row, left, right, corner_left, corner_right):
    ha, wa = lax.axis_index("ha"), lax.axis_index("xh") * 2 + lax.axis_index("core")
    col = lax.broadcasted_iota(jnp.int32, (16, 256), 0)
    is_top, is_low = (ha == 1).astype(F32), (ha == 0).astype(F32)
    has_left, has_right = (wa > 0).astype(F32), (wa < 3).astype(F32)
    for f in range(4):
        edge = row(f).astype(F32)
        lefts, rights = left(f).astype(F32) * has_left, right(f).astype(F32) * has_right
        cl = corner_left(f).astype(F32)[0:1] * has_left
        cr = corner_right(f).astype(F32)[0:1] * has_right
        for r in range(14):
            if r in (0, 13):
                keep = is_top if r == 0 else is_low
                cells, lo, hi = edge * keep, cl * keep, cr * keep
            else:
                cells = cell_row(f, r - 1).astype(F32)
                lo, hi = lefts[r - 1 : r], rights[r - 1 : r]
            put(f, r, 1, cells.astype(BF))
            put(f, r, 0, jnp.where(col == 0, lo, pltpu.roll(cells, 1, 0)).astype(BF))
            put(f, r, 2, jnp.where(col == 15, hi, pltpu.roll(cells, 15, 0)).astype(BF))


def put_back(wide):
    def put(f, r, which, cells):
        wide[f, r, :, (2 - which) * 256 : (3 - which) * 256] = cells

    return put


def weight_copies(weight, held, sem):
    return [
        pltpu.make_async_copy(weight.at[pl.ds(a * 9, 9)], held.at[pl.ds(a * 9, 9)], sem.at[a])
        for a in range(3)
    ]


def conv_sum(wide, held, copies, total):
    for a in (2, 1, 0):
        frames = a + 2
        copies[a].wait()
        for b in range(3):
            window = wide[2 - a : 4, 2 - b : 14 - b].reshape(frames * 192, 768)
            part = None
            for e in range(3):
                one = lax.dot_general(
                    window[:, e * 256 : (e + 1) * 256],
                    held[(a * 3 + b) * 3 + e],
                    NT,
                    preferred_element_type=F32,
                )
                part = one if part is None else part + one
            if a == 2 and b == 0:
                total[...] = part
            else:
                total[0 : frames * 192] += part


CONV_SCRATCH = [
    pltpu.VMEM((27, 256, 256), BF),
    pltpu.VMEM((768, 256), F32),
    pltpu.SemaphoreType.DMA((3,)),
]


def channel_order():
    lane = lax.broadcasted_iota(jnp.int32, (256, 256), 1)
    goal, kept = (lane >> 5) & 3, lax.axis_index("core") ^ (lane >> 7)
    source = ((goal & 1) << 7) + ((goal >> 1) << 6) + (kept << 5) + (lane & 31)
    return (lax.broadcasted_iota(jnp.int32, (256, 256), 0) == source).astype(BF)


def film_kernel(step, inputs, hidden, table, act_out, inp_out, slope, film, sem):
    start = step[0]
    whole = pl.multiple_of(start // 8 * 8, 8)
    film_copy = pltpu.make_async_copy(table.at[pl.ds(whole, 8)], film, sem)
    film_copy.start()
    order = channel_order()
    sort = lambda v: jnp.dot(v, order, preferred_element_type=F32).astype(BF)
    inp_out[...] = sort(inputs[...].reshape(768, 256)).reshape(4, 12, 16, 256)
    film_copy.wait()
    line = film[pl.ds(start - whole, 1), :]
    scale, shift = 1.0 + line[:, 0:256], line[:, 256:512]
    shifted = hidden[...].reshape(768, 256).astype(F32) * scale + shift
    sigma = jax.nn.sigmoid(shifted)
    act_out[...] = sort((shifted * sigma).astype(BF))
    slope[...] = scale * sigma * (1.0 + shifted * (1.0 - sigma))


def first_kernel(
    block, inp, slope, row, left, right, corner_left, corner_right, weight,
    wide_in, wide, hid_out, held, total, sem, side,
):
    copies = weight_copies(weight, held, sem)
    for a in (2, 1, 0):
        copies[a].start()
    sides = (row, left, right, corner_left, corner_right)
    build_shifted(
        put_back(wide), lambda f, r: block[f, r], *[lambda f, s=s: s[0, f] for s in sides]
    )
    order = channel_order()
    for n, ref in enumerate(sides):
        cells = jnp.dot(ref[1].reshape(64, 256), order, preferred_element_type=F32)
        side[n] = cells.reshape(4, 16, 256)

    def put(f, r, which, cells):
        at = which * 128
        wide_in[f, r, :, at : at + 128] = cells[:, 0:128]
        wide_in[f, r, :, at + 384 : at + 512] = cells[:, 128:256]

    build_shifted(put, lambda f, r: inp[f, r], *[lambda f, n=n: side[n, f] for n in range(5)])
    conv_sum(wide, held, copies, total)
    hid_out[...] = (total[...] * slope[...]).astype(BF).reshape(4, 12, 16, 256)


def input_conv_kernel(hid, block, row, left, right, weight, out, held, total, sem, wide):
    copies = weight_copies(weight, held, sem)
    for a in (2, 1, 0):
        copies[a].start()
    build_shifted(
        put_back(wide),
        lambda f, r: hid[f, r],
        lambda f: row[0, f],
        lambda f: left[f],
        lambda f: right[f],
        lambda f: row[1, f],
        lambda f: row[2, f],
    )
    conv_sum(wide, held, copies, total)
    grad = block[...].reshape(768, 256).astype(F32) + total[...]
    out[...] = grad.astype(BF).reshape(4, 12, 16, 256)


def second_part(wide, act, half, a, b):
    rows = (a + 2) * 192
    window = wide[2 - a : 4, 2 - b : 14 - b].reshape(rows, 768)
    left = act[0:rows, half * 128 : half * 128 + 128]
    return lax.dot_general(left, window, TN, preferred_element_type=F32)


def second_pair_kernel(wide, act, pair):
    for a in range(3):
        for b in range(3):
            pair[a * 3 + b] = second_part(wide, act, 1, a, b)


def second_own_kernel(wide, act, got, out, keep, held, sem):
    mine = pl.ds(pl.multiple_of(x_place() * 32, 32), 32)
    for a in range(3):
        for b in range(3):
            ab = a * 3 + b
            total = second_part(wide, act, 0, a, b) + got[ab]
            held[ab] = total
            for q in range(4):
                out[q, ab] = total[q * 32 : q * 32 + 32].astype(BF)
    kept = pltpu.make_async_copy(held.at[:, mine], keep, sem)
    kept.start()
    kept.wait()


def second_x_kernel(got, own, after, one, two, three, keep, held):
    del after
    x, y = x_place(), lax.axis_index("y")

    def tap(t):
        ab, lanes = t // 3, slice(t % 3 * 256, t % 3 * 256 + 256)
        total = own[ab, :, lanes]
        for d in range(1, 4):
            total = total + got[(x + d) & 3, ab, :, lanes].astype(F32)
        return total

    for g in range(7):
        parts = [tap(t) if t < 27 else jnp.zeros((32, 256), F32) for t in range(4 * g, 4 * g + 4)]
        held[...] = jnp.concatenate(parts, axis=0).T.reshape(8, 4, 8, 128)
        for d, out in enumerate((keep, one, two, three)):
            out[g] = held[:, (y + d) & 3].reshape(64, 128).astype(out.dtype)


def first_part(hid, wide, half, a, b):
    rows = (a + 2) * 192
    left = hid[2 - a : 4].reshape(rows, 256)
    window = wide[0 : a + 2, b : b + 12, :, half * 384 : half * 384 + 384].reshape(rows, 384)
    return lax.dot_general(left, window, TN, preferred_element_type=F32)


def first_pair_kernel(hid, wide, pair):
    for a in range(3):
        for b in range(3):
            pair[a * 3 + b] = first_part(hid, wide, 1, a, b)


def first_own_kernel(hid, wide, got, one, two, three, keep, held, own, sem):
    y = lax.axis_index("y")
    for a in range(3):
        for b in range(3):
            ab = a * 3 + b
            held[...] = (first_part(hid, wide, 0, a, b) + got[ab]).reshape(8, 4, 8, 384)
            for d, out in enumerate((own, one, two, three)):
                piece = held[:, (y + d) & 3].reshape(64, 384)
                for e in range(3):
                    out[ab * 3 + e] = piece[:, e * 128 : e * 128 + 128].astype(out.dtype)
    kept = pltpu.make_async_copy(own, keep, sem)
    kept.start()
    kept.wait()


def first_y_kernel(got1, got2, got3, own, one, two, three, keep, held):
    x = x_place()

    def tap(t):
        total = own[t]
        for got in (got1, got2, got3):
            total = total + got[t].astype(F32)
        return total

    for g in range(7):
        taps = [tap(t) if t < 27 else jnp.zeros((64, 128), F32) for t in range(4 * g, 4 * g + 4)]
        for q in range(4):
            held[q] = jnp.concatenate([v[:, q * 32 : q * 32 + 32] for v in taps], axis=1)
        for d, out in enumerate((keep, one, two, three)):
            out[g] = held[(x + d) & 3].astype(out.dtype)


def last_kernel(own_two, a1, a2, a3, own_one, b1, b2, b3, out, keep, held):
    for n, (own, got) in enumerate(((own_two, (a1, a2, a3)), (own_one, (b1, b2, b3)))):
        total = own[...]
        for ref in got:
            total = total + ref[...].astype(F32)
        held[n] = total.reshape(7, 8, 8, 128)

    def plane(z):
        return jnp.concatenate([held[n, :, z].reshape(56, 128) for n in range(2)], axis=0)

    for q in range(8):
        out[q] = plane(q).astype(BF)
    keep[...] = plane(lax.axis_index("z"))


def final_kernel(factor, got, own, one, two):
    z = lax.axis_index("z")
    total = own[...]
    for d in range(1, 8):
        total = total + got[(z + d) & 7].astype(F32)
    total = (total * factor).reshape(2, 7, 8, 128)
    for out, which in ((two, 0), (one, 1)):
        for t in range(27):
            out[t] = total[which, t // 4, :, t % 4 * 32 : t % 4 * 32 + 32]


def shards(activations, saved_hidden, cotangent, conv_one, conv_two, film_table, timesteps):
    inputs, hidden, block = activations[0], saved_hidden[0], cotangent[0]
    taps_one = conv_one.transpose(1, 2, 3, 0, 4).reshape(27, 256, 256)
    taps_two = conv_two.transpose(1, 2, 3, 0, 4).reshape(27, 256, 256)
    wide = near((4, 14, 16, 768), BF)
    quads = [near((7, 64, 128), BF)] * 3 + [near((7, 64, 128), F32)]
    to_x = lambda parts: [send(p, ring_pairs(d + 1, 0)) for d, p in enumerate(parts)]
    to_y = lambda parts: [send(p, ring_pairs(0, d + 1)) for d, p in enumerate(parts)]

    packed = call(
        pack_kernel,
        "pack_first",
        (block, inputs),
        "pp",
        [near((2, 4, 16, 256), BF)] * 5,
        [pltpu.VMEM((2, 768, 128), F32)],
    )
    ways = ((1, 0), (0, 1), (0, -1), (1, 1), (1, -1))
    sides = [send(p, block_pairs(*way)) for p, way in zip(packed, ways)]
    act, inp, slope = call(
        film_kernel,
        "film",
        (timesteps, inputs, hidden, film_table),
        "spph",
        [near((768, 256), BF), near((4, 12, 16, 256), BF), near((768, 256), F32)],
        [pltpu.VMEM((8, 512), F32), pltpu.SemaphoreType.DMA],
    )
    wide_in, wide_cot, grad_hidden = call(
        first_kernel,
        "conv_two_back",
        (block, inp, slope, *sides, taps_two),
        "pvv" + "v" * 5 + "h",
        [wide, wide, near((4, 12, 16, 256), BF)],
        [*CONV_SCRATCH, pltpu.VMEM((5, 4, 16, 256), F32)],
    )

    (pair_two,) = call(
        second_pair_kernel, "grad_two_pair", (wide_cot, act), "vv", [near((9, 128, 768), F32)]
    )
    pair_two = send(pair_two, core_pairs())
    (pair_one,) = call(
        first_pair_kernel, "grad_one_pair", (grad_hidden, wide_in), "vv", [near((9, 256, 384), F32)]
    )
    pair_one = send(pair_one, core_pairs())
    out, own_two = call(
        second_own_kernel,
        "grad_two_own",
        (wide_cot, act, pair_two),
        "vvv",
        [near((4, 9, 32, 768), BF), far((9, 32, 768), F32)],
        [pltpu.VMEM((9, 128, 768), F32), pltpu.SemaphoreType.DMA],
    )
    got_two = lax.all_to_all(out, ("xh", "ha"), 0, 0, tiled=True)
    *parts, own_one = call(
        first_own_kernel,
        "grad_one_own",
        (grad_hidden, wide_in, pair_one),
        "vvv",
        [near((27, 64, 128), BF)] * 3 + [far((27, 64, 128), F32)],
        [
            pltpu.VMEM((8, 4, 8, 384), F32),
            pltpu.VMEM((27, 64, 128), F32),
            pltpu.SemaphoreType.DMA,
        ],
    )
    got_one = to_y(parts)

    hi, lo = call(
        pack_columns_kernel,
        "pack_columns",
        (grad_hidden, own_one),
        "vh",
        [near((4, 16, 256), BF)] * 2,
        [pltpu.VMEM((2, 768, 128), F32)],
    )
    left, right = send(hi, block_pairs(0, 1)), send(lo, block_pairs(0, -1))
    (row,) = call(
        pack_rows_kernel, "pack_rows", (grad_hidden, left, right), "vvv", [near((3, 4, 16, 256), BF)]
    )
    row = send(row, block_pairs(1, 0))
    (grad_input,) = call(
        input_conv_kernel,
        "conv_one_back",
        (grad_hidden, block, row, left, right, taps_one),
        "vpvvvh",
        [(jax.ShapeDtypeStruct((4, 12, 16, 256), BF), "v")],
        [*CONV_SCRATCH, pltpu.VMEM((4, 14, 16, 768), BF)],
    )

    *parts, own_two = call(
        second_x_kernel,
        "grad_two_x",
        (got_two, own_two, grad_input),
        "vph",
        quads,
        [pltpu.VMEM((8, 4, 8, 128), F32)],
    )
    got_two = to_y(parts)
    *parts, own_one = call(
        first_y_kernel,
        "grad_one_y",
        (*got_one, own_one),
        "vvvp",
        quads,
        [pltpu.VMEM((4, 64, 128), F32)],
    )
    got_one = to_x(parts)

    out, own = call(
        last_kernel,
        "last_stage",
        (own_two, *got_two, own_one, *got_one),
        "v" * 8,
        [near((8, 112, 128), BF), near((112, 128), F32)],
        [pltpu.VMEM((2, 7, 8, 8, 128), F32)],
    )
    planes = lax.all_to_all(out, "z", 0, 0, tiled=True)
    factor = float(256 * 768) ** (-0.5)
    result = jax.ShapeDtypeStruct((27, 8, 32), F32), "v"
    grad_one, grad_two = call(
        functools.partial(final_kernel, factor), "final_sum", (planes, own), "vv", [result, result]
    )
    shape = lambda g: g.transpose(2, 0, 1).reshape(32, 3, 3, 3, 8)
    return grad_input[None], shape(grad_one), shape(grad_two)


def solution(mesh):
    fine = Mesh(mesh.devices.reshape(SIZES), AX)
    clip = ("z", "y")
    placed = P(clip, None, "ha", ("xh", "core"), None)
    weight = P(("ha", "xh", "core"), None, None, None, clip)
    return jax.shard_map(
        shards,
        mesh=fine,
        in_specs=(placed, placed, placed, P(), P(), P(), P(clip)),
        out_specs=(placed, weight, weight),
        check_vma=False,
    )
```

```python
import functools

import jax
import jax.numpy as jnp
from jax import lax
from jax.experimental import pallas as pl
from jax.experimental.pallas import tpu as pltpu
from jax.sharding import Mesh
from jax.sharding import PartitionSpec as P

BF = jnp.bfloat16
F32 = jnp.float32
AX = ("z", "y", "ha", "xh", "core")
SIZES = (8, 4, 2, 2, 2)
VM = pl.BlockSpec(memory_space=pltpu.VMEM)
HB = pl.BlockSpec(memory_space=pl.ANY)
SM = pl.BlockSpec(memory_space=pltpu.SMEM)
NT = (((1,), (1,)), ((), ()))
TN = (((0,), (0,)), ((), ()))


def core_pairs():
    return [(i, i ^ 1) for i in range(256)]


def block_pairs(dh, dw):
    return [(i, i // 8 * 8 + (i // 4 % 2 ^ dh) * 4 + (i + dw) % 4) for i in range(256)]


def ring_pairs(dx=0, dy=0, dz=0):
    pairs = []
    for i in range(256):
        core, xh, ha, y, z = i % 2, i // 2 % 2, i // 4 % 2, i // 8 % 4, i // 32
        x, y, z = (xh * 2 + ha + dx) % 4, (y + dy) % 4, (z + dz) % 8
        pairs.append((i, ((z * 4 + y) * 2 + x % 2) * 4 + x // 2 * 2 + core))
    return pairs


def send(value, pairs):
    return lax.ppermute(value, AX, pairs)


def call(kernel, name, args, spaces, outs, scratch=(), limit=16):
    where = {"v": pltpu.VMEM, "p": pltpu.HBM, "h": pltpu.HBM}
    args = [
        pltpu.with_memory_space_constraint(a, where[s]) if s in where else a
        for a, s in zip(args, spaces)
    ]
    specs = {"v": VM, "p": VM, "h": HB, "s": SM}
    return pl.pallas_call(
        kernel,
        out_shape=tuple(o for o, _ in outs),
        in_specs=[specs[s] for s in spaces],
        out_specs=tuple(specs[s] for _, s in outs),
        scratch_shapes=list(scratch),
        compiler_params=pltpu.CompilerParams(vmem_limit_bytes=limit * 2**20),
        name=name,
    )(*args)


def near(shape, dtype):
    return pltpu.VMEM(shape, dtype), "v"


def far(shape, dtype):
    return pltpu.HBM(shape, dtype), "p"


def x_place():
    return lax.axis_index("xh") * 2 + lax.axis_index("ha")


def column(wide, lanes_half, f, j):
    cells = wide[lanes_half, pl.ds(f * 192 + j, 12, stride=16), :]
    return jnp.concatenate([cells, jnp.zeros((4, 128), F32)], axis=0).astype(BF)


def spread(wide, block):
    flat = block[...].reshape(768, 256).astype(F32)
    wide[0] = flat[:, 0:128]
    wide[1] = flat[:, 128:256]


def pack_kernel(one, two, row, hi, lo, corner_hi, corner_lo, wide):
    edge = 11 * (1 - lax.axis_index("ha"))
    for n, block in enumerate((one, two)):
        spread(wide, block)
        for f in range(4):
            row[n, f] = block[f, edge]
            for j, out, corner in ((15, hi, corner_hi), (0, lo, corner_lo)):
                for h in range(2):
                    lanes = slice(h * 128, h * 128 + 128)
                    out[n, f, :, lanes] = column(wide, h, f, j)
                    cell = wide[h, pl.ds(f * 192 + edge * 16 + j, 1), :]
                    corner[n, f, :, lanes] = jnp.broadcast_to(cell, (16, 128)).astype(BF)


def pack_columns_kernel(block, after, hi, lo, wide):
    del after
    spread(wide, block)
    for f in range(4):
        for j, out in ((15, hi), (0, lo)):
            for h in range(2):
                out[f, :, h * 128 : h * 128 + 128] = column(wide, h, f, j)


def pack_rows_kernel(block, left, right, after, row):
    del after
    edge = 11 * (1 - lax.axis_index("ha"))
    for f in range(4):
        row[0, f] = block[f, edge]
        for n, side in ((1, left), (2, right)):
            cells = side[f].astype(F32)
            cell = jnp.where(edge == 0, cells[0:1], cells[11:12])
            row[n, f] = jnp.broadcast_to(cell, (16, 256)).astype(BF)


def build_shifted(put, cell_row, row, left, right, corner_left, corner_right):
    ha, wa = lax.axis_index("ha"), lax.axis_index("xh") * 2 + lax.axis_index("core")
    col = lax.broadcasted_iota(jnp.int32, (16, 256), 0)
    is_top, is_low = (ha == 1).astype(F32), (ha == 0).astype(F32)
    has_left, has_right = (wa > 0).astype(F32), (wa < 3).astype(F32)
    for f in range(4):
        edge = row(f).astype(F32)
        lefts, rights = left(f).astype(F32) * has_left, right(f).astype(F32) * has_right
        cl = corner_left(f).astype(F32)[0:1] * has_left
        cr = corner_right(f).astype(F32)[0:1] * has_right
        for r in range(14):
            if r in (0, 13):
                keep = is_top if r == 0 else is_low
                cells, lo, hi = edge * keep, cl * keep, cr * keep
            else:
                cells = cell_row(f, r - 1).astype(F32)
                lo, hi = lefts[r - 1 : r], rights[r - 1 : r]
            put(f, r, 1, cells.astype(BF))
            put(f, r, 0, jnp.where(col == 0, lo, pltpu.roll(cells, 1, 0)).astype(BF))
            put(f, r, 2, jnp.where(col == 15, hi, pltpu.roll(cells, 15, 0)).astype(BF))


def put_back(wide):
    def put(f, r, which, cells):
        wide[f, r, :, (2 - which) * 256 : (3 - which) * 256] = cells

    return put


def weight_copies(weight, held, sem):
    return [
        pltpu.make_async_copy(weight.at[pl.ds(a * 9, 9)], held.at[pl.ds(a * 9, 9)], sem.at[a])
        for a in range(3)
    ]


def conv_sum(wide, held, total):
    for a in (2, 1, 0):
        frames = a + 2
        for b in range(3):
            window = wide[2 - a : 4, 2 - b : 14 - b].reshape(frames * 192, 768)
            part = None
            for e in range(3):
                one = lax.dot_general(
                    window[:, e * 256 : (e + 1) * 256],
                    held[(a * 3 + b) * 3 + e],
                    NT,
                    preferred_element_type=F32,
                )
                part = one if part is None else part + one
            if a == 2 and b == 0:
                total[...] = part
            else:
                total[0 : frames * 192] += part


def channel_order():
    lane = lax.broadcasted_iota(jnp.int32, (256, 256), 1)
    goal, kept = (lane >> 5) & 3, lax.axis_index("core") ^ (lane >> 7)
    source = ((goal & 1) << 7) + ((goal >> 1) << 6) + (kept << 5) + (lane & 31)
    return (lax.broadcasted_iota(jnp.int32, (256, 256), 0) == source).astype(BF)


def film_kernel(
    step, inputs, hidden, table, weight, act_out, inp_out, slope, taps,
    film, blocks, sem, block_sem, tap_sem,
):
    start = step[0]
    whole = pl.multiple_of(start // 8 * 8, 8)
    film_copy = pltpu.make_async_copy(table.at[pl.ds(whole, 8)], film, sem)
    film_copy.start()
    block_copies = [
        pltpu.make_async_copy(ref, blocks.at[n], block_sem.at[n])
        for n, ref in enumerate((inputs, hidden))
    ]
    for copy in block_copies:
        copy.start()
    copies = weight_copies(weight, taps, tap_sem)
    for copy in copies:
        copy.start()
    order = channel_order()
    sort = lambda v: jnp.dot(v, order, preferred_element_type=F32).astype(BF)
    for copy in block_copies:
        copy.wait()
    film_copy.wait()
    inp_out[...] = sort(blocks[0].reshape(768, 256)).reshape(4, 12, 16, 256)
    line = film[pl.ds(start - whole, 1), :]
    scale, shift = 1.0 + line[:, 0:256], line[:, 256:512]
    shifted = blocks[1].reshape(768, 256).astype(F32) * scale + shift
    sigma = jax.nn.sigmoid(shifted)
    act_out[...] = sort((shifted * sigma).astype(BF))
    slope[...] = scale * sigma * (1.0 + shifted * (1.0 - sigma))
    for copy in copies:
        copy.wait()


def first_kernel(
    block, inp, slope, row, left, right, corner_left, corner_right, taps,
    wide_in, wide, hid_out, total, side,
):
    sides = (row, left, right, corner_left, corner_right)
    build_shifted(
        put_back(wide), lambda f, r: block[f, r], *[lambda f, s=s: s[0, f] for s in sides]
    )
    order = channel_order()
    for n, ref in enumerate(sides):
        cells = jnp.dot(ref[1].reshape(64, 256), order, preferred_element_type=F32)
        side[n] = cells.reshape(4, 16, 256)

    def put(f, r, which, cells):
        at = which * 128
        wide_in[f, r, :, at : at + 128] = cells[:, 0:128]
        wide_in[f, r, :, at + 384 : at + 512] = cells[:, 128:256]

    build_shifted(put, lambda f, r: inp[f, r], *[lambda f, n=n: side[n, f] for n in range(5)])
    conv_sum(wide, taps, total)
    hid_out[...] = (total[...] * slope[...]).astype(BF).reshape(4, 12, 16, 256)


def input_conv_kernel(hid, block, row, left, right, weight, out, held, total, sem, wide):
    copies = weight_copies(weight, held, sem)
    for copy in copies:
        copy.start()
    build_shifted(
        put_back(wide),
        lambda f, r: hid[f, r],
        lambda f: row[0, f],
        lambda f: left[f],
        lambda f: right[f],
        lambda f: row[1, f],
        lambda f: row[2, f],
    )
    for copy in copies:
        copy.wait()
    conv_sum(wide, held, total)
    grad = block[...].reshape(768, 256).astype(F32) + total[...]
    out[...] = grad.astype(BF).reshape(4, 12, 16, 256)


def second_part(wide, act, half, a, b):
    rows = (a + 2) * 192
    window = wide[2 - a : 4, 2 - b : 14 - b].reshape(rows, 768)
    left = act[0:rows, half * 128 : half * 128 + 128]
    return lax.dot_general(left, window, TN, preferred_element_type=F32)


def second_pair_kernel(wide, act, after, pair):
    del after
    for a in range(3):
        for b in range(3):
            pair[a * 3 + b] = second_part(wide, act, 1, a, b)


def second_own_kernel(wide, act, got, after, one, two, three, keep, held):
    del after
    x = x_place()
    for a in range(3):
        for b in range(3):
            ab = a * 3 + b
            held[...] = second_part(wide, act, 0, a, b) + got[ab]
            for d, out in enumerate((keep, one, two, three)):
                rows = pl.ds(pl.multiple_of(((x + d) & 3) * 32, 32), 32)
                out[ab] = held[rows, :].astype(out.dtype)


def second_x_kernel(got1, got2, got3, own, after, one, two, three, keep, held):
    del after
    y = lax.axis_index("y")

    def tap(t):
        ab, lanes = t // 3, slice(t % 3 * 256, t % 3 * 256 + 256)
        total = own[ab, :, lanes]
        for got in (got1, got2, got3):
            total = total + got[ab, :, lanes].astype(F32)
        return total

    for g in range(7):
        parts = [tap(t) if t < 27 else jnp.zeros((32, 256), F32) for t in range(4 * g, 4 * g + 4)]
        held[...] = jnp.concatenate(parts, axis=0).T.reshape(8, 4, 8, 128)
        for d, out in enumerate((keep, one, two, three)):
            out[g] = held[:, (y + d) & 3].reshape(64, 128).astype(out.dtype)


def first_grad_kernel(hid, wide, own, pair):
    for a in range(3):
        rows = (a + 2) * 192
        left = hid[2 - a : 4].reshape(rows, 256)
        for b in range(3):
            window = wide[0 : a + 2, b : b + 12].reshape(rows, 768)
            grad = lax.dot_general(left, window, TN, preferred_element_type=F32)
            grad = grad.reshape(8, 4, 8, 768)
            for q in range(4):
                piece = grad[:, q].reshape(64, 768)
                for e in range(3):
                    t = (a * 3 + b) * 3 + e
                    own[q, t] = piece[:, e * 128 : e * 128 + 128]
                    pair[q, t] = piece[:, e * 128 + 384 : e * 128 + 512]


def first_pair_kernel(own, pair, out, keep):
    y = lax.axis_index("y")
    for q in range(4):
        out[q] = (own[q] + pair[q]).astype(BF)
    keep[...] = own[y] + pair[y]


def first_y_kernel(got, own, after, one, two, three, keep, held):
    del after
    x, y = x_place(), lax.axis_index("y")

    def tap(t):
        total = own[t]
        for d in range(1, 4):
            total = total + got[(y + d) & 3, t].astype(F32)
        return total

    for g in range(7):
        taps = [tap(t) if t < 27 else jnp.zeros((64, 128), F32) for t in range(4 * g, 4 * g + 4)]
        for q in range(4):
            held[q] = jnp.concatenate([v[:, q * 32 : q * 32 + 32] for v in taps], axis=1)
        for d, out in enumerate((keep, one, two, three)):
            out[g] = held[(x + d) & 3].astype(out.dtype)


def last_kernel(own_two, a1, a2, a3, own_one, b1, b2, b3, *rest):
    outs, held = rest[:8], rest[8]
    for n, (own, got) in enumerate(((own_two, (a1, a2, a3)), (own_one, (b1, b2, b3)))):
        total = own[...]
        for ref in got:
            total = total + ref[...].astype(F32)
        held[n] = total.reshape(7, 8, 8, 128)
    z = lax.axis_index("z")
    for d, out in enumerate(outs):
        plane = [held[n, :, (z + d) & 7].reshape(56, 128) for n in range(2)]
        out[...] = jnp.concatenate(plane, axis=0).astype(out.dtype)


def final_kernel(factor, own, *rest):
    got, (one, two) = rest[:7], rest[7:]
    total = own[...]
    for ref in got:
        total = total + ref[...].astype(F32)
    total = (total * factor).reshape(2, 7, 8, 128)
    for out, which in ((two, 0), (one, 1)):
        for t in range(27):
            out[t] = total[which, t // 4, :, t % 4 * 32 : t % 4 * 32 + 32]


def shards(activations, saved_hidden, cotangent, conv_one, conv_two, film_table, timesteps):
    inputs, hidden, block = activations[0], saved_hidden[0], cotangent[0]
    taps_one = conv_one.transpose(1, 2, 3, 0, 4).reshape(27, 256, 256)
    taps_two = conv_two.transpose(1, 2, 3, 0, 4).reshape(27, 256, 256)
    wide = near((4, 14, 16, 768), BF)
    quads = [near((7, 64, 128), BF)] * 3 + [near((7, 64, 128), F32)]

    def ring(parts, axis):
        return [send(p, ring_pairs(**{axis: d + 1})) for d, p in enumerate(parts)]

    packed = call(
        pack_kernel,
        "pack_first",
        (block, inputs),
        "pp",
        [near((2, 4, 16, 256), BF)] * 5,
        [pltpu.VMEM((2, 768, 128), F32)],
    )
    ways = ((1, 0), (0, 1), (0, -1), (1, 1), (1, -1))
    sides = [send(p, block_pairs(*way)) for p, way in zip(packed, ways)]
    act, inp, slope, held_two = call(
        film_kernel,
        "film",
        (timesteps, inputs, hidden, film_table, taps_two),
        "shhhh",
        [
            near((768, 256), BF),
            near((4, 12, 16, 256), BF),
            near((768, 256), F32),
            near((27, 256, 256), BF),
        ],
        [
            pltpu.VMEM((8, 512), F32),
            pltpu.VMEM((2, 4, 12, 16, 256), BF),
            pltpu.SemaphoreType.DMA,
            pltpu.SemaphoreType.DMA((2,)),
            pltpu.SemaphoreType.DMA((3,)),
        ],
    )
    wide_in, wide_cot, grad_hidden = call(
        first_kernel,
        "conv_two_back",
        (block, inp, slope, *sides, held_two),
        "pvv" + "v" * 5 + "v",
        [wide, wide, near((4, 12, 16, 256), BF)],
        [pltpu.VMEM((768, 256), F32), pltpu.VMEM((5, 4, 16, 256), F32)],
    )

    split = near((4, 27, 64, 128), F32)
    own_one, pair_one = call(
        first_grad_kernel, "grad_one", (grad_hidden, wide_in), "vv", [split, split]
    )
    got_pair_one = send(pair_one, core_pairs())
    (pair_two,) = call(
        second_pair_kernel,
        "grad_two_pair",
        (wide_cot, act, pair_one),
        "vvv",
        [near((9, 128, 768), F32)],
    )
    got_pair_two = send(pair_two, core_pairs())
    hi, lo = call(
        pack_columns_kernel,
        "pack_columns",
        (grad_hidden, pair_two),
        "vv",
        [near((4, 16, 256), BF)] * 2,
        [pltpu.VMEM((2, 768, 128), F32)],
    )
    left, right = send(hi, block_pairs(0, 1)), send(lo, block_pairs(0, -1))
    out_one, own_one = call(
        first_pair_kernel,
        "grad_one_sum",
        (own_one, got_pair_one),
        "vv",
        [far((4, 27, 64, 128), BF), far((27, 64, 128), F32)],
    )
    got_one = lax.all_to_all(out_one, "y", 0, 0, tiled=True)
    *parts, own_two = call(
        second_own_kernel,
        "grad_two_own",
        (wide_cot, act, got_pair_two, out_one),
        "vvvh",
        [near((9, 32, 768), BF)] * 3 + [far((9, 32, 768), F32)],
        [pltpu.VMEM((128, 768), F32)],
    )
    got_two = ring(parts, "dx")

    (row,) = call(
        pack_rows_kernel,
        "pack_rows",
        (grad_hidden, left, right, parts[0]),
        "vvvv",
        [near((3, 4, 16, 256), BF)],
    )
    row = send(row, block_pairs(1, 0))
    (grad_input,) = call(
        input_conv_kernel,
        "conv_one_back",
        (grad_hidden, block, row, left, right, taps_one),
        "vpvvvh",
        [(jax.ShapeDtypeStruct((4, 12, 16, 256), BF), "v")],
        [
            pltpu.VMEM((27, 256, 256), BF),
            pltpu.VMEM((768, 256), F32),
            pltpu.SemaphoreType.DMA((3,)),
            pltpu.VMEM((4, 14, 16, 768), BF),
        ],
    )

    *parts, own_one = call(
        first_y_kernel,
        "grad_one_y",
        (got_one, own_one, grad_input),
        "vph",
        quads,
        [pltpu.VMEM((4, 64, 128), F32)],
    )
    got_one = ring(parts, "dx")
    *parts, own_two = call(
        second_x_kernel,
        "grad_two_x",
        (*got_two, own_two, grad_input),
        "vvvph",
        quads,
        [pltpu.VMEM((8, 4, 8, 128), F32)],
    )
    got_two = ring(parts, "dy")

    own, *parts = call(
        last_kernel,
        "last_stage",
        (own_two, *got_two, own_one, *got_one),
        "v" * 8,
        [near((112, 128), F32)] + [near((112, 128), BF)] * 7,
        [pltpu.VMEM((2, 7, 8, 8, 128), F32)],
    )
    planes = ring(parts, "dz")
    factor = float(256 * 768) ** (-0.5)
    result = jax.ShapeDtypeStruct((27, 8, 32), F32), "v"
    grad_one, grad_two = call(
        functools.partial(final_kernel, factor),
        "final_sum",
        (own, *planes),
        "v" * 8,
        [result, result],
    )
    shape = lambda g: g.transpose(2, 0, 1).reshape(32, 3, 3, 3, 8)
    return grad_input[None], shape(grad_one), shape(grad_two)


def solution(mesh):
    fine = Mesh(mesh.devices.reshape(SIZES), AX)
    clip = ("z", "y")
    placed = P(clip, None, "ha", ("xh", "core"), None)
    weight = P(("ha", "xh", "core"), None, None, None, clip)
    return jax.shard_map(
        shards,
        mesh=fine,
        in_specs=(placed, placed, placed, P(), P(), P(), P(clip)),
        out_specs=(placed, weight, weight),
        check_vma=False,
    )
```

```python
import functools

import jax
import jax.numpy as jnp
from jax import lax
from jax.experimental import pallas as pl
from jax.experimental.pallas import tpu as pltpu
from jax.sharding import Mesh
from jax.sharding import PartitionSpec as P

BF = jnp.bfloat16
F32 = jnp.float32
AX = ("z", "y", "ha", "xh", "core")
SIZES = (8, 4, 2, 2, 2)
VM = pl.BlockSpec(memory_space=pltpu.VMEM)
HB = pl.BlockSpec(memory_space=pl.ANY)
SM = pl.BlockSpec(memory_space=pltpu.SMEM)
NT = (((1,), (1,)), ((), ()))
TN = (((0,), (0,)), ((), ()))


def core_pairs():
    return [(i, i ^ 1) for i in range(256)]


def block_pairs(dh, dw):
    return [(i, i // 8 * 8 + (i // 4 % 2 ^ dh) * 4 + (i + dw) % 4) for i in range(256)]


def ring_pairs(dx=0, dy=0):
    pairs = []
    for i in range(256):
        core, xh, ha, y, z = i % 2, i // 2 % 2, i // 4 % 2, i // 8 % 4, i // 32
        x, y = (xh * 2 + ha + dx) % 4, (y + dy) % 4
        pairs.append((i, ((z * 4 + y) * 2 + x % 2) * 4 + x // 2 * 2 + core))
    return pairs


def send(value, pairs):
    return lax.ppermute(value, AX, pairs)


def call(kernel, name, args, spaces, outs, scratch=(), limit=16):
    where = {"v": pltpu.VMEM, "p": pltpu.HBM, "h": pltpu.HBM}
    args = [
        pltpu.with_memory_space_constraint(a, where[s]) if s in where else a
        for a, s in zip(args, spaces)
    ]
    specs = {"v": VM, "p": VM, "h": HB, "s": SM}
    return pl.pallas_call(
        kernel,
        out_shape=tuple(o for o, _ in outs),
        in_specs=[specs[s] for s in spaces],
        out_specs=tuple(specs[s] for _, s in outs),
        scratch_shapes=list(scratch),
        compiler_params=pltpu.CompilerParams(vmem_limit_bytes=limit * 2**20),
        name=name,
    )(*args)


def near(shape, dtype):
    return pltpu.VMEM(shape, dtype), "v"


def far(shape, dtype):
    return pltpu.HBM(shape, dtype), "p"


def x_place():
    return lax.axis_index("xh") * 2 + lax.axis_index("ha")


def column(wide, lanes_half, f, j):
    cells = wide[lanes_half, pl.ds(f * 192 + j, 12, stride=16), :]
    return jnp.concatenate([cells, jnp.zeros((4, 128), F32)], axis=0).astype(BF)


def spread(wide, block):
    flat = block[...].reshape(768, 256).astype(F32)
    wide[0] = flat[:, 0:128]
    wide[1] = flat[:, 128:256]


def pack_kernel(one, two, row, hi, lo, corner_hi, corner_lo, wide):
    edge = 11 * (1 - lax.axis_index("ha"))
    for n, block in enumerate((one, two)):
        spread(wide, block)
        for f in range(4):
            row[n, f] = block[f, edge]
            for j, out, corner in ((15, hi, corner_hi), (0, lo, corner_lo)):
                for h in range(2):
                    lanes = slice(h * 128, h * 128 + 128)
                    out[n, f, :, lanes] = column(wide, h, f, j)
                    cell = wide[h, pl.ds(f * 192 + edge * 16 + j, 1), :]
                    corner[n, f, :, lanes] = jnp.broadcast_to(cell, (16, 128)).astype(BF)


def pack_columns_kernel(block, hi, lo, wide):
    spread(wide, block)
    for f in range(4):
        for j, out in ((15, hi), (0, lo)):
            for h in range(2):
                out[f, :, h * 128 : h * 128 + 128] = column(wide, h, f, j)


def pack_rows_kernel(block, left, right, after, row):
    del after
    edge = 11 * (1 - lax.axis_index("ha"))
    for f in range(4):
        row[0, f] = block[f, edge]
        for n, side in ((1, left), (2, right)):
            cells = side[f].astype(F32)
            cell = jnp.where(edge == 0, cells[0:1], cells[11:12])
            row[n, f] = jnp.broadcast_to(cell, (16, 256)).astype(BF)


def build_shifted(put, cell_row, row, left, right, corner_left, corner_right):
    ha, wa = lax.axis_index("ha"), lax.axis_index("xh") * 2 + lax.axis_index("core")
    col = lax.broadcasted_iota(jnp.int32, (16, 256), 0)
    is_top, is_low = (ha == 1).astype(F32), (ha == 0).astype(F32)
    has_left, has_right = (wa > 0).astype(F32), (wa < 3).astype(F32)
    for f in range(4):
        edge = row(f).astype(F32)
        lefts, rights = left(f).astype(F32) * has_left, right(f).astype(F32) * has_right
        cl = corner_left(f).astype(F32)[0:1] * has_left
        cr = corner_right(f).astype(F32)[0:1] * has_right
        for r in range(14):
            if r in (0, 13):
                keep = is_top if r == 0 else is_low
                cells, lo, hi = edge * keep, cl * keep, cr * keep
            else:
                cells = cell_row(f, r - 1).astype(F32)
                lo, hi = lefts[r - 1 : r], rights[r - 1 : r]
            put(f, r, 1, cells.astype(BF))
            put(f, r, 0, jnp.where(col == 0, lo, pltpu.roll(cells, 1, 0)).astype(BF))
            put(f, r, 2, jnp.where(col == 15, hi, pltpu.roll(cells, 15, 0)).astype(BF))


def put_back(wide):
    def put(f, r, which, cells):
        wide[f, r, :, (2 - which) * 256 : (3 - which) * 256] = cells

    return put


def weight_copies(weight, held, sem):
    return [
        pltpu.make_async_copy(weight.at[pl.ds(a * 9, 9)], held.at[pl.ds(a * 9, 9)], sem.at[a])
        for a in range(3)
    ]


def conv_sum(wide, held, total):
    for a in (2, 1, 0):
        frames = a + 2
        for b in range(3):
            window = wide[2 - a : 4, 2 - b : 14 - b].reshape(frames * 192, 768)
            part = None
            for e in range(3):
                one = lax.dot_general(
                    window[:, e * 256 : (e + 1) * 256],
                    held[(a * 3 + b) * 3 + e],
                    NT,
                    preferred_element_type=F32,
                )
                part = one if part is None else part + one
            if a == 2 and b == 0:
                total[...] = part
            else:
                total[0 : frames * 192] += part


def channel_order():
    lane = lax.broadcasted_iota(jnp.int32, (256, 256), 1)
    goal, kept = (x_place() + (lane >> 5)) & 3, lax.axis_index("core") ^ (lane >> 7)
    source = ((goal & 1) << 7) + ((goal >> 1) << 6) + (kept << 5) + (lane & 31)
    return (lax.broadcasted_iota(jnp.int32, (256, 256), 0) == source).astype(BF)


def film_kernel(
    step, inputs, hidden, table, weight, act_out, inp_out, slope, taps,
    film, blocks, sem, block_sem, tap_sem,
):
    start = step[0]
    whole = pl.multiple_of(start // 8 * 8, 8)
    film_copy = pltpu.make_async_copy(table.at[pl.ds(whole, 8)], film, sem)
    film_copy.start()
    block_copies = [
        pltpu.make_async_copy(ref, blocks.at[n], block_sem.at[n])
        for n, ref in enumerate((inputs, hidden))
    ]
    for copy in block_copies:
        copy.start()
    copies = weight_copies(weight, taps, tap_sem)
    for copy in copies:
        copy.start()
    order = channel_order()
    sort = lambda v: jnp.dot(v, order, preferred_element_type=F32).astype(BF)
    for copy in block_copies:
        copy.wait()
    film_copy.wait()
    inp_out[...] = sort(blocks[0].reshape(768, 256)).reshape(4, 12, 16, 256)
    line = film[pl.ds(start - whole, 1), :]
    scale, shift = 1.0 + line[:, 0:256], line[:, 256:512]
    shifted = blocks[1].reshape(768, 256).astype(F32) * scale + shift
    sigma = jax.nn.sigmoid(shifted)
    act_out[...] = sort((shifted * sigma).astype(BF))
    slope[...] = scale * sigma * (1.0 + shifted * (1.0 - sigma))
    for copy in copies:
        copy.wait()


def first_kernel(
    block, slope, row, left, right, corner_left, corner_right, taps, wide, hid_out, total,
):
    sides = (row, left, right, corner_left, corner_right)
    build_shifted(
        put_back(wide), lambda f, r: block[f, r], *[lambda f, s=s: s[0, f] for s in sides]
    )
    conv_sum(wide, taps, total)
    hid_out[...] = (total[...] * slope[...]).astype(BF).reshape(4, 12, 16, 256)


def input_conv_kernel(
    hid, block, row, left, right, after, weight, out, held, total, sem, wide
):
    del after
    copies = weight_copies(weight, held, sem)
    for copy in copies:
        copy.start()
    build_shifted(
        put_back(wide),
        lambda f, r: hid[f, r],
        lambda f: row[0, f],
        lambda f: left[f],
        lambda f: right[f],
        lambda f: row[1, f],
        lambda f: row[2, f],
    )
    for copy in copies:
        copy.wait()
    conv_sum(wide, held, total)
    grad = block[...].reshape(768, 256).astype(F32) + total[...]
    out[...] = grad.astype(BF).reshape(4, 12, 16, 256)


def second_part(wide, act, half, a, b):
    rows = (a + 2) * 192
    window = wide[2 - a : 4, 2 - b : 14 - b].reshape(rows, 768)
    left = act[0:rows, half * 128 : half * 128 + 128]
    return lax.dot_general(left, window, TN, preferred_element_type=F32)


def second_pair_kernel(wide, act, after, pair):
    del after
    for a in range(3):
        for b in range(3):
            pair[a * 3 + b] = second_part(wide, act, 1, a, b)


def second_own_kernel(wide, act, got, after, also, keep, one, two, three):
    del after, also
    for a in range(3):
        for b in range(3):
            total = second_part(wide, act, 0, a, b) + got[a * 3 + b]
            for d, out in enumerate((keep, one, two, three)):
                out[a * 3 + b] = total[d * 32 : d * 32 + 32].astype(out.dtype)


def second_x_kernel(got1, got2, got3, own, after, keep, one, two, three, held):
    del after
    y = lax.axis_index("y")

    def tap(t):
        ab, lanes = t // 3, slice(t % 3 * 256, t % 3 * 256 + 256)
        total = own[ab, :, lanes]
        for got in (got1, got2, got3):
            total = total + got[ab, :, lanes].astype(F32)
        return total

    for g in range(7):
        parts = [tap(t) if t < 27 else jnp.zeros((32, 256), F32) for t in range(4 * g, 4 * g + 4)]
        held[...] = jnp.concatenate(parts, axis=0).T.reshape(8, 4, 8, 128)
        for d, out in enumerate((keep, one, two, three)):
            out[g] = held[:, (y + d) & 3].reshape(64, 128).astype(out.dtype)


def first_grad_kernel(
    hid, inp, row, left, right, corner_left, corner_right, after, own, pair, wide, side,
):
    del after
    order = channel_order()
    for n, ref in enumerate((row, left, right, corner_left, corner_right)):
        cells = jnp.dot(ref[1].reshape(64, 256), order, preferred_element_type=F32)
        side[n] = cells.reshape(4, 16, 256)

    def put(f, r, which, cells):
        at = which * 128
        wide[f, r, :, at : at + 128] = cells[:, 0:128]
        wide[f, r, :, at + 384 : at + 512] = cells[:, 128:256]

    build_shifted(put, lambda f, r: inp[f, r], *[lambda f, n=n: side[n, f] for n in range(5)])
    for a in range(3):
        rows = (a + 2) * 192
        left = hid[2 - a : 4].reshape(rows, 256)
        for b in range(3):
            window = wide[0 : a + 2, b : b + 12].reshape(rows, 768)
            grad = lax.dot_general(left, window, TN, preferred_element_type=F32)
            grad = grad.reshape(8, 4, 8, 768)
            for q in range(4):
                piece = grad[:, q].reshape(64, 768)
                for e in range(3):
                    t = (a * 3 + b) * 3 + e
                    own[q, t] = piece[:, e * 128 : e * 128 + 128]
                    pair[q, t] = piece[:, e * 128 + 384 : e * 128 + 512]


def first_sum_kernel(own, pair, after, keep, one, two, three):
    del after
    y = lax.axis_index("y")
    for d, out in enumerate((keep, one, two, three)):
        q = (y + d) & 3
        out[...] = (own[q] + pair[q]).astype(out.dtype)


def first_y_kernel(got1, got2, got3, own, after, keep, one, two, three):
    del after

    def tap(t):
        total = own[t]
        for got in (got1, got2, got3):
            total = total + got[t].astype(F32)
        return total

    for g in range(7):
        taps = [tap(t) if t < 27 else jnp.zeros((64, 128), F32) for t in range(4 * g, 4 * g + 4)]
        for d, out in enumerate((keep, one, two, three)):
            piece = jnp.concatenate([v[:, d * 32 : d * 32 + 32] for v in taps], axis=1)
            out[g] = piece.astype(out.dtype)


def last_kernel(own_two, a1, a2, a3, own_one, b1, b2, b3, out, keep, held):
    for n, (own, got) in enumerate(((own_two, (a1, a2, a3)), (own_one, (b1, b2, b3)))):
        total = own[...]
        for ref in got:
            total = total + ref[...].astype(F32)
        held[n] = total.reshape(7, 8, 8, 128)

    def plane(z):
        return jnp.concatenate([held[n, :, z].reshape(56, 128) for n in range(2)], axis=0)

    for q in range(8):
        out[q] = plane(q).astype(BF)
    keep[...] = plane(lax.axis_index("z"))


def final_kernel(factor, got, own, one, two):
    z = lax.axis_index("z")
    total = own[...]
    for d in range(1, 8):
        total = total + got[(z + d) & 7].astype(F32)
    total = (total * factor).reshape(2, 7, 8, 128)
    for out, which in ((two, 0), (one, 1)):
        for t in range(27):
            out[t] = total[which, t // 4, :, t % 4 * 32 : t % 4 * 32 + 32]


def shards(activations, saved_hidden, cotangent, conv_one, conv_two, film_table, timesteps):
    inputs, hidden, block = activations[0], saved_hidden[0], cotangent[0]
    taps_one = conv_one.transpose(1, 2, 3, 0, 4).reshape(27, 256, 256)
    taps_two = conv_two.transpose(1, 2, 3, 0, 4).reshape(27, 256, 256)
    wide = near((4, 14, 16, 768), BF)
    quads = [near((7, 64, 128), F32)] + [near((7, 64, 128), BF)] * 3

    def ring(parts, axis):
        return [send(parts[d - 1], ring_pairs(**{axis: d})) for d in (2, 1, 3)]

    packed = call(
        pack_kernel,
        "pack_first",
        (block, inputs),
        "pp",
        [near((2, 4, 16, 256), BF)] * 5,
        [pltpu.VMEM((2, 768, 128), F32)],
    )
    ways = ((1, 0), (0, 1), (0, -1), (1, 1), (1, -1))
    sides = [send(p, block_pairs(*way)) for p, way in zip(packed, ways)]
    act, inp, slope, held_two = call(
        film_kernel,
        "film",
        (timesteps, inputs, hidden, film_table, taps_two),
        "shhhh",
        [
            near((768, 256), BF),
            near((4, 12, 16, 256), BF),
            near((768, 256), F32),
            near((27, 256, 256), BF),
        ],
        [
            pltpu.VMEM((8, 512), F32),
            pltpu.VMEM((2, 4, 12, 16, 256), BF),
            pltpu.SemaphoreType.DMA,
            pltpu.SemaphoreType.DMA((2,)),
            pltpu.SemaphoreType.DMA((3,)),
        ],
    )
    wide_cot, grad_hidden = call(
        first_kernel,
        "conv_two_back",
        (block, slope, *sides, held_two),
        "pv" + "v" * 5 + "v",
        [wide, near((4, 12, 16, 256), BF)],
        [pltpu.VMEM((768, 256), F32)],
    )

    hi, lo = call(
        pack_columns_kernel,
        "pack_columns",
        (grad_hidden,),
        "v",
        [near((4, 16, 256), BF)] * 2,
        [pltpu.VMEM((2, 768, 128), F32)],
    )
    left, right = send(hi, block_pairs(0, 1)), send(lo, block_pairs(0, -1))
    (pair_two,) = call(
        second_pair_kernel, "grad_two_pair", (wide_cot, act, hi), "vvv", [near((9, 128, 768), F32)]
    )
    got_pair_two = send(pair_two, core_pairs())
    (row,) = call(
        pack_rows_kernel,
        "pack_rows",
        (grad_hidden, left, right, pair_two),
        "vvvv",
        [near((3, 4, 16, 256), BF)],
    )
    got_row = send(row, block_pairs(1, 0))
    split = near((4, 27, 64, 128), F32)
    own_one, pair_one = call(
        first_grad_kernel,
        "grad_one",
        (grad_hidden, inp, *sides, row),
        "vv" + "v" * 5 + "v",
        [split, split],
        [pltpu.VMEM((4, 14, 16, 768), BF), pltpu.VMEM((5, 4, 16, 256), F32)],
    )
    got_pair_one = send(pair_one, core_pairs())
    own_two, *parts = call(
        second_own_kernel,
        "grad_two_own",
        (wide_cot, act, got_pair_two, got_row, pair_one),
        "vvvvv",
        [near((9, 32, 768), F32)] + [near((9, 32, 768), BF)] * 3,
    )
    got_two = ring(parts, "dx")
    own_one, *parts_one = call(
        first_sum_kernel,
        "grad_one_sum",
        (own_one, got_pair_one, parts[0]),
        "vvv",
        [near((27, 64, 128), F32)] + [near((27, 64, 128), BF)] * 3,
    )
    got_one = ring(parts_one, "dy")

    (grad_input,) = call(
        input_conv_kernel,
        "conv_one_back",
        (grad_hidden, block, got_row, left, right, parts_one[0], taps_one),
        "vpvvvvh",
        [(jax.ShapeDtypeStruct((4, 12, 16, 256), BF), "v")],
        [
            pltpu.VMEM((27, 256, 256), BF),
            pltpu.VMEM((768, 256), F32),
            pltpu.SemaphoreType.DMA((3,)),
            pltpu.VMEM((4, 14, 16, 768), BF),
        ],
    )

    own_two, *parts = call(
        second_x_kernel,
        "grad_two_x",
        (*got_two, own_two, grad_input),
        "vvvvh",
        quads,
        [pltpu.VMEM((8, 4, 8, 128), F32)],
    )
    got_two = ring(parts, "dy")
    own_one, *parts_one = call(
        first_y_kernel, "grad_one_y", (*got_one, own_one, parts[0]), "vvvvv", quads
    )
    got_one = ring(parts_one, "dx")

    out, own = call(
        last_kernel,
        "last_stage",
        (own_two, *got_two, own_one, *got_one),
        "v" * 8,
        [far((8, 112, 128), BF), near((112, 128), F32)],
        [pltpu.VMEM((2, 7, 8, 8, 128), F32)],
    )
    planes = lax.all_to_all(out, "z", 0, 0, tiled=True)
    factor = float(256 * 768) ** (-0.5)
    result = jax.ShapeDtypeStruct((27, 8, 32), F32), "v"
    grad_one, grad_two = call(
        functools.partial(final_kernel, factor), "final_sum", (planes, own), "vv", [result, result]
    )
    shape = lambda g: g.transpose(2, 0, 1).reshape(32, 3, 3, 3, 8)
    return grad_input[None], shape(grad_one), shape(grad_two)


def solution(mesh):
    fine = Mesh(mesh.devices.reshape(SIZES), AX)
    clip = ("z", "y")
    placed = P(clip, None, "ha", ("xh", "core"), None)
    weight = P(("ha", "xh", "core"), None, None, None, clip)
    return jax.shard_map(
        shards,
        mesh=fine,
        in_specs=(placed, placed, placed, P(), P(), P(), P(clip)),
        out_specs=(placed, weight, weight),
        check_vma=False,
    )
```

```python
import functools

import jax
import jax.numpy as jnp
from jax import lax
from jax.experimental import pallas as pl
from jax.experimental.pallas import tpu as pltpu
from jax.sharding import Mesh
from jax.sharding import PartitionSpec as P

BF = jnp.bfloat16
F32 = jnp.float32
AX = ("z", "y", "ha", "xh", "core")
SIZES = (8, 4, 2, 2, 2)
VM = pl.BlockSpec(memory_space=pltpu.VMEM)
HB = pl.BlockSpec(memory_space=pl.ANY)
SM = pl.BlockSpec(memory_space=pltpu.SMEM)
NT = (((1,), (1,)), ((), ()))
TN = (((0,), (0,)), ((), ()))


def core_pairs():
    return [(i, i ^ 1) for i in range(256)]


def block_pairs(dh, dw):
    return [(i, i // 8 * 8 + (i // 4 % 2 ^ dh) * 4 + (i + dw) % 4) for i in range(256)]


def ring_pairs(dx=0, dy=0):
    pairs = []
    for i in range(256):
        core, xh, ha, y, z = i % 2, i // 2 % 2, i // 4 % 2, i // 8 % 4, i // 32
        x, y = (xh * 2 + ha + dx) % 4, (y + dy) % 4
        pairs.append((i, ((z * 4 + y) * 2 + x % 2) * 4 + x // 2 * 2 + core))
    return pairs


def send(value, pairs):
    return lax.ppermute(value, AX, pairs)


def call(kernel, name, args, spaces, outs, scratch=(), limit=16):
    where = {"v": pltpu.VMEM, "p": pltpu.HBM, "h": pltpu.HBM}
    args = [
        pltpu.with_memory_space_constraint(a, where[s]) if s in where else a
        for a, s in zip(args, spaces)
    ]
    specs = {"v": VM, "p": VM, "h": HB, "s": SM}
    return pl.pallas_call(
        kernel,
        out_shape=tuple(o for o, _ in outs),
        in_specs=[specs[s] for s in spaces],
        out_specs=tuple(specs[s] for _, s in outs),
        scratch_shapes=list(scratch),
        compiler_params=pltpu.CompilerParams(vmem_limit_bytes=limit * 2**20),
        name=name,
    )(*args)


def near(shape, dtype):
    return pltpu.VMEM(shape, dtype), "v"


def far(shape, dtype):
    return pltpu.HBM(shape, dtype), "p"


def x_place():
    return lax.axis_index("xh") * 2 + lax.axis_index("ha")


def column(wide, lanes_half, f, j):
    cells = wide[lanes_half, pl.ds(f * 192 + j, 12, stride=16), :]
    return jnp.concatenate([cells, jnp.zeros((4, 128), F32)], axis=0).astype(BF)


def spread(wide, block):
    flat = block[...].reshape(768, 256).astype(F32)
    wide[0] = flat[:, 0:128]
    wide[1] = flat[:, 128:256]


def pack_kernel(one, two, row, hi, lo, corner_hi, corner_lo, wide):
    edge = 11 * (1 - lax.axis_index("ha"))
    for n, block in enumerate((one, two)):
        spread(wide, block)
        for f in range(4):
            row[n, f] = block[f, edge]
            for j, out, corner in ((15, hi, corner_hi), (0, lo, corner_lo)):
                for h in range(2):
                    lanes = slice(h * 128, h * 128 + 128)
                    out[n, f, :, lanes] = column(wide, h, f, j)
                    cell = wide[h, pl.ds(f * 192 + edge * 16 + j, 1), :]
                    corner[n, f, :, lanes] = jnp.broadcast_to(cell, (16, 128)).astype(BF)


def pack_columns_kernel(block, after, hi, lo, wide):
    del after
    spread(wide, block)
    for f in range(4):
        for j, out in ((15, hi), (0, lo)):
            for h in range(2):
                out[f, :, h * 128 : h * 128 + 128] = column(wide, h, f, j)


def pack_rows_kernel(block, left, right, after, row):
    del after
    edge = 11 * (1 - lax.axis_index("ha"))
    for f in range(4):
        row[0, f] = block[f, edge]
        for n, side in ((1, left), (2, right)):
            cells = side[f].astype(F32)
            cell = jnp.where(edge == 0, cells[0:1], cells[11:12])
            row[n, f] = jnp.broadcast_to(cell, (16, 256)).astype(BF)


def build_shifted(put, cell_row, row, left, right, corner_left, corner_right):
    ha, wa = lax.axis_index("ha"), lax.axis_index("xh") * 2 + lax.axis_index("core")
    col = lax.broadcasted_iota(jnp.int32, (16, 256), 0)
    is_top, is_low = (ha == 1).astype(F32), (ha == 0).astype(F32)
    has_left, has_right = (wa > 0).astype(F32), (wa < 3).astype(F32)
    for f in range(4):
        edge = row(f).astype(F32)
        lefts, rights = left(f).astype(F32) * has_left, right(f).astype(F32) * has_right
        cl = corner_left(f).astype(F32)[0:1] * has_left
        cr = corner_right(f).astype(F32)[0:1] * has_right
        for r in range(14):
            if r in (0, 13):
                keep = is_top if r == 0 else is_low
                cells, lo, hi = edge * keep, cl * keep, cr * keep
            else:
                cells = cell_row(f, r - 1).astype(F32)
                lo, hi = lefts[r - 1 : r], rights[r - 1 : r]
            put(f, r, 1, cells.astype(BF))
            put(f, r, 0, jnp.where(col == 0, lo, pltpu.roll(cells, 1, 0)).astype(BF))
            put(f, r, 2, jnp.where(col == 15, hi, pltpu.roll(cells, 15, 0)).astype(BF))


def put_back(wide):
    def put(f, r, which, cells):
        wide[f, r, :, (2 - which) * 256 : (3 - which) * 256] = cells

    return put


def weight_copies(weight, held, sem):
    return [
        pltpu.make_async_copy(weight.at[pl.ds(a * 9, 9)], held.at[pl.ds(a * 9, 9)], sem.at[a])
        for a in range(3)
    ]


def conv_sum(wide, held, total):
    for a in (2, 1, 0):
        frames = a + 2
        for b in range(3):
            window = wide[2 - a : 4, 2 - b : 14 - b].reshape(frames * 192, 768)
            part = None
            for e in range(3):
                one = lax.dot_general(
                    window[:, e * 256 : (e + 1) * 256],
                    held[(a * 3 + b) * 3 + e],
                    NT,
                    preferred_element_type=F32,
                )
                part = one if part is None else part + one
            if a == 2 and b == 0:
                total[...] = part
            else:
                total[0 : frames * 192] += part


def channel_order():
    lane = lax.broadcasted_iota(jnp.int32, (256, 256), 1)
    goal, kept = (x_place() + (lane >> 5)) & 3, lax.axis_index("core") ^ (lane >> 7)
    source = ((goal & 1) << 7) + ((goal >> 1) << 6) + (kept << 5) + (lane & 31)
    return (lax.broadcasted_iota(jnp.int32, (256, 256), 0) == source).astype(BF)


def film_kernel(
    step, inputs, hidden, table, weight, act_out, inp_out, slope, taps,
    film, blocks, sem, block_sem, tap_sem,
):
    start = step[0]
    whole = pl.multiple_of(start // 8 * 8, 8)
    film_copy = pltpu.make_async_copy(table.at[pl.ds(whole, 8)], film, sem)
    film_copy.start()
    block_copies = [
        pltpu.make_async_copy(ref, blocks.at[n], block_sem.at[n])
        for n, ref in enumerate((inputs, hidden))
    ]
    for copy in block_copies:
        copy.start()
    copies = weight_copies(weight, taps, tap_sem)
    for copy in copies:
        copy.start()
    order = channel_order()
    sort = lambda v: jnp.dot(v, order, preferred_element_type=F32).astype(BF)
    for copy in block_copies:
        copy.wait()
    film_copy.wait()
    inp_out[...] = sort(blocks[0].reshape(768, 256)).reshape(4, 12, 16, 256)
    line = film[pl.ds(start - whole, 1), :]
    scale, shift = 1.0 + line[:, 0:256], line[:, 256:512]
    shifted = blocks[1].reshape(768, 256).astype(F32) * scale + shift
    sigma = jax.nn.sigmoid(shifted)
    act_out[...] = sort((shifted * sigma).astype(BF))
    slope[...] = scale * sigma * (1.0 + shifted * (1.0 - sigma))
    for copy in copies:
        copy.wait()


def first_kernel(
    block, slope, row, left, right, corner_left, corner_right, taps, wide, hid_out, total,
):
    sides = (row, left, right, corner_left, corner_right)
    build_shifted(
        put_back(wide), lambda f, r: block[f, r], *[lambda f, s=s: s[0, f] for s in sides]
    )
    conv_sum(wide, taps, total)
    hid_out[...] = (total[...] * slope[...]).astype(BF).reshape(4, 12, 16, 256)


def input_conv_kernel(
    hid, block, row, left, right, after, weight, out, held, total, sem, wide
):
    del after
    copies = weight_copies(weight, held, sem)
    for copy in copies:
        copy.start()
    build_shifted(
        put_back(wide),
        lambda f, r: hid[f, r],
        lambda f: row[0, f],
        lambda f: left[f],
        lambda f: right[f],
        lambda f: row[1, f],
        lambda f: row[2, f],
    )
    for copy in copies:
        copy.wait()
    conv_sum(wide, held, total)
    grad = block[...].reshape(768, 256).astype(F32) + total[...]
    out[...] = grad.astype(BF).reshape(4, 12, 16, 256)


def second_part(wide, act, half, a, b):
    rows = (a + 2) * 192
    window = wide[2 - a : 4, 2 - b : 14 - b].reshape(rows, 768)
    left = act[0:rows, half * 128 : half * 128 + 128]
    return lax.dot_general(left, window, TN, preferred_element_type=F32)


def second_pair_kernel(wide, act, pair):
    for a in range(3):
        for b in range(3):
            pair[a * 3 + b] = second_part(wide, act, 1, a, b)


def second_own_kernel(wide, act, got, after, also, keep, one, two, three):
    del after, also
    for a in range(3):
        for b in range(3):
            total = second_part(wide, act, 0, a, b) + got[a * 3 + b]
            for d, out in enumerate((keep, one, two, three)):
                out[a * 3 + b] = total[d * 32 : d * 32 + 32].astype(out.dtype)


def second_x_kernel(got1, got2, got3, own, after, keep, one, two, three, held):
    del after
    y = lax.axis_index("y")

    def tap(t):
        ab, lanes = t // 3, slice(t % 3 * 256, t % 3 * 256 + 256)
        total = own[ab, :, lanes]
        for got in (got1, got2, got3):
            total = total + got[ab, :, lanes].astype(F32)
        return total

    for g in range(7):
        parts = [tap(t) if t < 27 else jnp.zeros((32, 256), F32) for t in range(4 * g, 4 * g + 4)]
        held[...] = jnp.concatenate(parts, axis=0).T.reshape(8, 4, 8, 128)
        for d, out in enumerate((keep, one, two, three)):
            out[g] = held[:, (y + d) & 3].reshape(64, 128).astype(out.dtype)


def first_grad_kernel(
    hid, inp, row, left, right, corner_left, corner_right, after, own, pair, wide, side,
):
    del after
    order = channel_order()
    for n, ref in enumerate((row, left, right, corner_left, corner_right)):
        cells = jnp.dot(ref[1].reshape(64, 256), order, preferred_element_type=F32)
        side[n] = cells.reshape(4, 16, 256)

    def put(f, r, which, cells):
        at = which * 128
        wide[f, r, :, at : at + 128] = cells[:, 0:128]
        wide[f, r, :, at + 384 : at + 512] = cells[:, 128:256]

    build_shifted(put, lambda f, r: inp[f, r], *[lambda f, n=n: side[n, f] for n in range(5)])
    for a in range(3):
        rows = (a + 2) * 192
        left = hid[2 - a : 4].reshape(rows, 256)
        for b in range(3):
            window = wide[0 : a + 2, b : b + 12].reshape(rows, 768)
            grad = lax.dot_general(left, window, TN, preferred_element_type=F32)
            grad = grad.reshape(8, 4, 8, 768)
            for q in range(4):
                piece = grad[:, q].reshape(64, 768)
                for e in range(3):
                    t = (a * 3 + b) * 3 + e
                    own[q, t] = piece[:, e * 128 : e * 128 + 128]
                    pair[q, t] = piece[:, e * 128 + 384 : e * 128 + 512]


def first_sum_kernel(own, pair, after, keep, one, two, three):
    del after
    y = lax.axis_index("y")
    for d, out in enumerate((keep, one, two, three)):
        q = (y + d) & 3
        out[...] = (own[q] + pair[q]).astype(out.dtype)


def first_y_kernel(got1, got2, got3, own, after, keep, one, two, three):
    del after

    def tap(t):
        total = own[t]
        for got in (got1, got2, got3):
            total = total + got[t].astype(F32)
        return total

    for g in range(7):
        taps = [tap(t) if t < 27 else jnp.zeros((64, 128), F32) for t in range(4 * g, 4 * g + 4)]
        for d, out in enumerate((keep, one, two, three)):
            piece = jnp.concatenate([v[:, d * 32 : d * 32 + 32] for v in taps], axis=1)
            out[g] = piece.astype(out.dtype)


def last_kernel(own_two, a1, a2, a3, own_one, b1, b2, b3, out, keep, held):
    for n, (own, got) in enumerate(((own_two, (a1, a2, a3)), (own_one, (b1, b2, b3)))):
        total = own[...]
        for ref in got:
            total = total + ref[...].astype(F32)
        held[n] = total.reshape(7, 8, 8, 128)

    def plane(z):
        return jnp.concatenate([held[n, :, z].reshape(56, 128) for n in range(2)], axis=0)

    for q in range(8):
        out[q] = plane(q).astype(BF)
    keep[...] = plane(lax.axis_index("z"))


def final_kernel(factor, got, own, after, one, two):
    del after
    z = lax.axis_index("z")
    total = own[...]
    for d in range(1, 8):
        total = total + got[(z + d) & 7].astype(F32)
    total = (total * factor).reshape(2, 7, 8, 128)
    for out, which in ((two, 0), (one, 1)):
        for t in range(27):
            out[t] = total[which, t // 4, :, t % 4 * 32 : t % 4 * 32 + 32]


def shards(activations, saved_hidden, cotangent, conv_one, conv_two, film_table, timesteps):
    inputs, hidden, block = activations[0], saved_hidden[0], cotangent[0]
    taps_one = conv_one.transpose(1, 2, 3, 0, 4).reshape(27, 256, 256)
    taps_two = conv_two.transpose(1, 2, 3, 0, 4).reshape(27, 256, 256)
    wide = near((4, 14, 16, 768), BF)
    quads = [near((7, 64, 128), F32)] + [near((7, 64, 128), BF)] * 3

    def ring(parts, axis):
        return [send(parts[d - 1], ring_pairs(**{axis: d})) for d in (2, 1, 3)]

    packed = call(
        pack_kernel,
        "pack_first",
        (block, inputs),
        "pp",
        [near((2, 4, 16, 256), BF)] * 5,
        [pltpu.VMEM((2, 768, 128), F32)],
    )
    ways = ((1, 0), (0, 1), (0, -1), (1, 1), (1, -1))
    sides = [send(p, block_pairs(*way)) for p, way in zip(packed, ways)]
    act, inp, slope, held_two = call(
        film_kernel,
        "film",
        (timesteps, inputs, hidden, film_table, taps_two),
        "shhhh",
        [
            near((768, 256), BF),
            near((4, 12, 16, 256), BF),
            near((768, 256), F32),
            near((27, 256, 256), BF),
        ],
        [
            pltpu.VMEM((8, 512), F32),
            pltpu.VMEM((2, 4, 12, 16, 256), BF),
            pltpu.SemaphoreType.DMA,
            pltpu.SemaphoreType.DMA((2,)),
            pltpu.SemaphoreType.DMA((3,)),
        ],
    )
    wide_cot, grad_hidden = call(
        first_kernel,
        "conv_two_back",
        (block, slope, *sides, held_two),
        "pv" + "v" * 5 + "v",
        [wide, near((4, 12, 16, 256), BF)],
        [pltpu.VMEM((768, 256), F32)],
    )

    (pair_two,) = call(
        second_pair_kernel, "grad_two_pair", (wide_cot, act), "vv", [near((9, 128, 768), F32)]
    )
    got_pair_two = send(pair_two, core_pairs())
    split = near((4, 27, 64, 128), F32)
    own_one, pair_one = call(
        first_grad_kernel,
        "grad_one",
        (grad_hidden, inp, *sides, pair_two),
        "vv" + "v" * 5 + "v",
        [split, split],
        [pltpu.VMEM((4, 14, 16, 768), BF), pltpu.VMEM((5, 4, 16, 256), F32)],
    )
    got_pair_one = send(pair_one, core_pairs())
    hi, lo = call(
        pack_columns_kernel,
        "pack_columns",
        (grad_hidden, pair_one),
        "vv",
        [near((4, 16, 256), BF)] * 2,
        [pltpu.VMEM((2, 768, 128), F32)],
    )
    left, right = send(hi, block_pairs(0, 1)), send(lo, block_pairs(0, -1))
    own_two, *parts = call(
        second_own_kernel,
        "grad_two_own",
        (wide_cot, act, got_pair_two, left, right),
        "vvvvv",
        [near((9, 32, 768), F32)] + [near((9, 32, 768), BF)] * 3,
    )
    got_two = ring(parts, "dx")
    own_one, *parts_one = call(
        first_sum_kernel,
        "grad_one_sum",
        (own_one, got_pair_one, parts[0]),
        "vvv",
        [near((27, 64, 128), F32)] + [near((27, 64, 128), BF)] * 3,
    )
    got_one = ring(parts_one, "dy")

    (row,) = call(
        pack_rows_kernel,
        "pack_rows",
        (grad_hidden, left, right, parts_one[0]),
        "vvvv",
        [near((3, 4, 16, 256), BF)],
    )
    row = send(row, block_pairs(1, 0))

    own_two, *parts = call(
        second_x_kernel,
        "grad_two_x",
        (*got_two, own_two, row),
        "vvvvv",
        quads,
        [pltpu.VMEM((8, 4, 8, 128), F32)],
    )
    got_two = ring(parts, "dy")
    own_one, *parts_one = call(
        first_y_kernel, "grad_one_y", (*got_one, own_one, parts[0]), "vvvvv", quads
    )
    got_one = ring(parts_one, "dx")

    out, own = call(
        last_kernel,
        "last_stage",
        (own_two, *got_two, own_one, *got_one),
        "v" * 8,
        [far((8, 112, 128), BF), near((112, 128), F32)],
        [pltpu.VMEM((2, 7, 8, 8, 128), F32)],
    )
    planes = lax.all_to_all(out, "z", 0, 0, tiled=True)

    (grad_input,) = call(
        input_conv_kernel,
        "conv_one_back",
        (grad_hidden, block, row, left, right, own, taps_one),
        "vpvvvvh",
        [(jax.ShapeDtypeStruct((4, 12, 16, 256), BF), "v")],
        [
            pltpu.VMEM((27, 256, 256), BF),
            pltpu.VMEM((768, 256), F32),
            pltpu.SemaphoreType.DMA((3,)),
            pltpu.VMEM((4, 14, 16, 768), BF),
        ],
    )

    factor = float(256 * 768) ** (-0.5)
    result = jax.ShapeDtypeStruct((27, 8, 32), F32), "v"
    grad_one, grad_two = call(
        functools.partial(final_kernel, factor), "final_sum", (planes, own, grad_input), "vvh", [result, result]
    )
    shape = lambda g: g.transpose(2, 0, 1).reshape(32, 3, 3, 3, 8)
    return grad_input[None], shape(grad_one), shape(grad_two)


def solution(mesh):
    fine = Mesh(mesh.devices.reshape(SIZES), AX)
    clip = ("z", "y")
    placed = P(clip, None, "ha", ("xh", "core"), None)
    weight = P(("ha", "xh", "core"), None, None, None, clip)
    return jax.shard_map(
        shards,
        mesh=fine,
        in_specs=(placed, placed, placed, P(), P(), P(), P(clip)),
        out_specs=(placed, weight, weight),
        check_vma=False,
    )
```

```python
import functools

import jax
import jax.numpy as jnp
from jax import lax
from jax.experimental import pallas as pl
from jax.experimental.pallas import tpu as pltpu
from jax.sharding import Mesh
from jax.sharding import PartitionSpec as P

BF = jnp.bfloat16
F32 = jnp.float32
AX = ("z", "y", "ha", "xh", "core")
SIZES = (8, 4, 2, 2, 2)
VM = pl.BlockSpec(memory_space=pltpu.VMEM)
HB = pl.BlockSpec(memory_space=pl.ANY)
SM = pl.BlockSpec(memory_space=pltpu.SMEM)
NT = (((1,), (1,)), ((), ()))
TN = (((0,), (0,)), ((), ()))


def core_pairs():
    return [(i, i ^ 1) for i in range(256)]


def block_pairs(dh, dw):
    return [(i, i // 8 * 8 + (i // 4 % 2 ^ dh) * 4 + (i + dw) % 4) for i in range(256)]


def ring_pairs(dx=0, dy=0):
    pairs = []
    for i in range(256):
        core, xh, ha, y, z = i % 2, i // 2 % 2, i // 4 % 2, i // 8 % 4, i // 32
        x, y = (xh * 2 + ha + dx) % 4, (y + dy) % 4
        pairs.append((i, ((z * 4 + y) * 2 + x % 2) * 4 + x // 2 * 2 + core))
    return pairs


def send(value, pairs):
    return lax.ppermute(value, AX, pairs)


def call(kernel, name, args, spaces, outs, scratch=(), limit=16):
    where = {"v": pltpu.VMEM, "p": pltpu.HBM, "h": pltpu.HBM}
    args = [
        pltpu.with_memory_space_constraint(a, where[s]) if s in where else a
        for a, s in zip(args, spaces)
    ]
    specs = {"v": VM, "p": VM, "h": HB, "s": SM}
    return pl.pallas_call(
        kernel,
        out_shape=tuple(o for o, _ in outs),
        in_specs=[specs[s] for s in spaces],
        out_specs=tuple(specs[s] for _, s in outs),
        scratch_shapes=list(scratch),
        compiler_params=pltpu.CompilerParams(vmem_limit_bytes=limit * 2**20),
        name=name,
    )(*args)


def near(shape, dtype):
    return pltpu.VMEM(shape, dtype), "v"


def far(shape, dtype):
    return pltpu.HBM(shape, dtype), "p"


def x_place():
    return lax.axis_index("xh") * 2 + lax.axis_index("ha")


def column(wide, lanes_half, f, j):
    cells = wide[lanes_half, pl.ds(f * 192 + j, 12, stride=16), :]
    return jnp.concatenate([cells, jnp.zeros((4, 128), F32)], axis=0)


def spread(wide, block):
    flat = block[...].reshape(768, 256).astype(F32)
    wide[0] = flat[:, 0:128]
    wide[1] = flat[:, 128:256]


def pack_kernel(one, two, row, hi, lo, corner_hi, corner_lo, wide):
    edge = 11 * (1 - lax.axis_index("ha"))
    for n, block in enumerate((one, two)):
        spread(wide, block)
        for f in range(4):
            row[n, f] = block[f, edge]
            for j, out, corner in ((15, hi, corner_hi), (0, lo, corner_lo)):
                for h in range(2):
                    lanes = slice(h * 128, h * 128 + 128)
                    out[n, f, :, lanes] = column(wide, h, f, j).astype(BF)
                    cell = wide[h, pl.ds(f * 192 + edge * 16 + j, 1), :]
                    corner[n, f, :, lanes] = jnp.broadcast_to(cell, (16, 128)).astype(BF)


def build_shifted(put, cell_row, row, left, right, corner_left, corner_right):
    ha, wa = lax.axis_index("ha"), lax.axis_index("xh") * 2 + lax.axis_index("core")
    col = lax.broadcasted_iota(jnp.int32, (16, 256), 0)
    is_top, is_low = (ha == 1).astype(F32), (ha == 0).astype(F32)
    has_left, has_right = (wa > 0).astype(F32), (wa < 3).astype(F32)
    for f in range(4):
        edge = row(f).astype(F32)
        lefts, rights = left(f).astype(F32) * has_left, right(f).astype(F32) * has_right
        cl = corner_left(f).astype(F32)[0:1] * has_left
        cr = corner_right(f).astype(F32)[0:1] * has_right
        for r in range(14):
            if r in (0, 13):
                keep = is_top if r == 0 else is_low
                cells, lo, hi = edge * keep, cl * keep, cr * keep
            else:
                cells = cell_row(f, r - 1).astype(F32)
                lo, hi = lefts[r - 1 : r], rights[r - 1 : r]
            put(f, r, 1, cells.astype(BF))
            put(f, r, 0, jnp.where(col == 0, lo, pltpu.roll(cells, 1, 0)).astype(BF))
            put(f, r, 2, jnp.where(col == 15, hi, pltpu.roll(cells, 15, 0)).astype(BF))


def put_back(wide):
    def put(f, r, which, cells):
        wide[f, r, :, (2 - which) * 256 : (3 - which) * 256] = cells

    return put


def weight_copies(weight, held, sem):
    return [
        pltpu.make_async_copy(weight.at[pl.ds(a * 9, 9)], held.at[pl.ds(a * 9, 9)], sem.at[a])
        for a in range(3)
    ]


def conv_sum(wide, held, total):
    for a in (2, 1, 0):
        frames = a + 2
        for b in range(3):
            window = wide[2 - a : 4, 2 - b : 14 - b].reshape(frames * 192, 768)
            part = None
            for e in range(3):
                one = lax.dot_general(
                    window[:, e * 256 : (e + 1) * 256],
                    held[(a * 3 + b) * 3 + e],
                    NT,
                    preferred_element_type=F32,
                )
                part = one if part is None else part + one
            if a == 2 and b == 0:
                total[...] = part
            else:
                total[0 : frames * 192] += part


def channel_order():
    lane = lax.broadcasted_iota(jnp.int32, (256, 256), 1)
    goal, kept = (x_place() + (lane >> 5)) & 3, lax.axis_index("core") ^ (lane >> 7)
    source = ((goal & 1) << 7) + ((goal >> 1) << 6) + (kept << 5) + (lane & 31)
    return (lax.broadcasted_iota(jnp.int32, (256, 256), 0) == source).astype(BF)


def film_kernel(
    step, inputs, hidden, table, weight, act_out, inp_out, slope, taps,
    film, blocks, sem, block_sem, tap_sem,
):
    start = step[0]
    whole = pl.multiple_of(start // 8 * 8, 8)
    film_copy = pltpu.make_async_copy(table.at[pl.ds(whole, 8)], film, sem)
    film_copy.start()
    block_copies = [
        pltpu.make_async_copy(ref, blocks.at[n], block_sem.at[n])
        for n, ref in enumerate((inputs, hidden))
    ]
    for copy in block_copies:
        copy.start()
    copies = weight_copies(weight, taps, tap_sem)
    for copy in copies:
        copy.start()
    order = channel_order()
    sort = lambda v: jnp.dot(v, order, preferred_element_type=F32).astype(BF)
    for copy in block_copies:
        copy.wait()
    film_copy.wait()
    inp_out[...] = sort(blocks[0].reshape(768, 256)).reshape(4, 12, 16, 256)
    line = film[pl.ds(start - whole, 1), :]
    scale, shift = 1.0 + line[:, 0:256], line[:, 256:512]
    shifted = blocks[1].reshape(768, 256).astype(F32) * scale + shift
    sigma = jax.nn.sigmoid(shifted)
    act_out[...] = sort((shifted * sigma).astype(BF))
    slope[...] = scale * sigma * (1.0 + shifted * (1.0 - sigma))
    for copy in copies:
        copy.wait()


def first_kernel(
    block, slope, row, left, right, corner_left, corner_right, taps, wide, hid_out, total,
):
    sides = (row, left, right, corner_left, corner_right)
    build_shifted(
        put_back(wide), lambda f, r: block[f, r], *[lambda f, s=s: s[0, f] for s in sides]
    )
    conv_sum(wide, taps, total)
    hid_out[...] = (total[...] * slope[...]).astype(BF).reshape(4, 12, 16, 256)


def input_conv_kernel(hid, block, border, face, after, weight, out, held, total, sem, wide):
    del after
    copies = weight_copies(weight, held, sem)
    for copy in copies:
        copy.start()
    is_one = lax.axis_index("core") == 1

    def pick(when_one, when_zero):
        return jnp.where(is_one, when_one.astype(F32), when_zero.astype(F32))

    faces, outers = border[8].astype(F32), border[9].astype(F32)[4:8]
    build_shifted(
        put_back(wide),
        lambda f, r: hid[f, r],
        lambda f: border[f],
        lambda f: pick(face[f], border[4 + f]),
        lambda f: pick(border[4 + f], face[f]),
        lambda f: pick(faces[f : f + 1], outers[f : f + 1]),
        lambda f: pick(outers[f : f + 1], faces[f : f + 1]),
    )
    for copy in copies:
        copy.wait()
    conv_sum(wide, held, total)
    grad = block[...].reshape(768, 256).astype(F32) + total[...]
    out[...] = grad.astype(BF).reshape(4, 12, 16, 256)


def second_part(wide, act, half, a, b):
    rows = (a + 2) * 192
    window = wide[2 - a : 4, 2 - b : 14 - b].reshape(rows, 768)
    left = act[0:rows, half * 128 : half * 128 + 128]
    return lax.dot_general(left, window, TN, preferred_element_type=F32)


def tile(n):
    return slice(n // 3 * 16, n // 3 * 16 + 16), slice(n % 3 * 256, n % 3 * 256 + 256)


def second_pair_kernel(wide, act, hid, pair, flat):
    spread(flat, hid)
    pair[9] = jnp.zeros((128, 768), F32)
    for f in range(4):
        for n, j in ((f, 15), (4 + f, 0)):
            rows, lanes = tile(n)
            for h in range(2):
                at = slice(lanes.start + h * 128, lanes.start + h * 128 + 128)
                pair[9, rows, at] = column(flat, h, f, j)
    for a in range(3):
        for b in range(3):
            pair[a * 3 + b] = second_part(wide, act, 1, a, b)


def second_own_kernel(wide, act, hid, got, after, keep, one, two, three, face_out):
    del after
    is_one = lax.axis_index("core") == 1
    edge = 11 * (1 - lax.axis_index("ha"))
    faces, outers = [], []
    for f in range(4):
        hi, lo = got[(9, *tile(f))], got[(9, *tile(4 + f))]
        face, outer = jnp.where(is_one, hi, lo), jnp.where(is_one, lo, hi)
        face_out[f] = face.astype(BF)
        two[(9, *tile(f))] = outer.astype(BF)
        for out in (one, three):
            out[(9, *tile(f))] = hid[f, edge]
        faces.append(jnp.where(edge == 0, face[0:1], face[11:12]))
        outers.append(jnp.where(edge == 0, outer[0:1], outer[11:12]))
    corners = jnp.concatenate(faces + outers + [jnp.zeros((8, 256), F32)], axis=0).astype(BF)
    for out in (one, three):
        out[(9, *tile(4))] = corners
        out[(9, *tile(5))] = jnp.zeros((16, 256), BF)
    for n in (4, 5):
        two[(9, *tile(n))] = jnp.zeros((16, 256), BF)
    for a in range(3):
        for b in range(3):
            total = second_part(wide, act, 0, a, b) + got[a * 3 + b]
            for d, out in enumerate((keep, one, two, three)):
                out[a * 3 + b] = total[d * 32 : d * 32 + 32].astype(out.dtype)


def second_x_kernel(got2, got1, got3, own, keep, one, two, three, border, held):
    y, low = lax.axis_index("y"), lax.axis_index("ha") == 0
    for n in range(5):
        first, last = got1[(9, *tile(n))].astype(F32), got3[(9, *tile(n))].astype(F32)
        across, along = jnp.where(low, last, first), jnp.where(low, first, last)
        if n < 4:
            border[n] = across.astype(BF)
            border[4 + n] = got2[(9, *tile(n))]
        else:
            border[8], border[9] = across.astype(BF), along.astype(BF)

    def tap(t):
        ab, lanes = t // 3, slice(t % 3 * 256, t % 3 * 256 + 256)
        total = own[ab, :, lanes]
        for got in (got1, got2, got3):
            total = total + got[ab, :, lanes].astype(F32)
        return total

    for g in range(7):
        parts = [tap(t) if t < 27 else jnp.zeros((32, 256), F32) for t in range(4 * g, 4 * g + 4)]
        held[...] = jnp.concatenate(parts, axis=0).T.reshape(8, 4, 8, 128)
        for d, out in enumerate((keep, one, two, three)):
            out[g] = held[:, (y + d) & 3].reshape(64, 128).astype(out.dtype)


def first_grad_kernel(
    hid, inp, row, left, right, corner_left, corner_right, after, own, pair, wide, side,
):
    del after
    order = channel_order()
    for n, ref in enumerate((row, left, right, corner_left, corner_right)):
        cells = jnp.dot(ref[1].reshape(64, 256), order, preferred_element_type=F32)
        side[n] = cells.reshape(4, 16, 256)

    def put(f, r, which, cells):
        at = which * 128
        wide[f, r, :, at : at + 128] = cells[:, 0:128]
        wide[f, r, :, at + 384 : at + 512] = cells[:, 128:256]

    build_shifted(put, lambda f, r: inp[f, r], *[lambda f, n=n: side[n, f] for n in range(5)])
    for a in range(3):
        rows = (a + 2) * 192
        left = hid[2 - a : 4].reshape(rows, 256)
        for b in range(3):
            window = wide[0 : a + 2, b : b + 12].reshape(rows, 768)
            grad = lax.dot_general(left, window, TN, preferred_element_type=F32)
            grad = grad.reshape(8, 4, 8, 768)
            for q in range(4):
                piece = grad[:, q].reshape(64, 768)
                for e in range(3):
                    t = (a * 3 + b) * 3 + e
                    own[q, t] = piece[:, e * 128 : e * 128 + 128]
                    pair[q, t] = piece[:, e * 128 + 384 : e * 128 + 512]


def first_sum_kernel(own, pair, after, keep, one, two, three):
    del after
    y = lax.axis_index("y")
    for d, out in enumerate((keep, one, two, three)):
        q = (y + d) & 3
        out[...] = (own[q] + pair[q]).astype(out.dtype)


def first_y_kernel(got1, got2, got3, own, after, keep, one, two, three):
    del after

    def tap(t):
        total = own[t]
        for got in (got1, got2, got3):
            total = total + got[t].astype(F32)
        return total

    for g in range(7):
        taps = [tap(t) if t < 27 else jnp.zeros((64, 128), F32) for t in range(4 * g, 4 * g + 4)]
        for d, out in enumerate((keep, one, two, three)):
            piece = jnp.concatenate([v[:, d * 32 : d * 32 + 32] for v in taps], axis=1)
            out[g] = piece.astype(out.dtype)


def last_kernel(own_two, a1, a2, a3, own_one, b1, b2, b3, out, keep, held):
    for n, (own, got) in enumerate(((own_two, (a1, a2, a3)), (own_one, (b1, b2, b3)))):
        total = own[...]
        for ref in got:
            total = total + ref[...].astype(F32)
        held[n] = total.reshape(7, 8, 8, 128)

    def plane(z):
        return jnp.concatenate([held[n, :, z].reshape(56, 128) for n in range(2)], axis=0)

    for q in range(8):
        out[q] = plane(q).astype(BF)
    keep[...] = plane(lax.axis_index("z"))


def final_kernel(factor, got, own, after, one, two):
    del after
    z = lax.axis_index("z")
    total = own[...]
    for d in range(1, 8):
        total = total + got[(z + d) & 7].astype(F32)
    total = (total * factor).reshape(2, 7, 8, 128)
    for out, which in ((two, 0), (one, 1)):
        for t in range(27):
            out[t] = total[which, t // 4, :, t % 4 * 32 : t % 4 * 32 + 32]


def shards(activations, saved_hidden, cotangent, conv_one, conv_two, film_table, timesteps):
    inputs, hidden, block = activations[0], saved_hidden[0], cotangent[0]
    taps_one = conv_one.transpose(1, 2, 3, 0, 4).reshape(27, 256, 256)
    taps_two = conv_two.transpose(1, 2, 3, 0, 4).reshape(27, 256, 256)
    wide = near((4, 14, 16, 768), BF)
    quads = [near((7, 64, 128), F32)] + [near((7, 64, 128), BF)] * 3

    def ring(parts, axis):
        return [send(parts[d - 1], ring_pairs(**{axis: d})) for d in (2, 1, 3)]

    packed = call(
        pack_kernel,
        "pack_first",
        (block, inputs),
        "pp",
        [near((2, 4, 16, 256), BF)] * 5,
        [pltpu.VMEM((2, 768, 128), F32)],
    )
    ways = ((1, 0), (0, 1), (0, -1), (1, 1), (1, -1))
    sides = [send(p, block_pairs(*way)) for p, way in zip(packed, ways)]
    act, inp, slope, held_two = call(
        film_kernel,
        "film",
        (timesteps, inputs, hidden, film_table, taps_two),
        "shhhh",
        [
            near((768, 256), BF),
            near((4, 12, 16, 256), BF),
            near((768, 256), F32),
            near((27, 256, 256), BF),
        ],
        [
            pltpu.VMEM((8, 512), F32),
            pltpu.VMEM((2, 4, 12, 16, 256), BF),
            pltpu.SemaphoreType.DMA,
            pltpu.SemaphoreType.DMA((2,)),
            pltpu.SemaphoreType.DMA((3,)),
        ],
    )
    wide_cot, grad_hidden = call(
        first_kernel,
        "conv_two_back",
        (block, slope, *sides, held_two),
        "pv" + "v" * 5 + "v",
        [wide, near((4, 12, 16, 256), BF)],
        [pltpu.VMEM((768, 256), F32)],
    )

    (pair_two,) = call(
        second_pair_kernel,
        "grad_two_pair",
        (wide_cot, act, grad_hidden),
        "vvv",
        [near((10, 128, 768), F32)],
        [pltpu.VMEM((2, 768, 128), F32)],
    )
    got_pair_two = send(pair_two, core_pairs())
    split = near((4, 27, 64, 128), F32)
    own_one, pair_one = call(
        first_grad_kernel,
        "grad_one",
        (grad_hidden, inp, *sides, pair_two),
        "vv" + "v" * 5 + "v",
        [split, split],
        [pltpu.VMEM((4, 14, 16, 768), BF), pltpu.VMEM((5, 4, 16, 256), F32)],
    )
    got_pair_one = send(pair_one, core_pairs())
    own_two, *parts, face = call(
        second_own_kernel,
        "grad_two_own",
        (wide_cot, act, grad_hidden, got_pair_two, pair_one),
        "vvvvv",
        [near((9, 32, 768), F32)] + [near((10, 32, 768), BF)] * 3 + [near((4, 16, 256), BF)],
    )
    got_two = ring(parts, "dx")
    own_one, *parts_one = call(
        first_sum_kernel,
        "grad_one_sum",
        (own_one, got_pair_one, parts[0]),
        "vvv",
        [near((27, 64, 128), F32)] + [near((27, 64, 128), BF)] * 3,
    )
    got_one = ring(parts_one, "dy")

    own_two, *parts, border = call(
        second_x_kernel,
        "grad_two_x",
        (*got_two, own_two),
        "vvvv",
        quads + [near((10, 16, 256), BF)],
        [pltpu.VMEM((8, 4, 8, 128), F32)],
    )
    got_two = ring(parts, "dy")
    own_one, *parts_one = call(
        first_y_kernel, "grad_one_y", (*got_one, own_one, parts[0]), "vvvvv", quads
    )
    got_one = ring(parts_one, "dx")

    out, own = call(
        last_kernel,
        "last_stage",
        (own_two, *got_two, own_one, *got_one),
        "v" * 8,
        [far((8, 112, 128), BF), near((112, 128), F32)],
        [pltpu.VMEM((2, 7, 8, 8, 128), F32)],
    )
    planes = lax.all_to_all(out, "z", 0, 0, tiled=True)

    (grad_input,) = call(
        input_conv_kernel,
        "conv_one_back",
        (grad_hidden, block, border, face, own, taps_one),
        "vpvvvh",
        [(jax.ShapeDtypeStruct((4, 12, 16, 256), BF), "v")],
        [
            pltpu.VMEM((27, 256, 256), BF),
            pltpu.VMEM((768, 256), F32),
            pltpu.SemaphoreType.DMA((3,)),
            pltpu.VMEM((4, 14, 16, 768), BF),
        ],
    )

    factor = float(256 * 768) ** (-0.5)
    result = jax.ShapeDtypeStruct((27, 8, 32), F32), "v"
    grad_one, grad_two = call(
        functools.partial(final_kernel, factor), "final_sum", (planes, own, grad_input), "vvh", [result, result]
    )
    shape = lambda g: g.transpose(2, 0, 1).reshape(32, 3, 3, 3, 8)
    return grad_input[None], shape(grad_one), shape(grad_two)


def solution(mesh):
    fine = Mesh(mesh.devices.reshape(SIZES), AX)
    clip = ("z", "y")
    placed = P(clip, None, "ha", ("xh", "core"), None)
    weight = P(("ha", "xh", "core"), None, None, None, clip)
    return jax.shard_map(
        shards,
        mesh=fine,
        in_specs=(placed, placed, placed, P(), P(), P(), P(clip)),
        out_specs=(placed, weight, weight),
        check_vma=False,
    )
```

```python
import functools

import jax
import jax.numpy as jnp
from jax import lax
from jax.experimental import pallas as pl
from jax.experimental.pallas import tpu as pltpu
from jax.sharding import Mesh
from jax.sharding import PartitionSpec as P

BF = jnp.bfloat16
F32 = jnp.float32
AX = ("z", "y", "ha", "xh", "core")
SIZES = (8, 4, 2, 2, 2)
VM = pl.BlockSpec(memory_space=pltpu.VMEM)
HB = pl.BlockSpec(memory_space=pl.ANY)
SM = pl.BlockSpec(memory_space=pltpu.SMEM)
NT = (((1,), (1,)), ((), ()))
TN = (((0,), (0,)), ((), ()))


def core_pairs():
    return [(i, i ^ 1) for i in range(256)]


def block_pairs(dh, dw):
    return [(i, i // 8 * 8 + (i // 4 % 2 ^ dh) * 4 + (i + dw) % 4) for i in range(256)]


def ring_pairs(dx=0, dy=0):
    pairs = []
    for i in range(256):
        core, xh, ha, y, z = i % 2, i // 2 % 2, i // 4 % 2, i // 8 % 4, i // 32
        x, y = (xh * 2 + ha + dx) % 4, (y + dy) % 4
        pairs.append((i, ((z * 4 + y) * 2 + x % 2) * 4 + x // 2 * 2 + core))
    return pairs


def send(value, pairs):
    return lax.ppermute(value, AX, pairs)


def call(kernel, name, args, spaces, outs, scratch=(), limit=16):
    where = {"v": pltpu.VMEM, "p": pltpu.HBM, "h": pltpu.HBM}
    args = [
        pltpu.with_memory_space_constraint(a, where[s]) if s in where else a
        for a, s in zip(args, spaces)
    ]
    specs = {"v": VM, "p": VM, "h": HB, "s": SM}
    return pl.pallas_call(
        kernel,
        out_shape=tuple(o for o, _ in outs),
        in_specs=[specs[s] for s in spaces],
        out_specs=tuple(specs[s] for _, s in outs),
        scratch_shapes=list(scratch),
        compiler_params=pltpu.CompilerParams(vmem_limit_bytes=limit * 2**20),
        name=name,
    )(*args)


def near(shape, dtype):
    return pltpu.VMEM(shape, dtype), "v"


def far(shape, dtype):
    return pltpu.HBM(shape, dtype), "p"


def x_place():
    return lax.axis_index("xh") * 2 + lax.axis_index("ha")


def column(wide, lanes_half, f, j):
    cells = wide[lanes_half, pl.ds(f * 192 + j, 12, stride=16), :]
    return jnp.concatenate([cells, jnp.zeros((4, 128), F32)], axis=0)


def spread(wide, block):
    flat = block[...].reshape(768, 256).astype(F32)
    wide[0] = flat[:, 0:128]
    wide[1] = flat[:, 128:256]


def pack_kernel(one, two, row, hi, lo, corner_hi, corner_lo, wide):
    edge = 11 * (1 - lax.axis_index("ha"))
    for n, block in enumerate((one, two)):
        spread(wide, block)
        for f in range(4):
            row[n, f] = block[f, edge]
            for j, out, corner in ((15, hi, corner_hi), (0, lo, corner_lo)):
                for h in range(2):
                    lanes = slice(h * 128, h * 128 + 128)
                    out[n, f, :, lanes] = column(wide, h, f, j).astype(BF)
                    cell = wide[h, pl.ds(f * 192 + edge * 16 + j, 1), :]
                    corner[n, f, :, lanes] = jnp.broadcast_to(cell, (16, 128)).astype(BF)


def pad_block(put, block, row, left, right, corner_left, corner_right):
    ha, wa = lax.axis_index("ha"), lax.axis_index("xh") * 2 + lax.axis_index("core")
    is_top, is_low = (ha == 1).astype(F32), (ha == 0).astype(F32)
    rest = jnp.zeros((2, 256), F32)
    for f in range(4):
        edge = row(f).astype(F32)
        put(f, 0, edge * is_top)
        put(f, 13, edge * is_low)
        for r in range(12):
            put(f, r + 1, block(f, r))
        for n, side, corner, has in (
            (14, left, corner_left, (wa > 0).astype(F32)),
            (15, right, corner_right, (wa < 3).astype(F32)),
        ):
            cells, end = side(f).astype(F32)[0:12], corner(f).astype(F32)[0:1]
            cells = jnp.concatenate([end * is_top, cells, end * is_low, rest], axis=0)
            put(f, n, cells * has)


def build_shifted(put, padded):
    col = lax.broadcasted_iota(jnp.int32, (16, 256), 0)
    for f in range(4):
        lefts, rights = padded[f, 14].astype(F32), padded[f, 15].astype(F32)
        for r in range(14):
            cells, lo, hi = padded[f, r].astype(F32), lefts[r : r + 1], rights[r : r + 1]
            put(f, r, 1, padded[f, r])
            put(f, r, 0, jnp.where(col == 0, lo, pltpu.roll(cells, 1, 0)).astype(BF))
            put(f, r, 2, jnp.where(col == 15, hi, pltpu.roll(cells, 15, 0)).astype(BF))


def keep_in(padded):
    def put(f, n, cells):
        padded[f, n] = cells.astype(BF)

    return put


def put_back(wide):
    def put(f, r, which, cells):
        wide[f, r, :, (2 - which) * 256 : (3 - which) * 256] = cells

    return put


def weight_copies(weight, held, sem):
    return [
        pltpu.make_async_copy(weight.at[pl.ds(a * 9, 9)], held.at[pl.ds(a * 9, 9)], sem.at[a])
        for a in range(3)
    ]


def conv_sum(wide, held, total):
    for a in (2, 1, 0):
        frames = a + 2
        for b in range(3):
            window = wide[2 - a : 4, 2 - b : 14 - b].reshape(frames * 192, 768)
            part = None
            for e in range(3):
                one = lax.dot_general(
                    window[:, e * 256 : (e + 1) * 256],
                    held[(a * 3 + b) * 3 + e],
                    NT,
                    preferred_element_type=F32,
                )
                part = one if part is None else part + one
            if a == 2 and b == 0:
                total[...] = part
            else:
                total[0 : frames * 192] += part


def channel_order():
    lane = lax.broadcasted_iota(jnp.int32, (256, 256), 1)
    goal, kept = (x_place() + (lane >> 5)) & 3, lax.axis_index("core") ^ (lane >> 7)
    source = ((goal & 1) << 7) + ((goal >> 1) << 6) + (kept << 5) + (lane & 31)
    return (lax.broadcasted_iota(jnp.int32, (256, 256), 0) == source).astype(BF)


def film_kernel(
    step, inputs, hidden, table, weight, act_out, inp_out, slope, taps,
    film, blocks, sem, block_sem, tap_sem,
):
    start = step[0]
    whole = pl.multiple_of(start // 8 * 8, 8)
    film_copy = pltpu.make_async_copy(table.at[pl.ds(whole, 8)], film, sem)
    film_copy.start()
    block_copies = [
        pltpu.make_async_copy(ref, blocks.at[n], block_sem.at[n])
        for n, ref in enumerate((inputs, hidden))
    ]
    for copy in block_copies:
        copy.start()
    copies = weight_copies(weight, taps, tap_sem)
    for copy in copies:
        copy.start()
    order = channel_order()
    sort = lambda v: jnp.dot(v, order, preferred_element_type=F32).astype(BF)
    for copy in block_copies:
        copy.wait()
    film_copy.wait()
    inp_out[...] = sort(blocks[0].reshape(768, 256)).reshape(4, 12, 16, 256)
    line = film[pl.ds(start - whole, 1), :]
    scale, shift = 1.0 + line[:, 0:256], line[:, 256:512]
    shifted = blocks[1].reshape(768, 256).astype(F32) * scale + shift
    sigma = jax.nn.sigmoid(shifted)
    act_out[...] = sort((shifted * sigma).astype(BF))
    slope[...] = scale * sigma * (1.0 + shifted * (1.0 - sigma))
    for copy in copies:
        copy.wait()


def pad_kernel(block, row, left, right, corner_left, corner_right, act, out):
    sides = (row, left, right, corner_left, corner_right)
    pad_block(keep_in(out), lambda f, r: block[f, r], *[lambda f, s=s: s[0, f] for s in sides])
    for f in range(4):
        for n in range(12):
            cells = act[f * 192 + n * 16 : f * 192 + n * 16 + 16, 128:256]
            out[f, 16 + n % 6, :, n // 6 * 128 : n // 6 * 128 + 128] = cells


def first_kernel(padded, slope, taps, wide, hid_out, total):
    build_shifted(put_back(wide), padded)
    conv_sum(wide, taps, total)
    hid_out[...] = (total[...] * slope[...]).astype(BF).reshape(4, 12, 16, 256)


def input_conv_kernel(
    hid, block, border, cols, after, weight, out, held, total, sem, wide, padded
):
    del after
    copies = weight_copies(weight, held, sem)
    for copy in copies:
        copy.start()
    is_one = lax.axis_index("core") == 1

    def pick(when_one, when_zero):
        return jnp.where(is_one, when_one.astype(F32), when_zero.astype(F32))

    faces, outers = border[8].astype(F32), border[9].astype(F32)[4:8]
    pad_block(
        keep_in(padded),
        lambda f, r: hid[f, r],
        lambda f: border[f],
        lambda f: pick(cols[0, f], border[4 + f]),
        lambda f: pick(border[4 + f], cols[1, f]),
        lambda f: pick(faces[f : f + 1], outers[f : f + 1]),
        lambda f: pick(outers[f : f + 1], faces[f : f + 1]),
    )
    build_shifted(put_back(wide), padded)
    for copy in copies:
        copy.wait()
    conv_sum(wide, held, total)
    grad = block[...].reshape(768, 256).astype(F32) + total[...]
    out[...] = grad.astype(BF).reshape(4, 12, 16, 256)


def second_own_kernel(wide, act, got, after, keep, one, two, three, pair_wide, pair_act):
    del after
    build_shifted(put_back(pair_wide), got)
    for f in range(4):
        for n in range(12):
            cells = got[f, 16 + n % 6, :, n // 6 * 128 : n // 6 * 128 + 128]
            pair_act[f * 192 + n * 16 : f * 192 + n * 16 + 16, :] = cells
    for a in range(3):
        rows = (a + 2) * 192
        for b in range(3):
            total = None
            for left, right in ((act[0:rows, 0:128], wide), (pair_act[0:rows], pair_wide)):
                window = right[2 - a : 4, 2 - b : 14 - b].reshape(rows, 768)
                part = lax.dot_general(left, window, TN, preferred_element_type=F32)
                total = part if total is None else total + part
            for d, out in enumerate((keep, one, two, three)):
                out[a * 3 + b] = total[d * 32 : d * 32 + 32].astype(out.dtype)


def second_x_kernel(got1, got2, got3, own, keep, one, two, three, held):
    y = lax.axis_index("y")

    def tap(t):
        ab, lanes = t // 3, slice(t % 3 * 256, t % 3 * 256 + 256)
        total = own[ab, :, lanes]
        for got in (got1, got2, got3):
            total = total + got[ab, :, lanes].astype(F32)
        return total

    for g in range(7):
        parts = [tap(t) if t < 27 else jnp.zeros((32, 256), F32) for t in range(4 * g, 4 * g + 4)]
        held[...] = jnp.concatenate(parts, axis=0).T.reshape(8, 4, 8, 128)
        for d, out in enumerate((keep, one, two, three)):
            out[g] = held[:, (y + d) & 3].reshape(64, 128).astype(out.dtype)


def border_at(base, n, h):
    slot = n * 2 + h
    return base + slot // 4, slice(slot % 4 * 16, slot % 4 * 16 + 16)


def first_grad_kernel(
    hid, inp, row, left, right, corner_left, corner_right, after,
    own, pair, wide, padded, side, flat,
):
    del after
    order = channel_order()
    for n, ref in enumerate((row, left, right, corner_left, corner_right)):
        cells = jnp.dot(ref[1].reshape(64, 256), order, preferred_element_type=F32)
        side[n] = cells.reshape(4, 16, 256)

    def put(f, r, which, cells):
        at = which * 128
        wide[f, r, :, at : at + 128] = cells[:, 0:128]
        wide[f, r, :, at + 384 : at + 512] = cells[:, 128:256]

    pad_block(
        keep_in(padded), lambda f, r: inp[f, r], *[lambda f, n=n: side[n, f] for n in range(5)]
    )
    build_shifted(put, padded)
    spread(flat, hid)
    for f in range(4):
        for n, j in ((f, 15), (4 + f, 0)):
            for h in range(2):
                q, rows = border_at(0, n, h)
                pair[q, 27, rows] = column(flat, h, f, j)
    for a in range(3):
        rows = (a + 2) * 192
        left = hid[2 - a : 4].reshape(rows, 256)
        for b in range(3):
            window = wide[0 : a + 2, b : b + 12].reshape(rows, 768)
            grad = lax.dot_general(left, window, TN, preferred_element_type=F32)
            grad = grad.reshape(8, 4, 8, 768)
            for q in range(4):
                piece = grad[:, q].reshape(64, 768)
                for e in range(3):
                    t = (a * 3 + b) * 3 + e
                    own[q, t] = piece[:, e * 128 : e * 128 + 128]
                    pair[q, t] = piece[:, e * 128 + 384 : e * 128 + 512]


def first_sum_kernel(own, pair, after, keep, one, two, three, cols):
    del after
    y = lax.axis_index("y")
    for d, out in enumerate((keep, one, two, three)):
        q = (y + d) & 3
        out[...] = (own[q] + pair[q, 0:27]).astype(out.dtype)
    for n in range(8):
        for h in range(2):
            q, rows = border_at(0, n, h)
            cols[n // 4, n % 4, :, h * 128 : h * 128 + 128] = pair[q, 27, rows].astype(BF)


def first_y_kernel(got1, got2, got3, own, hid, cols, after, keep, one, two, three):
    del after

    def tap(t):
        total = own[t]
        for got in (got1, got2, got3):
            total = total + got[t].astype(F32)
        return total

    for g in range(7):
        taps = [tap(t) if t < 27 else jnp.zeros((64, 128), F32) for t in range(4 * g, 4 * g + 4)]
        for d, out in enumerate((keep, one, two, three)):
            piece = jnp.concatenate([v[:, d * 32 : d * 32 + 32] for v in taps], axis=1)
            out[g] = piece.astype(out.dtype)

    is_one = lax.axis_index("core") == 1
    edge = 11 * (1 - lax.axis_index("ha"))
    along, across, faces, outers = [], [], [], []
    for f in range(4):
        hi, lo = cols[0, f].astype(F32), cols[1, f].astype(F32)
        face, outer = jnp.where(is_one, hi, lo), jnp.where(is_one, lo, hi)
        along.append(hid[f, edge])
        across.append(outer.astype(BF))
        faces.append(jnp.where(edge == 0, face[0:1], face[11:12]))
        outers.append(jnp.where(edge == 0, outer[0:1], outer[11:12]))
    corners = jnp.concatenate(faces + outers + [jnp.zeros((8, 256), F32)], axis=0).astype(BF)
    rest = [jnp.zeros((16, 256), BF)] * 2
    along, across = along + [corners, rest[0]], across + rest
    for out, tiles in ((one, along), (two, across), (three, along)):
        for n, cells in enumerate(tiles):
            for h in range(2):
                out[border_at(7, n, h)] = cells[:, h * 128 : h * 128 + 128]


def last_kernel(own_two, a2, a1, a3, own_one, b2, b1, b3, out, keep, border, held):
    low = lax.axis_index("ha") == 0
    for h in range(2):
        lanes = slice(h * 128, h * 128 + 128)
        for n in range(5):
            first, last = b1[border_at(7, n, h)].astype(F32), b3[border_at(7, n, h)].astype(F32)
            across, along = jnp.where(low, last, first), jnp.where(low, first, last)
            if n < 4:
                border[n, :, lanes] = across.astype(BF)
                border[4 + n, :, lanes] = b2[border_at(7, n, h)]
            else:
                border[8, :, lanes], border[9, :, lanes] = across.astype(BF), along.astype(BF)
    for n, (own, got) in enumerate(((own_two, (a1, a2, a3)), (own_one, (b1, b2, b3)))):
        total = own[...]
        for ref in got:
            total = total + ref[0:7].astype(F32)
        held[n] = total.reshape(7, 8, 8, 128)

    def plane(z):
        return jnp.concatenate([held[n, :, z].reshape(56, 128) for n in range(2)], axis=0)

    for q in range(8):
        out[q] = plane(q).astype(BF)
    keep[...] = plane(lax.axis_index("z"))


def final_kernel(factor, got, own, after, one, two):
    del after
    z = lax.axis_index("z")
    total = own[...]
    for d in range(1, 8):
        total = total + got[(z + d) & 7].astype(F32)
    total = (total * factor).reshape(2, 7, 8, 128)
    for out, which in ((two, 0), (one, 1)):
        for t in range(27):
            out[t] = total[which, t // 4, :, t % 4 * 32 : t % 4 * 32 + 32]


def shards(activations, saved_hidden, cotangent, conv_one, conv_two, film_table, timesteps):
    inputs, hidden, block = activations[0], saved_hidden[0], cotangent[0]
    taps_one = conv_one.transpose(1, 2, 3, 0, 4).reshape(27, 256, 256)
    taps_two = conv_two.transpose(1, 2, 3, 0, 4).reshape(27, 256, 256)
    wide = near((4, 14, 16, 768), BF)
    quads = [near((7, 64, 128), F32)] + [near((7, 64, 128), BF)] * 3

    def ring(parts, axis):
        return [send(parts[d - 1], ring_pairs(**{axis: d})) for d in (2, 1, 3)]

    packed = call(
        pack_kernel,
        "pack_first",
        (block, inputs),
        "pp",
        [near((2, 4, 16, 256), BF)] * 5,
        [pltpu.VMEM((2, 768, 128), F32)],
    )
    ways = ((1, 0), (0, 1), (0, -1), (1, 1), (1, -1))
    sides = [send(p, block_pairs(*way)) for p, way in zip(packed, ways)]
    act, inp, slope, held_two = call(
        film_kernel,
        "film",
        (timesteps, inputs, hidden, film_table, taps_two),
        "shhhh",
        [
            near((768, 256), BF),
            near((4, 12, 16, 256), BF),
            near((768, 256), F32),
            near((27, 256, 256), BF),
        ],
        [
            pltpu.VMEM((8, 512), F32),
            pltpu.VMEM((2, 4, 12, 16, 256), BF),
            pltpu.SemaphoreType.DMA,
            pltpu.SemaphoreType.DMA((2,)),
            pltpu.SemaphoreType.DMA((3,)),
        ],
    )
    (padded,) = call(
        pad_kernel,
        "pad_cotangent",
        (block, *sides, act),
        "pvvvvvv",
        [near((4, 22, 16, 256), BF)],
    )
    pair_padded = send(padded, core_pairs())
    wide_cot, grad_hidden = call(
        first_kernel,
        "conv_two_back",
        (padded, slope, held_two),
        "vvv",
        [wide, near((4, 12, 16, 256), BF)],
        [pltpu.VMEM((768, 256), F32)],
    )

    own_one, pair_one = call(
        first_grad_kernel,
        "grad_one",
        (grad_hidden, inp, *sides, pair_padded),
        "vv" + "v" * 6,
        [near((4, 27, 64, 128), F32), near((4, 28, 64, 128), F32)],
        [
            pltpu.VMEM((4, 14, 16, 768), BF),
            pltpu.VMEM((4, 16, 16, 256), BF),
            pltpu.VMEM((5, 4, 16, 256), F32),
            pltpu.VMEM((2, 768, 128), F32),
        ],
    )
    got_pair_one = send(pair_one, core_pairs())
    own_two, *parts = call(
        second_own_kernel,
        "grad_two",
        (wide_cot, act, pair_padded, pair_one),
        "vvvv",
        [near((9, 32, 768), F32)] + [near((9, 32, 768), BF)] * 3,
        [pltpu.VMEM((4, 14, 16, 768), BF), pltpu.VMEM((768, 128), BF)],
    )
    got_two = ring(parts, "dx")
    own_one, *parts_one, cols = call(
        first_sum_kernel,
        "grad_one_sum",
        (own_one, got_pair_one, parts[0]),
        "vvv",
        [near((27, 64, 128), F32)]
        + [near((27, 64, 128), BF)] * 3
        + [near((2, 4, 16, 256), BF)],
    )
    got_one = ring(parts_one, "dy")

    own_two, *parts = call(
        second_x_kernel,
        "grad_two_x",
        (*got_two, own_two),
        "vvvv",
        quads,
        [pltpu.VMEM((8, 4, 8, 128), F32)],
    )
    got_two = ring(parts, "dy")
    own_one, *parts_one = call(
        first_y_kernel,
        "grad_one_y",
        (*got_one, own_one, grad_hidden, cols, parts[0]),
        "v" * 7,
        [near((7, 64, 128), F32)] + [near((10, 64, 128), BF)] * 3,
    )
    got_one = ring(parts_one, "dx")

    out, own, border = call(
        last_kernel,
        "last_stage",
        (own_two, *got_two, own_one, *got_one),
        "v" * 8,
        [far((8, 112, 128), BF), near((112, 128), F32), near((10, 16, 256), BF)],
        [pltpu.VMEM((2, 7, 8, 8, 128), F32)],
    )
    planes = lax.all_to_all(out, "z", 0, 0, tiled=True)

    (grad_input,) = call(
        input_conv_kernel,
        "conv_one_back",
        (grad_hidden, block, border, cols, own, taps_one),
        "vpvvvh",
        [(jax.ShapeDtypeStruct((4, 12, 16, 256), BF), "v")],
        [
            pltpu.VMEM((27, 256, 256), BF),
            pltpu.VMEM((768, 256), F32),
            pltpu.SemaphoreType.DMA((3,)),
            pltpu.VMEM((4, 14, 16, 768), BF),
            pltpu.VMEM((4, 16, 16, 256), BF),
        ],
    )

    factor = float(256 * 768) ** (-0.5)
    result = jax.ShapeDtypeStruct((27, 8, 32), F32), "v"
    grad_one, grad_two = call(
        functools.partial(final_kernel, factor), "final_sum", (planes, own, grad_input), "vvh", [result, result]
    )
    shape = lambda g: g.transpose(2, 0, 1).reshape(32, 3, 3, 3, 8)
    return grad_input[None], shape(grad_one), shape(grad_two)


def solution(mesh):
    fine = Mesh(mesh.devices.reshape(SIZES), AX)
    clip = ("z", "y")
    placed = P(clip, None, "ha", ("xh", "core"), None)
    weight = P(("ha", "xh", "core"), None, None, None, clip)
    return jax.shard_map(
        shards,
        mesh=fine,
        in_specs=(placed, placed, placed, P(), P(), P(), P(clip)),
        out_specs=(placed, weight, weight),
        check_vma=False,
    )
```

```python
import functools

import jax
import jax.numpy as jnp
from jax import lax
from jax.experimental import pallas as pl
from jax.experimental.pallas import tpu as pltpu
from jax.sharding import Mesh
from jax.sharding import PartitionSpec as P

BF = jnp.bfloat16
F32 = jnp.float32
AX = ("z", "y", "ha", "xh", "core")
SIZES = (8, 4, 2, 2, 2)
VM = pl.BlockSpec(memory_space=pltpu.VMEM)
HB = pl.BlockSpec(memory_space=pl.ANY)
SM = pl.BlockSpec(memory_space=pltpu.SMEM)
NT = (((1,), (1,)), ((), ()))
TN = (((0,), (0,)), ((), ()))


def core_pairs():
    return [(i, i ^ 1) for i in range(256)]


def block_pairs(dh, dw):
    return [(i, i // 8 * 8 + (i // 4 % 2 ^ dh) * 4 + (i + dw) % 4) for i in range(256)]


def ring_pairs(dx=0, dy=0):
    pairs = []
    for i in range(256):
        core, xh, ha, y, z = i % 2, i // 2 % 2, i // 4 % 2, i // 8 % 4, i // 32
        x, y = (xh * 2 + ha + dx) % 4, (y + dy) % 4
        pairs.append((i, ((z * 4 + y) * 2 + x % 2) * 4 + x // 2 * 2 + core))
    return pairs


def send(value, pairs):
    return lax.ppermute(value, AX, pairs)


def call(kernel, name, args, spaces, outs, scratch=(), limit=16):
    where = {"v": pltpu.VMEM, "p": pltpu.HBM, "h": pltpu.HBM}
    args = [
        pltpu.with_memory_space_constraint(a, where[s]) if s in where else a
        for a, s in zip(args, spaces)
    ]
    specs = {"v": VM, "p": VM, "h": HB, "s": SM}
    return pl.pallas_call(
        kernel,
        out_shape=tuple(o for o, _ in outs),
        in_specs=[specs[s] for s in spaces],
        out_specs=tuple(specs[s] for _, s in outs),
        scratch_shapes=list(scratch),
        compiler_params=pltpu.CompilerParams(vmem_limit_bytes=limit * 2**20),
        name=name,
    )(*args)


def near(shape, dtype):
    return pltpu.VMEM(shape, dtype), "v"


def far(shape, dtype):
    return pltpu.HBM(shape, dtype), "p"


def x_place():
    return lax.axis_index("xh") * 2 + lax.axis_index("ha")


def column(wide, lanes_half, f, j):
    cells = wide[lanes_half, pl.ds(f * 192 + j, 12, stride=16), :]
    return jnp.concatenate([cells, jnp.zeros((4, 128), F32)], axis=0)


def spread(wide, block):
    flat = block[...].reshape(768, 256).astype(F32)
    wide[0] = flat[:, 0:128]
    wide[1] = flat[:, 128:256]


def pack_columns_kernel(one, two, hi, lo, wide):
    for n, block in enumerate((one, two)):
        spread(wide, block)
        for f in range(4):
            for j, out in ((15, hi), (0, lo)):
                for h in range(2):
                    out[n, f, :, h * 128 : h * 128 + 128] = column(wide, h, f, j).astype(BF)


def pack_rows_kernel(one, two, left, right, after, row):
    del after
    edge = 11 * (1 - lax.axis_index("ha"))
    for n, block in enumerate((one, two)):
        for f in range(4):
            row[n, f] = block[f, edge]
        for at, side in ((0, left), (4, right)):
            cells = [side[n, f].astype(F32) for f in range(4)]
            cells = [jnp.where(edge == 0, c[0:1], c[11:12]) for c in cells]
            cells = jnp.concatenate(cells + [jnp.zeros((4, 256), F32)], axis=0)
            row[n, 4 + at // 4] = jnp.concatenate([cells, cells], axis=0).astype(BF)


def pad_block(put, block, row, left, right, corner_left, corner_right):
    ha, wa = lax.axis_index("ha"), lax.axis_index("xh") * 2 + lax.axis_index("core")
    is_top, is_low = (ha == 1).astype(F32), (ha == 0).astype(F32)
    rest = jnp.zeros((2, 256), F32)
    for f in range(4):
        edge = row(f).astype(F32)
        put(f, 0, edge * is_top)
        put(f, 13, edge * is_low)
        for r in range(12):
            put(f, r + 1, block(f, r))
        for n, side, corner, has in (
            (14, left, corner_left, (wa > 0).astype(F32)),
            (15, right, corner_right, (wa < 3).astype(F32)),
        ):
            cells, end = side(f).astype(F32)[0:12], corner(f).astype(F32)[0:1]
            cells = jnp.concatenate([end * is_top, cells, end * is_low, rest], axis=0)
            put(f, n, cells * has)


def build_shifted(put, padded):
    col = lax.broadcasted_iota(jnp.int32, (16, 256), 0)
    for f in range(4):
        lefts, rights = padded[f, 14].astype(F32), padded[f, 15].astype(F32)
        for r in range(14):
            cells, lo, hi = padded[f, r].astype(F32), lefts[r : r + 1], rights[r : r + 1]
            put(f, r, 1, padded[f, r])
            put(f, r, 0, jnp.where(col == 0, lo, pltpu.roll(cells, 1, 0)).astype(BF))
            put(f, r, 2, jnp.where(col == 15, hi, pltpu.roll(cells, 15, 0)).astype(BF))


def keep_in(padded):
    def put(f, n, cells):
        padded[f, n] = cells.astype(BF)

    return put


def put_back(wide):
    def put(f, r, which, cells):
        wide[f, r, :, (2 - which) * 256 : (3 - which) * 256] = cells

    return put


def weight_copies(weight, held, sem):
    return [
        pltpu.make_async_copy(weight.at[pl.ds(a * 9, 9)], held.at[pl.ds(a * 9, 9)], sem.at[a])
        for a in range(3)
    ]


def conv_sum(wide, held, total):
    for a in (2, 1, 0):
        frames = a + 2
        for b in range(3):
            window = wide[2 - a : 4, 2 - b : 14 - b].reshape(frames * 192, 768)
            part = None
            for e in range(3):
                one = lax.dot_general(
                    window[:, e * 256 : (e + 1) * 256],
                    held[(a * 3 + b) * 3 + e],
                    NT,
                    preferred_element_type=F32,
                )
                part = one if part is None else part + one
            if a == 2 and b == 0:
                total[...] = part
            else:
                total[0 : frames * 192] += part


def channel_order():
    lane = lax.broadcasted_iota(jnp.int32, (256, 256), 1)
    goal, kept = (x_place() + (lane >> 5)) & 3, lax.axis_index("core") ^ (lane >> 7)
    source = ((goal & 1) << 7) + ((goal >> 1) << 6) + (kept << 5) + (lane & 31)
    return (lax.broadcasted_iota(jnp.int32, (256, 256), 0) == source).astype(BF)


def sort_kernel(inputs, weight, inp_out, taps, block, sem, tap_sem):
    block_copy = pltpu.make_async_copy(inputs, block, sem)
    block_copy.start()
    copies = weight_copies(weight, taps, tap_sem)
    for copy in copies:
        copy.start()
    order = channel_order()
    block_copy.wait()
    cells = jnp.dot(block[...].reshape(768, 256), order, preferred_element_type=F32)
    inp_out[...] = cells.astype(BF).reshape(4, 12, 16, 256)
    for copy in copies:
        copy.wait()


def film_kernel(step, hidden, table, act_out, slope, film, block, sem, block_sem):
    start = step[0]
    whole = pl.multiple_of(start // 8 * 8, 8)
    film_copy = pltpu.make_async_copy(table.at[pl.ds(whole, 8)], film, sem)
    film_copy.start()
    block_copy = pltpu.make_async_copy(hidden, block, block_sem)
    block_copy.start()
    order = channel_order()
    block_copy.wait()
    film_copy.wait()
    line = film[pl.ds(start - whole, 1), :]
    scale, shift = 1.0 + line[:, 0:256], line[:, 256:512]
    shifted = block[...].reshape(768, 256).astype(F32) * scale + shift
    sigma = jax.nn.sigmoid(shifted)
    activated = (shifted * sigma).astype(BF)
    act_out[...] = jnp.dot(activated, order, preferred_element_type=F32).astype(BF)
    slope[...] = scale * sigma * (1.0 + shifted * (1.0 - sigma))


def pad_kernel(block, row, left, right, act, out):
    pad_block(
        keep_in(out),
        lambda f, r: block[f, r],
        lambda f: row[0, f],
        lambda f: left[0, f],
        lambda f: right[0, f],
        lambda f: row[0, 4].astype(F32)[f : f + 1],
        lambda f: row[0, 5].astype(F32)[f : f + 1],
    )
    for f in range(4):
        for n in range(12):
            cells = act[f * 192 + n * 16 : f * 192 + n * 16 + 16, 128:256]
            out[f, 16 + n % 6, :, n // 6 * 128 : n // 6 * 128 + 128] = cells


def first_kernel(padded, slope, taps, wide, hid_out, total):
    build_shifted(put_back(wide), padded)
    conv_sum(wide, taps, total)
    hid_out[...] = (total[...] * slope[...]).astype(BF).reshape(4, 12, 16, 256)


def input_conv_kernel(
    hid, block, border, cols, after, weight, out, held, total, sem, wide, padded
):
    del after
    copies = weight_copies(weight, held, sem)
    for copy in copies:
        copy.start()
    is_one = lax.axis_index("core") == 1

    def pick(when_one, when_zero):
        return jnp.where(is_one, when_one.astype(F32), when_zero.astype(F32))

    faces, outers = border[8].astype(F32), border[9].astype(F32)[4:8]
    pad_block(
        keep_in(padded),
        lambda f, r: hid[f, r],
        lambda f: border[f],
        lambda f: pick(cols[0, f], border[4 + f]),
        lambda f: pick(border[4 + f], cols[1, f]),
        lambda f: pick(faces[f : f + 1], outers[f : f + 1]),
        lambda f: pick(outers[f : f + 1], faces[f : f + 1]),
    )
    build_shifted(put_back(wide), padded)
    for copy in copies:
        copy.wait()
    conv_sum(wide, held, total)
    grad = block[...].reshape(768, 256).astype(F32) + total[...]
    out[...] = grad.astype(BF).reshape(4, 12, 16, 256)


def second_own_kernel(wide, act, got, after, keep, one, two, three, pair_wide, pair_act):
    del after
    build_shifted(put_back(pair_wide), got)
    for f in range(4):
        for n in range(12):
            cells = got[f, 16 + n % 6, :, n // 6 * 128 : n // 6 * 128 + 128]
            pair_act[f * 192 + n * 16 : f * 192 + n * 16 + 16, :] = cells
    for a in range(3):
        rows = (a + 2) * 192
        for b in range(3):
            total = None
            for left, right in ((act[0:rows, 0:128], wide), (pair_act[0:rows], pair_wide)):
                window = right[2 - a : 4, 2 - b : 14 - b].reshape(rows, 768)
                part = lax.dot_general(left, window, TN, preferred_element_type=F32)
                total = part if total is None else total + part
            for d, out in enumerate((keep, one, two, three)):
                out[a * 3 + b] = total[d * 32 : d * 32 + 32].astype(out.dtype)


def second_x_kernel(got1, got2, got3, own, out, keep, held):
    y = lax.axis_index("y")

    def tap(t):
        ab, lanes = t // 3, slice(t % 3 * 256, t % 3 * 256 + 256)
        total = own[ab, :, lanes]
        for got in (got1, got2, got3):
            total = total + got[ab, :, lanes].astype(F32)
        return total

    for g in range(7):
        parts = [tap(t) if t < 27 else jnp.zeros((32, 256), F32) for t in range(4 * g, 4 * g + 4)]
        held[...] = jnp.concatenate(parts, axis=0).T.reshape(8, 4, 8, 128)
        for q in range(4):
            out[q, g] = held[:, q].reshape(64, 128).astype(BF)
        keep[g] = held[:, y].reshape(64, 128)


def border_at(base, n, h):
    slot = n * 2 + h
    return base + slot // 4, slice(slot % 4 * 16, slot % 4 * 16 + 16)


def first_grad_kernel(
    hid, inp, row, left, right, after, own, pair, wide, padded, side, flat,
):
    del after
    order = channel_order()
    for at, ref, size in ((0, row, 6), (6, left, 4), (10, right, 4)):
        cells = jnp.dot(ref[1].reshape(size * 16, 256), order, preferred_element_type=F32)
        side[at : at + size] = cells.reshape(size, 16, 256)

    def put(f, r, which, cells):
        at = which * 128
        wide[f, r, :, at : at + 128] = cells[:, 0:128]
        wide[f, r, :, at + 384 : at + 512] = cells[:, 128:256]

    pad_block(
        keep_in(padded),
        lambda f, r: inp[f, r],
        lambda f: side[f],
        lambda f: side[6 + f],
        lambda f: side[10 + f],
        lambda f: side[4, f : f + 1],
        lambda f: side[5, f : f + 1],
    )
    build_shifted(put, padded)
    spread(flat, hid)
    for f in range(4):
        for n, j in ((f, 15), (4 + f, 0)):
            for h in range(2):
                q, rows = border_at(0, n, h)
                pair[q, 27, rows] = column(flat, h, f, j)
    for a in range(3):
        rows = (a + 2) * 192
        left = hid[2 - a : 4].reshape(rows, 256)
        for b in range(3):
            window = wide[0 : a + 2, b : b + 12].reshape(rows, 768)
            grad = lax.dot_general(left, window, TN, preferred_element_type=F32)
            grad = grad.reshape(8, 4, 8, 768)
            for q in range(4):
                piece = grad[:, q].reshape(64, 768)
                for e in range(3):
                    t = (a * 3 + b) * 3 + e
                    own[q, t] = piece[:, e * 128 : e * 128 + 128]
                    pair[q, t] = piece[:, e * 128 + 384 : e * 128 + 512]


def first_sum_kernel(own, pair, after, keep, one, two, three, cols):
    del after
    y = lax.axis_index("y")
    for d, out in enumerate((keep, one, two, three)):
        q = (y + d) & 3
        out[...] = (own[q] + pair[q, 0:27]).astype(out.dtype)
    for n in range(8):
        for h in range(2):
            q, rows = border_at(0, n, h)
            cols[n // 4, n % 4, :, h * 128 : h * 128 + 128] = pair[q, 27, rows].astype(BF)


def first_y_kernel(got1, got2, got3, own, hid, cols, after, keep, one, two, three):
    del after

    def tap(t):
        total = own[t]
        for got in (got1, got2, got3):
            total = total + got[t].astype(F32)
        return total

    for g in range(7):
        taps = [tap(t) if t < 27 else jnp.zeros((64, 128), F32) for t in range(4 * g, 4 * g + 4)]
        for d, out in enumerate((keep, one, two, three)):
            piece = jnp.concatenate([v[:, d * 32 : d * 32 + 32] for v in taps], axis=1)
            out[g] = piece.astype(out.dtype)

    is_one = lax.axis_index("core") == 1
    edge = 11 * (1 - lax.axis_index("ha"))
    along, across, faces, outers = [], [], [], []
    for f in range(4):
        hi, lo = cols[0, f].astype(F32), cols[1, f].astype(F32)
        face, outer = jnp.where(is_one, hi, lo), jnp.where(is_one, lo, hi)
        along.append(hid[f, edge])
        across.append(outer.astype(BF))
        faces.append(jnp.where(edge == 0, face[0:1], face[11:12]))
        outers.append(jnp.where(edge == 0, outer[0:1], outer[11:12]))
    corners = jnp.concatenate(faces + outers + [jnp.zeros((8, 256), F32)], axis=0).astype(BF)
    rest = [jnp.zeros((16, 256), BF)] * 2
    along, across = along + [corners, rest[0]], across + rest
    for out, tiles in ((one, along), (two, across), (three, along)):
        for n, cells in enumerate(tiles):
            for h in range(2):
                out[border_at(7, n, h)] = cells[:, h * 128 : h * 128 + 128]


def last_kernel(own_two, got_two, own_one, b2, b1, b3, out, keep, border, held):
    low = lax.axis_index("ha") == 0
    for h in range(2):
        lanes = slice(h * 128, h * 128 + 128)
        for n in range(5):
            first, last = b1[border_at(7, n, h)].astype(F32), b3[border_at(7, n, h)].astype(F32)
            across, along = jnp.where(low, last, first), jnp.where(low, first, last)
            if n < 4:
                border[n, :, lanes] = across.astype(BF)
                border[4 + n, :, lanes] = b2[border_at(7, n, h)]
            else:
                border[8, :, lanes], border[9, :, lanes] = across.astype(BF), along.astype(BF)
    y = lax.axis_index("y")
    parts_two = [got_two[(y + d) & 3] for d in range(1, 4)]
    parts_one = [ref[0:7] for ref in (b1, b2, b3)]
    for n, (own, parts) in enumerate(((own_two, parts_two), (own_one, parts_one))):
        total = own[...]
        for part in parts:
            total = total + part.astype(F32)
        held[n] = total.reshape(7, 8, 8, 128)

    def plane(z):
        return jnp.concatenate([held[n, :, z].reshape(56, 128) for n in range(2)], axis=0)

    for q in range(8):
        out[q] = plane(q).astype(BF)
    keep[...] = plane(lax.axis_index("z"))


def final_kernel(factor, got, own, after, one, two):
    del after
    z = lax.axis_index("z")
    total = own[...]
    for d in range(1, 8):
        total = total + got[(z + d) & 7].astype(F32)
    total = (total * factor).reshape(2, 7, 8, 128)
    for out, which in ((two, 0), (one, 1)):
        for t in range(27):
            out[t] = total[which, t // 4, :, t % 4 * 32 : t % 4 * 32 + 32]


def shards(activations, saved_hidden, cotangent, conv_one, conv_two, film_table, timesteps):
    inputs, hidden, block = activations[0], saved_hidden[0], cotangent[0]
    taps_one = conv_one.transpose(1, 2, 3, 0, 4).reshape(27, 256, 256)
    taps_two = conv_two.transpose(1, 2, 3, 0, 4).reshape(27, 256, 256)
    wide = near((4, 14, 16, 768), BF)
    def ring(parts, axis):
        return [send(parts[d - 1], ring_pairs(**{axis: d})) for d in (2, 1, 3)]

    hi, lo = call(
        pack_columns_kernel,
        "pack_columns",
        (block, inputs),
        "pp",
        [near((2, 4, 16, 256), BF)] * 2,
        [pltpu.VMEM((2, 768, 128), F32)],
    )
    left, right = send(hi, block_pairs(0, 1)), send(lo, block_pairs(0, -1))
    inp, held_two = call(
        sort_kernel,
        "sort_input",
        (inputs, taps_two),
        "hh",
        [near((4, 12, 16, 256), BF), near((27, 256, 256), BF)],
        [
            pltpu.VMEM((4, 12, 16, 256), BF),
            pltpu.SemaphoreType.DMA,
            pltpu.SemaphoreType.DMA((3,)),
        ],
    )
    (row,) = call(
        pack_rows_kernel,
        "pack_rows",
        (block, inputs, left, right, inp),
        "ppvvv",
        [near((2, 6, 16, 256), BF)],
    )
    row = send(row, block_pairs(1, 0))
    act, slope = call(
        film_kernel,
        "film",
        (timesteps, hidden, film_table),
        "shh",
        [near((768, 256), BF), near((768, 256), F32)],
        [
            pltpu.VMEM((8, 512), F32),
            pltpu.VMEM((4, 12, 16, 256), BF),
            pltpu.SemaphoreType.DMA,
            pltpu.SemaphoreType.DMA,
        ],
    )
    (padded,) = call(
        pad_kernel,
        "pad_cotangent",
        (block, row, left, right, act),
        "pvvvv",
        [near((4, 22, 16, 256), BF)],
    )
    pair_padded = send(padded, core_pairs())
    wide_cot, grad_hidden = call(
        first_kernel,
        "conv_two_back",
        (padded, slope, held_two),
        "vvv",
        [wide, near((4, 12, 16, 256), BF)],
        [pltpu.VMEM((768, 256), F32)],
    )

    own_one, pair_one = call(
        first_grad_kernel,
        "grad_one",
        (grad_hidden, inp, row, left, right, pair_padded),
        "v" * 6,
        [near((4, 27, 64, 128), F32), near((4, 28, 64, 128), F32)],
        [
            pltpu.VMEM((4, 14, 16, 768), BF),
            pltpu.VMEM((4, 16, 16, 256), BF),
            pltpu.VMEM((14, 16, 256), F32),
            pltpu.VMEM((2, 768, 128), F32),
        ],
    )
    got_pair_one = send(pair_one, core_pairs())
    own_two, *parts = call(
        second_own_kernel,
        "grad_two",
        (wide_cot, act, pair_padded, pair_one),
        "vvvv",
        [near((9, 32, 768), F32)] + [near((9, 32, 768), BF)] * 3,
        [pltpu.VMEM((4, 14, 16, 768), BF), pltpu.VMEM((768, 128), BF)],
    )
    got_two = ring(parts, "dx")
    own_one, *parts_one, cols = call(
        first_sum_kernel,
        "grad_one_sum",
        (own_one, got_pair_one, parts[0]),
        "vvv",
        [near((27, 64, 128), F32)]
        + [near((27, 64, 128), BF)] * 3
        + [near((2, 4, 16, 256), BF)],
    )
    got_one = ring(parts_one, "dy")

    out_two, own_two = call(
        second_x_kernel,
        "grad_two_x",
        (*got_two, own_two),
        "vvvv",
        [far((4, 7, 64, 128), BF), near((7, 64, 128), F32)],
        [pltpu.VMEM((8, 4, 8, 128), F32)],
    )
    got_two = lax.all_to_all(out_two, "y", 0, 0, tiled=True)
    own_one, *parts_one = call(
        first_y_kernel,
        "grad_one_y",
        (*got_one, own_one, grad_hidden, cols, own_two),
        "v" * 7,
        [near((7, 64, 128), F32)] + [near((10, 64, 128), BF)] * 3,
    )
    got_one = ring(parts_one, "dx")

    out, own, border = call(
        last_kernel,
        "last_stage",
        (own_two, got_two, own_one, *got_one),
        "v" * 6,
        [far((8, 112, 128), BF), near((112, 128), F32), near((10, 16, 256), BF)],
        [pltpu.VMEM((2, 7, 8, 8, 128), F32)],
    )
    planes = lax.all_to_all(out, "z", 0, 0, tiled=True)

    (grad_input,) = call(
        input_conv_kernel,
        "conv_one_back",
        (grad_hidden, block, border, cols, own, taps_one),
        "vpvvvh",
        [(jax.ShapeDtypeStruct((4, 12, 16, 256), BF), "v")],
        [
            pltpu.VMEM((27, 256, 256), BF),
            pltpu.VMEM((768, 256), F32),
            pltpu.SemaphoreType.DMA((3,)),
            pltpu.VMEM((4, 14, 16, 768), BF),
            pltpu.VMEM((4, 16, 16, 256), BF),
        ],
    )

    factor = float(256 * 768) ** (-0.5)
    result = jax.ShapeDtypeStruct((27, 8, 32), F32), "v"
    grad_one, grad_two = call(
        functools.partial(final_kernel, factor), "final_sum", (planes, own, grad_input), "vvh", [result, result]
    )
    shape = lambda g: g.transpose(2, 0, 1).reshape(32, 3, 3, 3, 8)
    return grad_input[None], shape(grad_one), shape(grad_two)


def solution(mesh):
    fine = Mesh(mesh.devices.reshape(SIZES), AX)
    clip = ("z", "y")
    placed = P(clip, None, "ha", ("xh", "core"), None)
    weight = P(("ha", "xh", "core"), None, None, None, clip)
    return jax.shard_map(
        shards,
        mesh=fine,
        in_specs=(placed, placed, placed, P(), P(), P(), P(clip)),
        out_specs=(placed, weight, weight),
        check_vma=False,
    )
```

```python
import functools

import jax
import jax.numpy as jnp
from jax import lax
from jax.experimental import pallas as pl
from jax.experimental.pallas import tpu as pltpu
from jax.sharding import Mesh
from jax.sharding import PartitionSpec as P

BF = jnp.bfloat16
F32 = jnp.float32
AX = ("z", "y", "ha", "xh", "core")
SIZES = (8, 4, 2, 2, 2)
VM = pl.BlockSpec(memory_space=pltpu.VMEM)
HB = pl.BlockSpec(memory_space=pl.ANY)
SM = pl.BlockSpec(memory_space=pltpu.SMEM)
NT = (((1,), (1,)), ((), ()))
TN = (((0,), (0,)), ((), ()))


def core_pairs():
    return [(i, i ^ 1) for i in range(256)]


def block_pairs(dh, dw):
    return [(i, i // 8 * 8 + (i // 4 % 2 ^ dh) * 4 + (i + dw) % 4) for i in range(256)]


def ring_pairs(dx=0, dy=0):
    pairs = []
    for i in range(256):
        core, xh, ha, y, z = i % 2, i // 2 % 2, i // 4 % 2, i // 8 % 4, i // 32
        x, y = (xh * 2 + ha + dx) % 4, (y + dy) % 4
        pairs.append((i, ((z * 4 + y) * 2 + x % 2) * 4 + x // 2 * 2 + core))
    return pairs


def send(value, pairs):
    return lax.ppermute(value, AX, pairs)


def call(kernel, name, args, spaces, outs, scratch=(), limit=16):
    where = {"v": pltpu.VMEM, "p": pltpu.HBM, "h": pltpu.HBM}
    args = [
        pltpu.with_memory_space_constraint(a, where[s]) if s in where else a
        for a, s in zip(args, spaces)
    ]
    specs = {"v": VM, "p": VM, "h": HB, "s": SM}
    return pl.pallas_call(
        kernel,
        out_shape=tuple(o for o, _ in outs),
        in_specs=[specs[s] for s in spaces],
        out_specs=tuple(specs[s] for _, s in outs),
        scratch_shapes=list(scratch),
        compiler_params=pltpu.CompilerParams(vmem_limit_bytes=limit * 2**20),
        name=name,
    )(*args)


def near(shape, dtype):
    return pltpu.VMEM(shape, dtype), "v"


def far(shape, dtype):
    return pltpu.HBM(shape, dtype), "p"


def x_place():
    return lax.axis_index("xh") * 2 + lax.axis_index("ha")


def column(wide, lanes_half, f, j):
    cells = wide[lanes_half, pl.ds(f * 192 + j, 12, stride=16), :]
    return jnp.concatenate([cells, jnp.zeros((4, 128), F32)], axis=0)


def spread(wide, block):
    flat = block[...].reshape(768, 256).astype(F32)
    wide[0] = flat[:, 0:128]
    wide[1] = flat[:, 128:256]


def pack_kernel(one, two, row, hi, lo, corner_hi, corner_lo, same, wide):
    same[...] = one[...]
    edge = 11 * (1 - lax.axis_index("ha"))
    for n, block in enumerate((one, two)):
        spread(wide, block)
        for f in range(4):
            row[n, f] = block[f, edge]
            for j, out, corner in ((15, hi, corner_hi), (0, lo, corner_lo)):
                for h in range(2):
                    lanes = slice(h * 128, h * 128 + 128)
                    out[n, f, :, lanes] = column(wide, h, f, j).astype(BF)
                    cell = wide[h, pl.ds(f * 192 + edge * 16 + j, 1), :]
                    corner[n, f, :, lanes] = jnp.broadcast_to(cell, (16, 128)).astype(BF)


def pad_block(put, block, row, left, right, corner_left, corner_right):
    ha, wa = lax.axis_index("ha"), lax.axis_index("xh") * 2 + lax.axis_index("core")
    is_top, is_low = (ha == 1).astype(F32), (ha == 0).astype(F32)
    rest = jnp.zeros((2, 256), F32)
    for f in range(4):
        edge = row(f).astype(F32)
        put(f, 0, edge * is_top)
        put(f, 13, edge * is_low)
        for r in range(12):
            put(f, r + 1, block(f, r))
        for n, side, corner, has in (
            (14, left, corner_left, (wa > 0).astype(F32)),
            (15, right, corner_right, (wa < 3).astype(F32)),
        ):
            cells, end = side(f).astype(F32)[0:12], corner(f).astype(F32)[0:1]
            cells = jnp.concatenate([end * is_top, cells, end * is_low, rest], axis=0)
            put(f, n, cells * has)


def build_shifted(put, padded):
    col = lax.broadcasted_iota(jnp.int32, (16, 256), 0)
    for f in range(4):
        lefts, rights = padded[f, 14].astype(F32), padded[f, 15].astype(F32)
        for r in range(14):
            cells, lo, hi = padded[f, r].astype(F32), lefts[r : r + 1], rights[r : r + 1]
            put(f, r, 1, padded[f, r])
            put(f, r, 0, jnp.where(col == 0, lo, pltpu.roll(cells, 1, 0)).astype(BF))
            put(f, r, 2, jnp.where(col == 15, hi, pltpu.roll(cells, 15, 0)).astype(BF))


def keep_in(padded):
    def put(f, n, cells):
        padded[f, n] = cells.astype(BF)

    return put


def put_back(wide):
    def put(f, r, which, cells):
        wide[f, r, :, (2 - which) * 256 : (3 - which) * 256] = cells

    return put


def weight_copies(weight, held, sem):
    return [
        pltpu.make_async_copy(weight.at[pl.ds(a * 9, 9)], held.at[pl.ds(a * 9, 9)], sem.at[a])
        for a in range(3)
    ]


def conv_sum(wide, held, total):
    for a in (2, 1, 0):
        frames = a + 2
        for b in range(3):
            window = wide[2 - a : 4, 2 - b : 14 - b].reshape(frames * 192, 768)
            part = None
            for e in range(3):
                one = lax.dot_general(
                    window[:, e * 256 : (e + 1) * 256],
                    held[(a * 3 + b) * 3 + e],
                    NT,
                    preferred_element_type=F32,
                )
                part = one if part is None else part + one
            if a == 2 and b == 0:
                total[...] = part
            else:
                total[0 : frames * 192] += part


def channel_order():
    lane = lax.broadcasted_iota(jnp.int32, (256, 256), 1)
    goal, kept = (x_place() + (lane >> 5)) & 3, lax.axis_index("core") ^ (lane >> 7)
    source = ((goal & 1) << 7) + ((goal >> 1) << 6) + (kept << 5) + (lane & 31)
    return (lax.broadcasted_iota(jnp.int32, (256, 256), 0) == source).astype(BF)


def film_kernel(
    step, inputs, hidden, table, weight, act_out, inp_out, slope, taps,
    film, blocks, sem, block_sem, tap_sem,
):
    start = step[0]
    whole = pl.multiple_of(start // 8 * 8, 8)
    film_copy = pltpu.make_async_copy(table.at[pl.ds(whole, 8)], film, sem)
    film_copy.start()
    block_copies = [
        pltpu.make_async_copy(ref, blocks.at[n], block_sem.at[n])
        for n, ref in enumerate((inputs, hidden))
    ]
    for copy in block_copies:
        copy.start()
    copies = weight_copies(weight, taps, tap_sem)
    for copy in copies:
        copy.start()
    order = channel_order()
    sort = lambda v: jnp.dot(v, order, preferred_element_type=F32).astype(BF)
    for copy in block_copies:
        copy.wait()
    film_copy.wait()
    inp_out[...] = sort(blocks[0].reshape(768, 256)).reshape(4, 12, 16, 256)
    line = film[pl.ds(start - whole, 1), :]
    scale, shift = 1.0 + line[:, 0:256], line[:, 256:512]
    shifted = blocks[1].reshape(768, 256).astype(F32) * scale + shift
    sigma = jax.nn.sigmoid(shifted)
    act_out[...] = sort((shifted * sigma).astype(BF))
    slope[...] = scale * sigma * (1.0 + shifted * (1.0 - sigma))
    for copy in copies:
        copy.wait()


def pad_kernel(block, row, left, right, corner_left, corner_right, act, out):
    sides = (row, left, right, corner_left, corner_right)
    pad_block(keep_in(out), lambda f, r: block[f, r], *[lambda f, s=s: s[0, f] for s in sides])
    for f in range(4):
        for n in range(12):
            cells = act[f * 192 + n * 16 : f * 192 + n * 16 + 16, 128:256]
            out[f, 16 + n % 6, :, n // 6 * 128 : n // 6 * 128 + 128] = cells


def first_kernel(padded, slope, taps, wide, hid_out, total):
    build_shifted(put_back(wide), padded)
    conv_sum(wide, taps, total)
    hid_out[...] = (total[...] * slope[...]).astype(BF).reshape(4, 12, 16, 256)


def input_conv_kernel(
    hid, block, border, cols, after, weight, out, held, total, sem, wide, padded, near_block
):
    del after
    copies = weight_copies(weight, held, sem)
    copies.append(pltpu.make_async_copy(block, near_block, sem.at[3]))
    for copy in copies:
        copy.start()
    is_one = lax.axis_index("core") == 1

    def pick(when_one, when_zero):
        return jnp.where(is_one, when_one.astype(F32), when_zero.astype(F32))

    faces, outers = border[8].astype(F32), border[9].astype(F32)[4:8]
    pad_block(
        keep_in(padded),
        lambda f, r: hid[f, r],
        lambda f: border[f],
        lambda f: pick(cols[0, f], border[4 + f]),
        lambda f: pick(border[4 + f], cols[1, f]),
        lambda f: pick(faces[f : f + 1], outers[f : f + 1]),
        lambda f: pick(outers[f : f + 1], faces[f : f + 1]),
    )
    build_shifted(put_back(wide), padded)
    for copy in copies:
        copy.wait()
    conv_sum(wide, held, total)
    grad = near_block[...].reshape(768, 256).astype(F32) + total[...]
    out[...] = grad.astype(BF).reshape(4, 12, 16, 256)


def second_own_kernel(wide, act, got, after, keep, one, two, three, pair_wide, pair_act):
    del after
    build_shifted(put_back(pair_wide), got)
    for f in range(4):
        for n in range(12):
            cells = got[f, 16 + n % 6, :, n // 6 * 128 : n // 6 * 128 + 128]
            pair_act[f * 192 + n * 16 : f * 192 + n * 16 + 16, :] = cells
    for a in range(3):
        rows = (a + 2) * 192
        for b in range(3):
            total = None
            for left, right in ((act[0:rows, 0:128], wide), (pair_act[0:rows], pair_wide)):
                window = right[2 - a : 4, 2 - b : 14 - b].reshape(rows, 768)
                part = lax.dot_general(left, window, TN, preferred_element_type=F32)
                total = part if total is None else total + part
            for d, out in enumerate((keep, one, two, three)):
                out[a * 3 + b] = total[d * 32 : d * 32 + 32].astype(out.dtype)


def second_x_kernel(got1, got2, got3, own, keep, one, two, three, held):
    y = lax.axis_index("y")

    def tap(t):
        ab, lanes = t // 3, slice(t % 3 * 256, t % 3 * 256 + 256)
        total = own[ab, :, lanes]
        for got in (got1, got2, got3):
            total = total + got[ab, :, lanes].astype(F32)
        return total

    for g in range(7):
        parts = [tap(t) if t < 27 else jnp.zeros((32, 256), F32) for t in range(4 * g, 4 * g + 4)]
        held[...] = jnp.concatenate(parts, axis=0).T.reshape(8, 4, 8, 128)
        for d, out in enumerate((keep, one, two, three)):
            out[g] = held[:, (y + d) & 3].reshape(64, 128).astype(out.dtype)
    for out in (one, two, three):
        out[7:10] = jnp.zeros((3, 64, 128), BF)


def border_at(base, n, h):
    slot = n * 2 + h
    return base + slot // 4, slice(slot % 4 * 16, slot % 4 * 16 + 16)


def first_grad_kernel(
    hid, inp, row, left, right, corner_left, corner_right, after,
    own, pair, wide, padded, side, flat,
):
    del after
    order = channel_order()
    for n, ref in enumerate((row, left, right, corner_left, corner_right)):
        cells = jnp.dot(ref[1].reshape(64, 256), order, preferred_element_type=F32)
        side[n] = cells.reshape(4, 16, 256)

    def put(f, r, which, cells):
        at = which * 128
        wide[f, r, :, at : at + 128] = cells[:, 0:128]
        wide[f, r, :, at + 384 : at + 512] = cells[:, 128:256]

    pad_block(
        keep_in(padded), lambda f, r: inp[f, r], *[lambda f, n=n: side[n, f] for n in range(5)]
    )
    build_shifted(put, padded)
    spread(flat, hid)
    for f in range(4):
        for n, j in ((f, 15), (4 + f, 0)):
            for h in range(2):
                q, rows = border_at(0, n, h)
                pair[q, 27, rows] = column(flat, h, f, j)
    for a in range(3):
        rows = (a + 2) * 192
        left = hid[2 - a : 4].reshape(rows, 256)
        for b in range(3):
            window = wide[0 : a + 2, b : b + 12].reshape(rows, 768)
            grad = lax.dot_general(left, window, TN, preferred_element_type=F32)
            grad = grad.reshape(8, 4, 8, 768)
            for q in range(4):
                piece = grad[:, q].reshape(64, 768)
                for e in range(3):
                    t = (a * 3 + b) * 3 + e
                    own[q, t] = piece[:, e * 128 : e * 128 + 128]
                    pair[q, t] = piece[:, e * 128 + 384 : e * 128 + 512]


def first_sum_kernel(own, pair, after, keep, one, two, three, cols):
    del after
    y = lax.axis_index("y")
    for d, out in enumerate((keep, one, two, three)):
        q = (y + d) & 3
        out[...] = (own[q] + pair[q, 0:27]).astype(out.dtype)
    for n in range(8):
        for h in range(2):
            q, rows = border_at(0, n, h)
            cols[n // 4, n % 4, :, h * 128 : h * 128 + 128] = pair[q, 27, rows].astype(BF)


def first_y_kernel(got1, got2, got3, own, hid, cols, after, keep, one, two, three):
    del after

    def tap(t):
        total = own[t]
        for got in (got1, got2, got3):
            total = total + got[t].astype(F32)
        return total

    for g in range(7):
        taps = [tap(t) if t < 27 else jnp.zeros((64, 128), F32) for t in range(4 * g, 4 * g + 4)]
        for d, out in enumerate((keep, one, two, three)):
            piece = jnp.concatenate([v[:, d * 32 : d * 32 + 32] for v in taps], axis=1)
            out[g] = piece.astype(out.dtype)

    is_one = lax.axis_index("core") == 1
    edge = 11 * (1 - lax.axis_index("ha"))
    along, across, faces, outers = [], [], [], []
    for f in range(4):
        hi, lo = cols[0, f].astype(F32), cols[1, f].astype(F32)
        face, outer = jnp.where(is_one, hi, lo), jnp.where(is_one, lo, hi)
        along.append(hid[f, edge])
        across.append(outer.astype(BF))
        faces.append(jnp.where(edge == 0, face[0:1], face[11:12]))
        outers.append(jnp.where(edge == 0, outer[0:1], outer[11:12]))
    corners = jnp.concatenate(faces + outers + [jnp.zeros((8, 256), F32)], axis=0).astype(BF)
    rest = [jnp.zeros((16, 256), BF)] * 2
    along, across = along + [corners, rest[0]], across + rest
    for out, tiles in ((one, along), (two, across), (three, along)):
        for n, cells in enumerate(tiles):
            for h in range(2):
                out[border_at(7, n, h)] = cells[:, h * 128 : h * 128 + 128]


def last_kernel(own_two, a2, a1, a3, own_one, b2, b1, b3, out, keep, border, held):
    low = lax.axis_index("ha") == 0
    for h in range(2):
        lanes = slice(h * 128, h * 128 + 128)
        for n in range(5):
            first, last = b1[border_at(7, n, h)].astype(F32), b3[border_at(7, n, h)].astype(F32)
            across, along = jnp.where(low, last, first), jnp.where(low, first, last)
            if n < 4:
                border[n, :, lanes] = across.astype(BF)
                border[4 + n, :, lanes] = b2[border_at(7, n, h)]
            else:
                border[8, :, lanes], border[9, :, lanes] = across.astype(BF), along.astype(BF)
    for n, (own, got) in enumerate(((own_two, (a1, a2, a3)), (own_one, (b1, b2, b3)))):
        total = own[...]
        for ref in got:
            total = total + ref[0:7].astype(F32)
        held[n] = total.reshape(7, 8, 8, 128)

    def plane(z):
        return jnp.concatenate([held[n, :, z].reshape(56, 128) for n in range(2)], axis=0)

    for q in range(8):
        out[q] = plane(q).astype(BF)
    keep[...] = plane(lax.axis_index("z"))


def final_kernel(factor, got, own, after, one, two):
    del after
    z = lax.axis_index("z")
    total = own[...]
    for d in range(1, 8):
        total = total + got[(z + d) & 7].astype(F32)
    total = (total * factor).reshape(2, 7, 8, 128)
    for out, which in ((two, 0), (one, 1)):
        for t in range(27):
            out[t] = total[which, t // 4, :, t % 4 * 32 : t % 4 * 32 + 32]


def shards(activations, saved_hidden, cotangent, conv_one, conv_two, film_table, timesteps):
    inputs, hidden, block = activations[0], saved_hidden[0], cotangent[0]
    taps_one = conv_one.transpose(1, 2, 3, 0, 4).reshape(27, 256, 256)
    taps_two = conv_two.transpose(1, 2, 3, 0, 4).reshape(27, 256, 256)
    wide = near((4, 14, 16, 768), BF)
    quads = [near((7, 64, 128), F32)] + [near((10, 64, 128), BF)] * 3

    def ring(parts, axis):
        return [send(parts[d - 1], ring_pairs(**{axis: d})) for d in (2, 1, 3)]

    *packed, held_block = call(
        pack_kernel,
        "pack_first",
        (block, inputs),
        "pp",
        [near((2, 4, 16, 256), BF)] * 5 + [near((4, 12, 16, 256), BF)],
        [pltpu.VMEM((2, 768, 128), F32)],
    )
    ways = ((1, 0), (0, 1), (0, -1), (1, 1), (1, -1))
    sides = [send(p, block_pairs(*way)) for p, way in zip(packed, ways)]
    act, inp, slope, held_two = call(
        film_kernel,
        "film",
        (timesteps, inputs, hidden, film_table, taps_two),
        "shhhh",
        [
            near((768, 256), BF),
            near((4, 12, 16, 256), BF),
            near((768, 256), F32),
            near((27, 256, 256), BF),
        ],
        [
            pltpu.VMEM((8, 512), F32),
            pltpu.VMEM((2, 4, 12, 16, 256), BF),
            pltpu.SemaphoreType.DMA,
            pltpu.SemaphoreType.DMA((2,)),
            pltpu.SemaphoreType.DMA((3,)),
        ],
    )
    (padded,) = call(
        pad_kernel,
        "pad_cotangent",
        (held_block, *sides, act),
        "vvvvvvv",
        [near((4, 22, 16, 256), BF)],
    )
    pair_padded = send(padded, core_pairs())
    wide_cot, grad_hidden = call(
        first_kernel,
        "conv_two_back",
        (padded, slope, held_two),
        "vvv",
        [wide, near((4, 12, 16, 256), BF)],
        [pltpu.VMEM((768, 256), F32)],
    )

    own_one, pair_one = call(
        first_grad_kernel,
        "grad_one",
        (grad_hidden, inp, *sides, pair_padded),
        "vv" + "v" * 6,
        [near((4, 27, 64, 128), F32), near((4, 28, 64, 128), F32)],
        [
            pltpu.VMEM((4, 14, 16, 768), BF),
            pltpu.VMEM((4, 16, 16, 256), BF),
            pltpu.VMEM((5, 4, 16, 256), F32),
            pltpu.VMEM((2, 768, 128), F32),
        ],
    )
    got_pair_one = send(pair_one, core_pairs())
    own_two, *parts = call(
        second_own_kernel,
        "grad_two",
        (wide_cot, act, pair_padded, pair_one),
        "vvvv",
        [near((9, 32, 768), F32)] + [near((9, 32, 768), BF)] * 3,
        [pltpu.VMEM((4, 14, 16, 768), BF), pltpu.VMEM((768, 128), BF)],
    )
    got_two = ring(parts, "dx")
    own_one, *parts_one, cols = call(
        first_sum_kernel,
        "grad_one_sum",
        (own_one, got_pair_one, parts[0]),
        "vvv",
        [near((27, 64, 128), F32)]
        + [near((27, 64, 128), BF)] * 3
        + [near((2, 4, 16, 256), BF)],
    )
    got_one = ring(parts_one, "dy")

    own_two, *parts = call(
        second_x_kernel,
        "grad_two_x",
        (*got_two, own_two),
        "vvvv",
        quads,
        [pltpu.VMEM((8, 4, 8, 128), F32)],
    )
    got_two = ring(parts, "dy")
    own_one, *parts_one = call(
        first_y_kernel,
        "grad_one_y",
        (*got_one, own_one, grad_hidden, cols, parts[0]),
        "v" * 7,
        quads,
    )
    got_one = ring(parts_one, "dx")

    out, own, border = call(
        last_kernel,
        "last_stage",
        (own_two, *got_two, own_one, *got_one),
        "v" * 8,
        [far((8, 112, 128), BF), near((112, 128), F32), near((10, 16, 256), BF)],
        [pltpu.VMEM((2, 7, 8, 8, 128), F32)],
    )
    planes = lax.all_to_all(out, "z", 0, 0, tiled=True)

    (grad_input,) = call(
        input_conv_kernel,
        "conv_one_back",
        (grad_hidden, block, border, cols, own, taps_one),
        "vhvvvh",
        [(jax.ShapeDtypeStruct((4, 12, 16, 256), BF), "v")],
        [
            pltpu.VMEM((27, 256, 256), BF),
            pltpu.VMEM((768, 256), F32),
            pltpu.SemaphoreType.DMA((4,)),
            pltpu.VMEM((4, 14, 16, 768), BF),
            pltpu.VMEM((4, 16, 16, 256), BF),
            pltpu.VMEM((4, 12, 16, 256), BF),
        ],
    )

    factor = float(256 * 768) ** (-0.5)
    result = jax.ShapeDtypeStruct((27, 8, 32), F32), "v"
    grad_one, grad_two = call(
        functools.partial(final_kernel, factor), "final_sum", (planes, own, grad_input), "vvh", [result, result]
    )
    shape = lambda g: g.transpose(2, 0, 1).reshape(32, 3, 3, 3, 8)
    return grad_input[None], shape(grad_one), shape(grad_two)


def solution(mesh):
    fine = Mesh(mesh.devices.reshape(SIZES), AX)
    clip = ("z", "y")
    placed = P(clip, None, "ha", ("xh", "core"), None)
    weight = P(("ha", "xh", "core"), None, None, None, clip)
    return jax.shard_map(
        shards,
        mesh=fine,
        in_specs=(placed, placed, placed, P(), P(), P(), P(clip)),
        out_specs=(placed, weight, weight),
        check_vma=False,
    )
```

```python
import functools

import jax
import jax.numpy as jnp
from jax import lax
from jax.experimental import pallas as pl
from jax.experimental.pallas import tpu as pltpu
from jax.sharding import Mesh
from jax.sharding import PartitionSpec as P

BF = jnp.bfloat16
F32 = jnp.float32
AX = ("z", "y", "ha", "xh", "core")
SIZES = (8, 4, 2, 2, 2)
VM = pl.BlockSpec(memory_space=pltpu.VMEM)
HB = pl.BlockSpec(memory_space=pl.ANY)
SM = pl.BlockSpec(memory_space=pltpu.SMEM)
NT = (((1,), (1,)), ((), ()))
TN = (((0,), (0,)), ((), ()))


def core_pairs():
    return [(i, i ^ 1) for i in range(256)]


def block_pairs(dh, dw):
    return [(i, i // 8 * 8 + (i // 4 % 2 ^ dh) * 4 + (i + dw) % 4) for i in range(256)]


def ring_pairs(dx=0, dy=0):
    pairs = []
    for i in range(256):
        core, xh, ha, y, z = i % 2, i // 2 % 2, i // 4 % 2, i // 8 % 4, i // 32
        x, y = (xh * 2 + ha + dx) % 4, (y + dy) % 4
        pairs.append((i, ((z * 4 + y) * 2 + x % 2) * 4 + x // 2 * 2 + core))
    return pairs


def send(value, pairs):
    return lax.ppermute(value, AX, pairs)


def call(kernel, name, args, spaces, outs, scratch=(), limit=16):
    where = {"v": pltpu.VMEM, "p": pltpu.HBM, "h": pltpu.HBM}
    args = [
        pltpu.with_memory_space_constraint(a, where[s]) if s in where else a
        for a, s in zip(args, spaces)
    ]
    specs = {"v": VM, "p": VM, "h": HB, "s": SM}
    return pl.pallas_call(
        kernel,
        out_shape=tuple(o for o, _ in outs),
        in_specs=[specs[s] for s in spaces],
        out_specs=tuple(specs[s] for _, s in outs),
        scratch_shapes=list(scratch),
        compiler_params=pltpu.CompilerParams(vmem_limit_bytes=limit * 2**20),
        name=name,
    )(*args)


def near(shape, dtype):
    return pltpu.VMEM(shape, dtype), "v"


def far(shape, dtype):
    return pltpu.HBM(shape, dtype), "p"


def x_place():
    return lax.axis_index("xh") * 2 + lax.axis_index("ha")


def border_cells(block, rows):
    edge = 11 * (1 - lax.axis_index("ha"))
    row = lax.broadcasted_iota(jnp.int32, (rows, 1), 0)
    column = jnp.where(row < 64, 15, 0) + (row >> 4 & 3) * 192 + (row & 15) * 16
    column = jnp.where((row & 15) < 12, column, -1)
    corner = jnp.where(row < 144, 15, 0) + (row & 15) * 192 + edge * 16
    corner = jnp.where((row & 15) < 4, corner, -1)
    source = jnp.where(row < 128, column, corner)
    chosen = (lax.broadcasted_iota(jnp.int32, (rows, 768), 1) == source).astype(BF)
    return jnp.dot(chosen, block.reshape(768, 256), preferred_element_type=F32)


def pack_kernel(one, two, row, hi, lo, corner_hi, corner_lo, same):
    same[...] = one[...]
    edge = 11 * (1 - lax.axis_index("ha"))
    for n, block in enumerate((one, two)):
        cells = border_cells(block[...], 160).astype(BF)
        hi[n] = cells[0:64].reshape(4, 16, 256)
        lo[n] = cells[64:128].reshape(4, 16, 256)
        corner_hi[n], corner_lo[n] = cells[128:144], cells[144:160]
        for f in range(4):
            row[n, f] = block[f, edge]


def pad_block(put, block, row, left, right, corner_left, corner_right):
    ha, wa = lax.axis_index("ha"), lax.axis_index("xh") * 2 + lax.axis_index("core")
    is_top, is_low = (ha == 1).astype(F32), (ha == 0).astype(F32)
    rest = jnp.zeros((2, 256), F32)
    for f in range(4):
        edge = row(f).astype(F32)
        put(f, 0, edge * is_top)
        put(f, 13, edge * is_low)
        for r in range(12):
            put(f, r + 1, block(f, r))
        for n, side, corner, has in (
            (14, left, corner_left, (wa > 0).astype(F32)),
            (15, right, corner_right, (wa < 3).astype(F32)),
        ):
            cells, end = side(f).astype(F32)[0:12], corner(f).astype(F32)[0:1]
            cells = jnp.concatenate([end * is_top, cells, end * is_low, rest], axis=0)
            put(f, n, cells * has)


def build_shifted(put, padded):
    col = lax.broadcasted_iota(jnp.int32, (16, 256), 0)
    for f in range(4):
        lefts, rights = padded[f, 14].astype(F32), padded[f, 15].astype(F32)
        for r in range(14):
            cells, lo, hi = padded[f, r].astype(F32), lefts[r : r + 1], rights[r : r + 1]
            put(f, r, 1, padded[f, r])
            put(f, r, 0, jnp.where(col == 0, lo, pltpu.roll(cells, 1, 0)).astype(BF))
            put(f, r, 2, jnp.where(col == 15, hi, pltpu.roll(cells, 15, 0)).astype(BF))


def keep_in(padded):
    def put(f, n, cells):
        padded[f, n] = cells.astype(BF)

    return put


def put_back(wide):
    def put(f, r, which, cells):
        wide[f, r, :, (2 - which) * 256 : (3 - which) * 256] = cells

    return put


def weight_copies(weight, held, sem):
    return [
        pltpu.make_async_copy(weight.at[pl.ds(a * 9, 9)], held.at[pl.ds(a * 9, 9)], sem.at[a])
        for a in range(3)
    ]


def conv_sum(wide, held, total):
    for a in (2, 1, 0):
        frames = a + 2
        for b in range(3):
            window = wide[2 - a : 4, 2 - b : 14 - b].reshape(frames * 192, 768)
            part = None
            for e in range(3):
                one = lax.dot_general(
                    window[:, e * 256 : (e + 1) * 256],
                    held[(a * 3 + b) * 3 + e],
                    NT,
                    preferred_element_type=F32,
                )
                part = one if part is None else part + one
            if a == 2 and b == 0:
                total[...] = part
            else:
                total[0 : frames * 192] += part


def channel_order():
    lane = lax.broadcasted_iota(jnp.int32, (256, 256), 1)
    goal, kept = (x_place() + (lane >> 5)) & 3, lax.axis_index("core") ^ (lane >> 7)
    source = ((goal & 1) << 7) + ((goal >> 1) << 6) + (kept << 5) + (lane & 31)
    return (lax.broadcasted_iota(jnp.int32, (256, 256), 0) == source).astype(BF)


def film_kernel(
    step, inputs, hidden, table, weight, act_out, inp_out, slope, taps,
    film, blocks, sem, block_sem, tap_sem,
):
    start = step[0]
    whole = pl.multiple_of(start // 8 * 8, 8)
    film_copy = pltpu.make_async_copy(table.at[pl.ds(whole, 8)], film, sem)
    film_copy.start()
    block_copies = [
        pltpu.make_async_copy(ref, blocks.at[n], block_sem.at[n])
        for n, ref in enumerate((inputs, hidden))
    ]
    for copy in block_copies:
        copy.start()
    copies = weight_copies(weight, taps, tap_sem)
    for copy in copies:
        copy.start()
    order = channel_order()
    sort = lambda v: jnp.dot(v, order, preferred_element_type=F32).astype(BF)
    for copy in block_copies:
        copy.wait()
    inp_out[...] = sort(blocks[0].reshape(768, 256)).reshape(4, 12, 16, 256)
    film_copy.wait()
    line = film[pl.ds(start - whole, 1), :]
    scale, shift = 1.0 + line[:, 0:256], line[:, 256:512]
    shifted = blocks[1].reshape(768, 256).astype(F32) * scale + shift
    sigma = jax.nn.sigmoid(shifted)
    act_out[...] = sort((shifted * sigma).astype(BF))
    slope[...] = scale * sigma * (1.0 + shifted * (1.0 - sigma))
    for copy in copies:
        copy.wait()


def pad_kernel(block, row, left, right, corner_left, corner_right, act, out):
    pad_block(
        keep_in(out),
        lambda f, r: block[f, r],
        *[lambda f, s=s: s[0, f] for s in (row, left, right)],
        *[lambda f, s=s: s[0].astype(F32)[f : f + 1] for s in (corner_left, corner_right)],
    )
    for f in range(4):
        for n in range(12):
            cells = act[f * 192 + n * 16 : f * 192 + n * 16 + 16, 128:256]
            out[f, 16 + n % 6, :, n // 6 * 128 : n // 6 * 128 + 128] = cells


def first_kernel(padded, slope, taps, wide, hid_out, total):
    build_shifted(put_back(wide), padded)
    conv_sum(wide, taps, total)
    hid_out[...] = (total[...] * slope[...]).astype(BF).reshape(4, 12, 16, 256)


def input_conv_kernel(
    hid, block, border, cols, after, weight, out, held, total, sem, wide, padded, near_block
):
    del after
    copies = weight_copies(weight, held, sem)
    copies.append(pltpu.make_async_copy(block, near_block, sem.at[3]))
    for copy in copies:
        copy.start()
    is_one = lax.axis_index("core") == 1

    def pick(when_one, when_zero):
        return jnp.where(is_one, when_one.astype(F32), when_zero.astype(F32))

    faces, outers = border[8].astype(F32), border[9].astype(F32)[4:8]
    pad_block(
        keep_in(padded),
        lambda f, r: hid[f, r],
        lambda f: border[f],
        lambda f: pick(cols[0, f], border[4 + f]),
        lambda f: pick(border[4 + f], cols[1, f]),
        lambda f: pick(faces[f : f + 1], outers[f : f + 1]),
        lambda f: pick(outers[f : f + 1], faces[f : f + 1]),
    )
    build_shifted(put_back(wide), padded)
    for copy in copies:
        copy.wait()
    conv_sum(wide, held, total)
    grad = near_block[...].reshape(768, 256).astype(F32) + total[...]
    out[...] = grad.astype(BF).reshape(4, 12, 16, 256)


def second_own_kernel(wide, act, got, after, keep, one, two, three, pair_wide, pair_act):
    del after
    build_shifted(put_back(pair_wide), got)
    for f in range(4):
        for n in range(12):
            cells = got[f, 16 + n % 6, :, n // 6 * 128 : n // 6 * 128 + 128]
            pair_act[f * 192 + n * 16 : f * 192 + n * 16 + 16, :] = cells
    for a in range(3):
        rows = (a + 2) * 192
        for b in range(3):
            total = None
            for left, right in ((act[0:rows, 0:128], wide), (pair_act[0:rows], pair_wide)):
                window = right[2 - a : 4, 2 - b : 14 - b].reshape(rows, 768)
                part = lax.dot_general(left, window, TN, preferred_element_type=F32)
                total = part if total is None else total + part
            for d, out in enumerate((keep, one, two, three)):
                out[a * 3 + b] = total[d * 32 : d * 32 + 32].astype(out.dtype)


def second_x_kernel(got1, got2, got3, own, keep, one, two, three, held):
    y = lax.axis_index("y")

    def tap(t):
        ab, lanes = t // 3, slice(t % 3 * 256, t % 3 * 256 + 256)
        total = own[ab, :, lanes]
        for got in (got1, got2, got3):
            total = total + got[ab, :, lanes].astype(F32)
        return total

    for g in range(7):
        parts = [tap(t) if t < 27 else jnp.zeros((32, 256), F32) for t in range(4 * g, 4 * g + 4)]
        held[...] = jnp.concatenate(parts, axis=0).T.reshape(8, 4, 8, 128)
        for d, out in enumerate((keep, one, two, three)):
            out[g] = held[:, (y + d) & 3].reshape(64, 128).astype(out.dtype)
    for out in (one, two, three):
        out[7:10] = jnp.zeros((3, 64, 128), BF)


def border_at(base, n, h):
    slot = n * 2 + h
    return base + slot // 4, slice(slot % 4 * 16, slot % 4 * 16 + 16)


def first_grad_kernel(
    hid, inp, row, left, right, corner_left, corner_right, after,
    own, pair, wide, padded, side,
):
    del after
    order = channel_order()
    for at, ref in ((0, row), (4, left), (8, right), (12, corner_left), (13, corner_right)):
        size = 4 if at < 12 else 1
        cells = jnp.dot(ref[1].reshape(size * 16, 256), order, preferred_element_type=F32)
        side[at : at + size] = cells.reshape(size, 16, 256)

    def put(f, r, which, cells):
        at = which * 128
        wide[f, r, :, at : at + 128] = cells[:, 0:128]
        wide[f, r, :, at + 384 : at + 512] = cells[:, 128:256]

    pad_block(
        keep_in(padded),
        lambda f, r: inp[f, r],
        *[lambda f, n=n: side[n + f] for n in (0, 4, 8)],
        *[lambda f, n=n: side[n, f : f + 1] for n in (12, 13)],
    )
    build_shifted(put, padded)
    cells = border_cells(hid[...], 128)
    for n in range(8):
        for h in range(2):
            q, rows = border_at(0, n, h)
            pair[q, 27, rows] = cells[n * 16 : n * 16 + 16, h * 128 : h * 128 + 128]
    for a in range(3):
        rows = (a + 2) * 192
        left = hid[2 - a : 4].reshape(rows, 256)
        for b in range(3):
            window = wide[0 : a + 2, b : b + 12].reshape(rows, 768)
            grad = lax.dot_general(left, window, TN, preferred_element_type=F32)
            grad = grad.reshape(8, 4, 8, 768)
            for q in range(4):
                piece = grad[:, q].reshape(64, 768)
                for e in range(3):
                    t = (a * 3 + b) * 3 + e
                    own[q, t] = piece[:, e * 128 : e * 128 + 128]
                    pair[q, t] = piece[:, e * 128 + 384 : e * 128 + 512]


def first_sum_kernel(own, pair, after, keep, one, two, three, cols):
    del after
    y = lax.axis_index("y")
    for d, out in enumerate((keep, one, two, three)):
        q = (y + d) & 3
        out[...] = (own[q] + pair[q, 0:27]).astype(out.dtype)
    for n in range(8):
        for h in range(2):
            q, rows = border_at(0, n, h)
            cols[n // 4, n % 4, :, h * 128 : h * 128 + 128] = pair[q, 27, rows].astype(BF)


def first_y_kernel(got1, got2, got3, own, hid, cols, after, keep, one, two, three):
    del after

    def tap(t):
        total = own[t]
        for got in (got1, got2, got3):
            total = total + got[t].astype(F32)
        return total

    for g in range(7):
        taps = [tap(t) if t < 27 else jnp.zeros((64, 128), F32) for t in range(4 * g, 4 * g + 4)]
        for d, out in enumerate((keep, one, two, three)):
            piece = jnp.concatenate([v[:, d * 32 : d * 32 + 32] for v in taps], axis=1)
            out[g] = piece.astype(out.dtype)

    is_one = lax.axis_index("core") == 1
    edge = 11 * (1 - lax.axis_index("ha"))
    along, across, faces, outers = [], [], [], []
    for f in range(4):
        hi, lo = cols[0, f].astype(F32), cols[1, f].astype(F32)
        face, outer = jnp.where(is_one, hi, lo), jnp.where(is_one, lo, hi)
        along.append(hid[f, edge])
        across.append(outer.astype(BF))
        faces.append(jnp.where(edge == 0, face[0:1], face[11:12]))
        outers.append(jnp.where(edge == 0, outer[0:1], outer[11:12]))
    corners = jnp.concatenate(faces + outers + [jnp.zeros((8, 256), F32)], axis=0).astype(BF)
    rest = [jnp.zeros((16, 256), BF)] * 2
    along, across = along + [corners, rest[0]], across + rest
    for out, tiles in ((one, along), (two, across), (three, along)):
        for n, cells in enumerate(tiles):
            for h in range(2):
                out[border_at(7, n, h)] = cells[:, h * 128 : h * 128 + 128]


def last_kernel(own_two, a2, a1, a3, own_one, b2, b1, b3, out, keep, border, held):
    low = lax.axis_index("ha") == 0
    for h in range(2):
        lanes = slice(h * 128, h * 128 + 128)
        for n in range(5):
            first, last = b1[border_at(7, n, h)].astype(F32), b3[border_at(7, n, h)].astype(F32)
            across, along = jnp.where(low, last, first), jnp.where(low, first, last)
            if n < 4:
                border[n, :, lanes] = across.astype(BF)
                border[4 + n, :, lanes] = b2[border_at(7, n, h)]
            else:
                border[8, :, lanes], border[9, :, lanes] = across.astype(BF), along.astype(BF)
    for n, (own, got) in enumerate(((own_two, (a1, a2, a3)), (own_one, (b1, b2, b3)))):
        total = own[...]
        for ref in got:
            total = total + ref[0:7].astype(F32)
        held[n] = total.reshape(7, 8, 8, 128)

    def plane(z):
        return jnp.concatenate([held[n, :, z].reshape(56, 128) for n in range(2)], axis=0)

    for q in range(8):
        out[q] = plane(q).astype(BF)
    keep[...] = plane(lax.axis_index("z"))


def final_kernel(factor, got, own, after, one, two):
    del after
    z = lax.axis_index("z")
    total = own[...]
    for d in range(1, 8):
        total = total + got[(z + d) & 7].astype(F32)
    total = (total * factor).reshape(2, 7, 8, 128)
    for out, which in ((two, 0), (one, 1)):
        for t in range(27):
            out[t] = total[which, t // 4, :, t % 4 * 32 : t % 4 * 32 + 32]


def shards(activations, saved_hidden, cotangent, conv_one, conv_two, film_table, timesteps):
    inputs, hidden, block = activations[0], saved_hidden[0], cotangent[0]
    taps_one = conv_one.transpose(1, 2, 3, 0, 4).reshape(27, 256, 256)
    taps_two = conv_two.transpose(1, 2, 3, 0, 4).reshape(27, 256, 256)
    wide = near((4, 14, 16, 768), BF)
    quads = [near((7, 64, 128), F32)] + [near((10, 64, 128), BF)] * 3

    def ring(parts, axis):
        return [send(parts[d - 1], ring_pairs(**{axis: d})) for d in (2, 1, 3)]

    *packed, held_block = call(
        pack_kernel,
        "pack_first",
        (block, inputs),
        "pp",
        [near((2, 4, 16, 256), BF)] * 3
        + [near((2, 16, 256), BF)] * 2
        + [near((4, 12, 16, 256), BF)],
    )
    ways = ((1, 0), (0, 1), (0, -1), (1, 1), (1, -1))
    sides = [send(p, block_pairs(*way)) for p, way in zip(packed, ways)]
    act, inp, slope, held_two = call(
        film_kernel,
        "film",
        (timesteps, inputs, hidden, film_table, taps_two),
        "shhhh",
        [
            near((768, 256), BF),
            near((4, 12, 16, 256), BF),
            near((768, 256), F32),
            near((27, 256, 256), BF),
        ],
        [
            pltpu.VMEM((8, 512), F32),
            pltpu.VMEM((2, 4, 12, 16, 256), BF),
            pltpu.SemaphoreType.DMA,
            pltpu.SemaphoreType.DMA((2,)),
            pltpu.SemaphoreType.DMA((3,)),
        ],
    )
    (padded,) = call(
        pad_kernel,
        "pad_cotangent",
        (held_block, *sides, act),
        "vvvvvvv",
        [near((4, 22, 16, 256), BF)],
    )
    pair_padded = send(padded, core_pairs())
    wide_cot, grad_hidden = call(
        first_kernel,
        "conv_two_back",
        (padded, slope, held_two),
        "vvv",
        [wide, near((4, 12, 16, 256), BF)],
        [pltpu.VMEM((768, 256), F32)],
    )

    own_one, pair_one = call(
        first_grad_kernel,
        "grad_one",
        (grad_hidden, inp, *sides, pair_padded),
        "vv" + "v" * 6,
        [near((4, 27, 64, 128), F32), near((4, 28, 64, 128), F32)],
        [
            pltpu.VMEM((4, 14, 16, 768), BF),
            pltpu.VMEM((4, 16, 16, 256), BF),
            pltpu.VMEM((14, 16, 256), F32),
        ],
    )
    got_pair_one = send(pair_one, core_pairs())
    own_two, *parts = call(
        second_own_kernel,
        "grad_two",
        (wide_cot, act, pair_padded, pair_one),
        "vvvv",
        [near((9, 32, 768), F32)] + [near((9, 32, 768), BF)] * 3,
        [pltpu.VMEM((4, 14, 16, 768), BF), pltpu.VMEM((768, 128), BF)],
    )
    got_two = ring(parts, "dx")
    own_one, *parts_one, cols = call(
        first_sum_kernel,
        "grad_one_sum",
        (own_one, got_pair_one, parts[0]),
        "vvv",
        [near((27, 64, 128), F32)]
        + [near((27, 64, 128), BF)] * 3
        + [near((2, 4, 16, 256), BF)],
    )
    got_one = ring(parts_one, "dy")

    own_two, *parts = call(
        second_x_kernel,
        "grad_two_x",
        (*got_two, own_two),
        "vvvv",
        quads,
        [pltpu.VMEM((8, 4, 8, 128), F32)],
    )
    got_two = ring(parts, "dy")
    own_one, *parts_one = call(
        first_y_kernel,
        "grad_one_y",
        (*got_one, own_one, grad_hidden, cols, parts[0]),
        "v" * 7,
        quads,
    )
    got_one = ring(parts_one, "dx")

    out, own, border = call(
        last_kernel,
        "last_stage",
        (own_two, *got_two, own_one, *got_one),
        "v" * 8,
        [far((8, 112, 128), BF), near((112, 128), F32), near((10, 16, 256), BF)],
        [pltpu.VMEM((2, 7, 8, 8, 128), F32)],
    )
    planes = lax.all_to_all(out, "z", 0, 0, tiled=True)

    (grad_input,) = call(
        input_conv_kernel,
        "conv_one_back",
        (grad_hidden, block, border, cols, own, taps_one),
        "vhvvvh",
        [(jax.ShapeDtypeStruct((4, 12, 16, 256), BF), "v")],
        [
            pltpu.VMEM((27, 256, 256), BF),
            pltpu.VMEM((768, 256), F32),
            pltpu.SemaphoreType.DMA((4,)),
            pltpu.VMEM((4, 14, 16, 768), BF),
            pltpu.VMEM((4, 16, 16, 256), BF),
            pltpu.VMEM((4, 12, 16, 256), BF),
        ],
    )

    factor = float(256 * 768) ** (-0.5)
    result = jax.ShapeDtypeStruct((27, 8, 32), F32), "v"
    grad_one, grad_two = call(
        functools.partial(final_kernel, factor), "final_sum", (planes, own, grad_input), "vvh", [result, result]
    )
    shape = lambda g: g.transpose(2, 0, 1).reshape(32, 3, 3, 3, 8)
    return grad_input[None], shape(grad_one), shape(grad_two)


def solution(mesh):
    fine = Mesh(mesh.devices.reshape(SIZES), AX)
    clip = ("z", "y")
    placed = P(clip, None, "ha", ("xh", "core"), None)
    weight = P(("ha", "xh", "core"), None, None, None, clip)
    return jax.shard_map(
        shards,
        mesh=fine,
        in_specs=(placed, placed, placed, P(), P(), P(), P(clip)),
        out_specs=(placed, weight, weight),
        check_vma=False,
    )
```

```python
import functools

import jax
import jax.numpy as jnp
from jax import lax
from jax.experimental import pallas as pl
from jax.experimental.pallas import tpu as pltpu
from jax.sharding import Mesh
from jax.sharding import PartitionSpec as P

BF = jnp.bfloat16
F32 = jnp.float32
AX = ("z", "y", "ha", "xh", "core")
SIZES = (8, 4, 2, 2, 2)
VM = pl.BlockSpec(memory_space=pltpu.VMEM)
HB = pl.BlockSpec(memory_space=pl.ANY)
SM = pl.BlockSpec(memory_space=pltpu.SMEM)
NT = (((1,), (1,)), ((), ()))
TN = (((0,), (0,)), ((), ()))


def core_pairs():
    return [(i, i ^ 1) for i in range(256)]


def block_pairs(dh, dw):
    return [(i, i ^ (dh * 4 + dw)) for i in range(256)]


def ring_pairs(dx=0, dy=0):
    pairs = []
    for i in range(256):
        core, xh, ha, y, z = i % 2, i // 2 % 2, i // 4 % 2, i // 8 % 4, i // 32
        x, y = (xh * 2 + ha) ^ dx, y ^ dy
        pairs.append((i, ((z * 4 + y) * 2 + x % 2) * 4 + x // 2 * 2 + core))
    return pairs


def send(value, pairs):
    return lax.ppermute(value, AX, pairs)


def call(kernel, name, args, spaces, outs, scratch=(), limit=16):
    where = {"v": pltpu.VMEM, "p": pltpu.HBM, "h": pltpu.HBM}
    args = [
        pltpu.with_memory_space_constraint(a, where[s]) if s in where else a
        for a, s in zip(args, spaces)
    ]
    specs = {"v": VM, "p": VM, "h": HB, "s": SM}
    return pl.pallas_call(
        kernel,
        out_shape=tuple(o for o, _ in outs),
        in_specs=[specs[s] for s in spaces],
        out_specs=tuple(specs[s] for _, s in outs),
        scratch_shapes=list(scratch),
        compiler_params=pltpu.CompilerParams(vmem_limit_bytes=limit * 2**20),
        name=name,
    )(*args)


def near(shape, dtype):
    return pltpu.VMEM(shape, dtype), "v"


def far(shape, dtype):
    return pltpu.HBM(shape, dtype), "p"


def x_place():
    return lax.axis_index("xh") * 2 + lax.axis_index("ha")


def by_core(when_one, when_zero):
    return jnp.where(lax.axis_index("core") == 1, when_one, when_zero)


def border_cells(block, rows):
    edge = 11 * (1 - lax.axis_index("ha"))
    row = lax.broadcasted_iota(jnp.int32, (rows, 1), 0)
    column = jnp.where(row < 64, 15, 0) + (row >> 4 & 3) * 192 + (row & 15) * 16
    column = jnp.where((row & 15) < 12, column, -1)
    corner = jnp.where(row < 144, 15, 0) + (row & 15) * 192 + edge * 16
    corner = jnp.where((row & 15) < 4, corner, -1)
    source = jnp.where(row < 128, column, corner)
    chosen = (lax.broadcasted_iota(jnp.int32, (rows, 768), 1) == source).astype(BF)
    return jnp.dot(chosen, block.reshape(768, 256), preferred_element_type=F32)


def pack_kernel(one, two, row, face, outer, corner_face, corner_outer, same):
    same[...] = one[...]
    edge = 11 * (1 - lax.axis_index("ha"))
    for n, block in enumerate((one, two)):
        cells = border_cells(block[...], 160)
        hi, lo = cells[0:64].reshape(4, 16, 256), cells[64:128].reshape(4, 16, 256)
        face[n], outer[n] = by_core(lo, hi).astype(BF), by_core(hi, lo).astype(BF)
        hi, lo = cells[128:144], cells[144:160]
        corner_face[n], corner_outer[n] = by_core(lo, hi).astype(BF), by_core(hi, lo).astype(BF)
        for f in range(4):
            row[n, f] = block[f, edge]


def pad_block(put, block, row, left, right, corner_left, corner_right):
    ha, wa = lax.axis_index("ha"), lax.axis_index("xh") * 2 + lax.axis_index("core")
    is_top, is_low = (ha == 1).astype(F32), (ha == 0).astype(F32)
    rest = jnp.zeros((2, 256), F32)
    for f in range(4):
        edge = row(f).astype(F32)
        put(f, 0, edge * is_top)
        put(f, 13, edge * is_low)
        for r in range(12):
            put(f, r + 1, block(f, r))
        for n, side, corner, has in (
            (14, left, corner_left, (wa > 0).astype(F32)),
            (15, right, corner_right, (wa < 3).astype(F32)),
        ):
            cells, end = side(f).astype(F32)[0:12], corner(f).astype(F32)[0:1]
            cells = jnp.concatenate([end * is_top, cells, end * is_low, rest], axis=0)
            put(f, n, cells * has)


def build_shifted(put, padded):
    col = lax.broadcasted_iota(jnp.int32, (16, 256), 0)
    for f in range(4):
        lefts, rights = padded[f, 14].astype(F32), padded[f, 15].astype(F32)
        for r in range(14):
            cells, lo, hi = padded[f, r].astype(F32), lefts[r : r + 1], rights[r : r + 1]
            put(f, r, 1, padded[f, r])
            put(f, r, 0, jnp.where(col == 0, lo, pltpu.roll(cells, 1, 0)).astype(BF))
            put(f, r, 2, jnp.where(col == 15, hi, pltpu.roll(cells, 15, 0)).astype(BF))


def keep_in(padded):
    def put(f, n, cells):
        padded[f, n] = cells.astype(BF)

    return put


def put_back(wide):
    def put(f, r, which, cells):
        wide[f, r, :, (2 - which) * 256 : (3 - which) * 256] = cells

    return put


def weight_copies(weight, held, sem):
    return [
        pltpu.make_async_copy(weight.at[pl.ds(a * 9, 9)], held.at[pl.ds(a * 9, 9)], sem.at[a])
        for a in range(3)
    ]


def conv_sum(wide, held, total):
    for a in (2, 1, 0):
        frames = a + 2
        for b in range(3):
            window = wide[2 - a : 4, 2 - b : 14 - b].reshape(frames * 192, 768)
            part = None
            for e in range(3):
                one = lax.dot_general(
                    window[:, e * 256 : (e + 1) * 256],
                    held[(a * 3 + b) * 3 + e],
                    NT,
                    preferred_element_type=F32,
                )
                part = one if part is None else part + one
            if a == 2 and b == 0:
                total[...] = part
            else:
                total[0 : frames * 192] += part


def channel_order():
    lane = lax.broadcasted_iota(jnp.int32, (256, 256), 1)
    goal, kept = x_place() ^ ((lane >> 5) & 3), lax.axis_index("core") ^ (lane >> 7)
    source = ((goal & 1) << 7) + ((goal >> 1) << 6) + (kept << 5) + (lane & 31)
    return (lax.broadcasted_iota(jnp.int32, (256, 256), 0) == source).astype(BF)


def film_kernel(
    step, inputs, hidden, table, weight, act_out, inp_out, slope, taps,
    film, blocks, sem, block_sem, tap_sem,
):
    start = step[0]
    whole = pl.multiple_of(start // 8 * 8, 8)
    film_copy = pltpu.make_async_copy(table.at[pl.ds(whole, 8)], film, sem)
    film_copy.start()
    block_copies = [
        pltpu.make_async_copy(ref, blocks.at[n], block_sem.at[n])
        for n, ref in enumerate((inputs, hidden))
    ]
    for copy in block_copies:
        copy.start()
    copies = weight_copies(weight, taps, tap_sem)
    for copy in copies:
        copy.start()
    order = channel_order()
    sort = lambda v: jnp.dot(v, order, preferred_element_type=F32).astype(BF)
    for copy in block_copies:
        copy.wait()
    inp_out[...] = sort(blocks[0].reshape(768, 256)).reshape(4, 12, 16, 256)
    film_copy.wait()
    line = film[pl.ds(start - whole, 1), :]
    scale, shift = 1.0 + line[:, 0:256], line[:, 256:512]
    shifted = blocks[1].reshape(768, 256).astype(F32) * scale + shift
    sigma = jax.nn.sigmoid(shifted)
    act_out[...] = sort((shifted * sigma).astype(BF))
    slope[...] = scale * sigma * (1.0 + shifted * (1.0 - sigma))
    for copy in copies:
        copy.wait()


def pad_kernel(block, row, face, outer, corner_face, corner_outer, act, out):
    near_cells, far_cells = face[0].astype(F32), outer[0].astype(F32)
    near_ends, far_ends = corner_face[0].astype(F32), corner_outer[0].astype(F32)
    pad_block(
        keep_in(out),
        lambda f, r: block[f, r],
        lambda f: row[0, f],
        lambda f: by_core(near_cells[f], far_cells[f]),
        lambda f: by_core(far_cells[f], near_cells[f]),
        lambda f: by_core(near_ends[f : f + 1], far_ends[f : f + 1]),
        lambda f: by_core(far_ends[f : f + 1], near_ends[f : f + 1]),
    )
    for f in range(4):
        for n in range(12):
            cells = act[f * 192 + n * 16 : f * 192 + n * 16 + 16, 128:256]
            out[f, 16 + n % 6, :, n // 6 * 128 : n // 6 * 128 + 128] = cells


def first_kernel(padded, slope, taps, wide, hid_out, total):
    build_shifted(put_back(wide), padded)
    conv_sum(wide, taps, total)
    hid_out[...] = (total[...] * slope[...]).astype(BF).reshape(4, 12, 16, 256)


def input_conv_kernel(
    hid, block, border, cols, after, weight, out, held, total, sem, wide, padded, near_block
):
    del after
    copies = weight_copies(weight, held, sem)
    copies.append(pltpu.make_async_copy(block, near_block, sem.at[3]))
    for copy in copies:
        copy.start()
    faces, outers = border[8].astype(F32), border[9].astype(F32)
    pad_block(
        keep_in(padded),
        lambda f, r: hid[f, r],
        lambda f: border[f],
        lambda f: by_core(cols[0, f].astype(F32), border[4 + f].astype(F32)),
        lambda f: by_core(border[4 + f].astype(F32), cols[1, f].astype(F32)),
        lambda f: by_core(faces[f : f + 1], outers[f : f + 1]),
        lambda f: by_core(outers[f : f + 1], faces[f : f + 1]),
    )
    build_shifted(put_back(wide), padded)
    for copy in copies:
        copy.wait()
    conv_sum(wide, held, total)
    grad = near_block[...].reshape(768, 256).astype(F32) + total[...]
    out[...] = grad.astype(BF).reshape(4, 12, 16, 256)


def second_own_kernel(wide, act, got, after, keep, one, two, three, pair_wide, pair_act):
    del after
    build_shifted(put_back(pair_wide), got)
    for f in range(4):
        for n in range(12):
            cells = got[f, 16 + n % 6, :, n // 6 * 128 : n // 6 * 128 + 128]
            pair_act[f * 192 + n * 16 : f * 192 + n * 16 + 16, :] = cells
    for a in range(3):
        rows = (a + 2) * 192
        for b in range(3):
            total = None
            for left, right in ((act[0:rows, 0:128], wide), (pair_act[0:rows], pair_wide)):
                window = right[2 - a : 4, 2 - b : 14 - b].reshape(rows, 768)
                part = lax.dot_general(left, window, TN, preferred_element_type=F32)
                total = part if total is None else total + part
            for d, out in enumerate((keep, one, two, three)):
                out[a * 3 + b] = total[d * 32 : d * 32 + 32].astype(out.dtype)


def second_x_kernel(got1, got2, got3, own, keep, one, two, three, held):
    y = lax.axis_index("y")

    def tap(t):
        ab, lanes = t // 3, slice(t % 3 * 256, t % 3 * 256 + 256)
        total = own[ab, :, lanes]
        for got in (got1, got2, got3):
            total = total + got[ab, :, lanes].astype(F32)
        return total

    for g in range(7):
        parts = [tap(t) if t < 27 else jnp.zeros((32, 256), F32) for t in range(4 * g, 4 * g + 4)]
        held[...] = jnp.concatenate(parts, axis=0).T.reshape(8, 4, 8, 128)
        for d, out in enumerate((keep, one, two, three)):
            out[g * 64 : g * 64 + 64] = held[:, y ^ d].reshape(64, 128).astype(out.dtype)
    for out in (one, two, three):
        out[448:592] = jnp.zeros((144, 128), BF)


def border_at(n, h):
    slot = n * 2 + h
    return slot // 4, slice(slot % 4 * 16, slot % 4 * 16 + 16)


def border_rows(n, h):
    return slice(448 + (n * 2 + h) * 16, 464 + (n * 2 + h) * 16)


def first_grad_kernel(
    hid, inp, row, face, outer, corner_face, corner_outer, after,
    own, pair, wide, padded, side,
):
    del after
    order = channel_order()
    for at, ref in ((0, row), (4, face), (8, outer), (12, corner_face), (13, corner_outer)):
        size = 4 if at < 12 else 1
        cells = jnp.dot(ref[1].reshape(size * 16, 256), order, preferred_element_type=F32)
        side[at : at + size] = cells.reshape(size, 16, 256)

    def put(f, r, which, cells):
        at = which * 128
        wide[f, r, :, at : at + 128] = cells[:, 0:128]
        wide[f, r, :, at + 384 : at + 512] = cells[:, 128:256]

    pad_block(
        keep_in(padded),
        lambda f, r: inp[f, r],
        lambda f: side[f],
        lambda f: by_core(side[4 + f], side[8 + f]),
        lambda f: by_core(side[8 + f], side[4 + f]),
        lambda f: by_core(side[12, f : f + 1], side[13, f : f + 1]),
        lambda f: by_core(side[13, f : f + 1], side[12, f : f + 1]),
    )
    build_shifted(put, padded)
    cells = border_cells(hid[...], 128)
    for n in range(8):
        for h in range(2):
            q, rows = border_at(n, h)
            pair[q, 27, rows] = cells[n * 16 : n * 16 + 16, h * 128 : h * 128 + 128]
    for a in range(3):
        rows = (a + 2) * 192
        left = hid[2 - a : 4].reshape(rows, 256)
        for b in range(3):
            window = wide[0 : a + 2, b : b + 12].reshape(rows, 768)
            grad = lax.dot_general(left, window, TN, preferred_element_type=F32)
            grad = grad.reshape(8, 4, 8, 768)
            for q in range(4):
                piece = grad[:, q].reshape(64, 768)
                for e in range(3):
                    t = (a * 3 + b) * 3 + e
                    own[q, t] = piece[:, e * 128 : e * 128 + 128]
                    pair[q, t] = piece[:, e * 128 + 384 : e * 128 + 512]


def first_sum_kernel(own, pair, after, keep, one, two, three, cols):
    del after
    y = lax.axis_index("y")
    for d, out in enumerate((keep, one, two, three)):
        q = y ^ d
        out[...] = (own[q] + pair[q, 0:27]).astype(out.dtype)
    for n in range(8):
        for h in range(2):
            q, rows = border_at(n, h)
            cols[n // 4, n % 4, :, h * 128 : h * 128 + 128] = pair[q, 27, rows].astype(BF)


def first_y_kernel(got1, got2, got3, own, hid, cols, after, keep, one, two, three):
    del after

    def tap(t):
        total = own[t]
        for got in (got1, got2, got3):
            total = total + got[t].astype(F32)
        return total

    for g in range(7):
        taps = [tap(t) if t < 27 else jnp.zeros((64, 128), F32) for t in range(4 * g, 4 * g + 4)]
        for d, out in enumerate((keep, one, two, three)):
            piece = jnp.concatenate([v[:, d * 32 : d * 32 + 32] for v in taps], axis=1)
            out[g * 64 : g * 64 + 64] = piece.astype(out.dtype)

    edge = 11 * (1 - lax.axis_index("ha"))
    faces, outers = [], []
    for f in range(4):
        hi, lo = cols[0, f].astype(F32), cols[1, f].astype(F32)
        face, outer = by_core(hi, lo), by_core(lo, hi)
        row, across = hid[f, edge], outer.astype(BF)
        for h in range(2):
            lanes = slice(h * 128, h * 128 + 128)
            one[border_rows(f, h)] = row[:, lanes]
            two[border_rows(f, h)] = across[:, lanes]
        faces.append(jnp.where(edge == 0, face[0:1], face[11:12]))
        outers.append(jnp.where(edge == 0, outer[0:1], outer[11:12]))
    rest = [jnp.zeros((8, 128), F32)]
    for out, rows, cells in ((one, slice(576, 592), faces), (three, slice(448, 464), outers)):
        halves = [c[:, 0:128] for c in cells] + [c[:, 128:256] for c in cells]
        out[rows] = jnp.concatenate(halves + rest, axis=0).astype(BF)


def last_kernel(own_two, a2, a1, a3, own_one, b2, b1, b3, out, keep, border, held):
    for f in range(4):
        for h in range(2):
            lanes = slice(h * 128, h * 128 + 128)
            border[f, :, lanes] = b1[border_rows(f, h)]
            border[4 + f, :, lanes] = b2[border_rows(f, h)]
    for n, corners in ((8, b1[576:592]), (9, b3[448:464])):
        corners = corners.astype(F32)
        for h in range(2):
            cells = corners[h * 4 : h * 4 + 4]
            cells = jnp.concatenate([cells, jnp.zeros((12, 128), F32)], axis=0)
            border[n, :, h * 128 : h * 128 + 128] = cells.astype(BF)
    for n, (own, got) in enumerate(((own_two, (a1, a2, a3)), (own_one, (b1, b2, b3)))):
        total = own[...]
        for ref in got:
            total = total + ref[0:448].astype(F32)
        held[n] = total.reshape(7, 8, 8, 128)

    def plane(z):
        return jnp.concatenate([held[n, :, z].reshape(56, 128) for n in range(2)], axis=0)

    for q in range(8):
        out[q] = plane(q).astype(BF)
    keep[...] = plane(lax.axis_index("z"))


def final_kernel(factor, got, own, after, one, two):
    del after
    z = lax.axis_index("z")
    total = own[...]
    for d in range(1, 8):
        total = total + got[(z + d) & 7].astype(F32)
    total = (total * factor).reshape(2, 7, 8, 128)
    for out, which in ((two, 0), (one, 1)):
        for t in range(27):
            out[t] = total[which, t // 4, :, t % 4 * 32 : t % 4 * 32 + 32]


def shards(activations, saved_hidden, cotangent, conv_one, conv_two, film_table, timesteps):
    inputs, hidden, block = activations[0], saved_hidden[0], cotangent[0]
    taps_one = conv_one.transpose(1, 2, 3, 0, 4).reshape(27, 256, 256)
    taps_two = conv_two.transpose(1, 2, 3, 0, 4).reshape(27, 256, 256)
    wide = near((4, 14, 16, 768), BF)
    def ring(parts, axis):
        return [send(parts[d - 1], ring_pairs(**{axis: d})) for d in (2, 1, 3)]

    *packed, held_block = call(
        pack_kernel,
        "pack_first",
        (block, inputs),
        "pp",
        [near((2, 4, 16, 256), BF)] * 3
        + [near((2, 16, 256), BF)] * 2
        + [near((4, 12, 16, 256), BF)],
    )
    ways = ((1, 0), (0, 1), (0, 3), (1, 1), (1, 3))
    sides = [send(p, block_pairs(*way)) for p, way in zip(packed, ways)]
    act, inp, slope, held_two = call(
        film_kernel,
        "film",
        (timesteps, inputs, hidden, film_table, taps_two),
        "shhhh",
        [
            near((768, 256), BF),
            near((4, 12, 16, 256), BF),
            near((768, 256), F32),
            near((27, 256, 256), BF),
        ],
        [
            pltpu.VMEM((8, 512), F32),
            pltpu.VMEM((2, 4, 12, 16, 256), BF),
            pltpu.SemaphoreType.DMA,
            pltpu.SemaphoreType.DMA((2,)),
            pltpu.SemaphoreType.DMA((3,)),
        ],
    )
    (padded,) = call(
        pad_kernel,
        "pad_cotangent",
        (held_block, *sides, act),
        "vvvvvvv",
        [near((4, 22, 16, 256), BF)],
    )
    pair_padded = send(padded, core_pairs())
    wide_cot, grad_hidden = call(
        first_kernel,
        "conv_two_back",
        (padded, slope, held_two),
        "vvv",
        [wide, near((4, 12, 16, 256), BF)],
        [pltpu.VMEM((768, 256), F32)],
    )

    own_one, pair_one = call(
        first_grad_kernel,
        "grad_one",
        (grad_hidden, inp, *sides, pair_padded),
        "vv" + "v" * 6,
        [near((4, 27, 64, 128), F32), near((4, 28, 64, 128), F32)],
        [
            pltpu.VMEM((4, 14, 16, 768), BF),
            pltpu.VMEM((4, 16, 16, 256), BF),
            pltpu.VMEM((14, 16, 256), F32),
        ],
    )
    got_pair_one = send(pair_one, core_pairs())
    own_two, *parts = call(
        second_own_kernel,
        "grad_two",
        (wide_cot, act, pair_padded, pair_one),
        "vvvv",
        [near((9, 32, 768), F32)] + [near((9, 32, 768), BF)] * 3,
        [pltpu.VMEM((4, 14, 16, 768), BF), pltpu.VMEM((768, 128), BF)],
    )
    got_two = ring(parts, "dx")
    own_one, *parts_one, cols = call(
        first_sum_kernel,
        "grad_one_sum",
        (own_one, got_pair_one, parts[0]),
        "vvv",
        [near((27, 64, 128), F32)]
        + [near((27, 64, 128), BF)] * 3
        + [near((2, 4, 16, 256), BF)],
    )
    got_one = ring(parts_one, "dy")

    own_two, *parts = call(
        second_x_kernel,
        "grad_two_x",
        (*got_two, own_two),
        "vvvv",
        [near((448, 128), F32)] + [near((592, 128), BF)] * 3,
        [pltpu.VMEM((8, 4, 8, 128), F32)],
    )
    got_two = ring(parts, "dy")
    own_one, *parts_one = call(
        first_y_kernel,
        "grad_one_y",
        (*got_one, own_one, grad_hidden, cols, parts[0]),
        "v" * 7,
        [near((448, 128), F32), near((592, 128), BF), near((576, 128), BF), near((464, 128), BF)],
    )
    got_one = ring(parts_one, "dx")

    out, own, border = call(
        last_kernel,
        "last_stage",
        (own_two, *got_two, own_one, *got_one),
        "v" * 8,
        [far((8, 112, 128), BF), near((112, 128), F32), near((10, 16, 256), BF)],
        [pltpu.VMEM((2, 7, 8, 8, 128), F32)],
    )
    planes = lax.all_to_all(out, "z", 0, 0, tiled=True)

    (grad_input,) = call(
        input_conv_kernel,
        "conv_one_back",
        (grad_hidden, block, border, cols, own, taps_one),
        "vhvvvh",
        [(jax.ShapeDtypeStruct((4, 12, 16, 256), BF), "v")],
        [
            pltpu.VMEM((27, 256, 256), BF),
            pltpu.VMEM((768, 256), F32),
            pltpu.SemaphoreType.DMA((4,)),
            pltpu.VMEM((4, 14, 16, 768), BF),
            pltpu.VMEM((4, 16, 16, 256), BF),
            pltpu.VMEM((4, 12, 16, 256), BF),
        ],
    )

    factor = float(256 * 768) ** (-0.5)
    result = jax.ShapeDtypeStruct((27, 8, 32), F32), "v"
    grad_one, grad_two = call(
        functools.partial(final_kernel, factor), "final_sum", (planes, own, grad_input), "vvh", [result, result]
    )
    shape = lambda g: g.transpose(2, 0, 1).reshape(32, 3, 3, 3, 8)
    return grad_input[None], shape(grad_one), shape(grad_two)


def solution(mesh):
    fine = Mesh(mesh.devices.reshape(SIZES), AX)
    clip = ("z", "y")
    placed = P(clip, None, "ha", ("xh", "core"), None)
    weight = P(("ha", "xh", "core"), None, None, None, clip)
    return jax.shard_map(
        shards,
        mesh=fine,
        in_specs=(placed, placed, placed, P(), P(), P(), P(clip)),
        out_specs=(placed, weight, weight),
        check_vma=False,
    )
```

```python
import functools

import jax
import jax.numpy as jnp
from jax import lax
from jax.experimental import pallas as pl
from jax.experimental.pallas import tpu as pltpu
from jax.sharding import Mesh
from jax.sharding import PartitionSpec as P

BF = jnp.bfloat16
F32 = jnp.float32
AX = ("z", "y", "ha", "xh", "core")
SIZES = (8, 4, 2, 2, 2)
VM = pl.BlockSpec(memory_space=pltpu.VMEM)
HB = pl.BlockSpec(memory_space=pl.ANY)
SM = pl.BlockSpec(memory_space=pltpu.SMEM)
NT = (((1,), (1,)), ((), ()))
TN = (((0,), (0,)), ((), ()))


def core_pairs():
    return [(i, i ^ 1) for i in range(256)]


def block_pairs(dh, dw):
    return [(i, i ^ (dh * 4 + dw)) for i in range(256)]


def ring_pairs(dx=0, dy=0):
    pairs = []
    for i in range(256):
        core, xh, ha, y, z = i % 2, i // 2 % 2, i // 4 % 2, i // 8 % 4, i // 32
        x, y = (xh * 2 + ha) ^ dx, y ^ dy
        pairs.append((i, ((z * 4 + y) * 2 + x % 2) * 4 + x // 2 * 2 + core))
    return pairs


def send(value, pairs):
    return lax.ppermute(value, AX, pairs)


def call(kernel, name, args, spaces, outs, scratch=(), limit=16):
    where = {"v": pltpu.VMEM, "p": pltpu.HBM, "h": pltpu.HBM}
    args = [
        pltpu.with_memory_space_constraint(a, where[s]) if s in where else a
        for a, s in zip(args, spaces)
    ]
    specs = {"v": VM, "p": VM, "h": HB, "s": SM}
    return pl.pallas_call(
        kernel,
        out_shape=tuple(o for o, _ in outs),
        in_specs=[specs[s] for s in spaces],
        out_specs=tuple(specs[s] for _, s in outs),
        scratch_shapes=list(scratch),
        compiler_params=pltpu.CompilerParams(vmem_limit_bytes=limit * 2**20),
        name=name,
    )(*args)


def near(shape, dtype):
    return pltpu.VMEM(shape, dtype), "v"


def far(shape, dtype):
    return pltpu.HBM(shape, dtype), "p"


def x_place():
    return lax.axis_index("xh") * 2 + lax.axis_index("ha")


def by_core(when_one, when_zero):
    return jnp.where(lax.axis_index("core") == 1, when_one, when_zero)


def border_cells(block, rows):
    edge = 11 * (1 - lax.axis_index("ha"))
    row = lax.broadcasted_iota(jnp.int32, (rows, 1), 0)
    column = jnp.where(row < 64, 15, 0) + (row >> 4 & 3) * 192 + (row & 15) * 16
    column = jnp.where((row & 15) < 12, column, -1)
    corner = jnp.where(row < 144, 15, 0) + (row & 15) * 192 + edge * 16
    corner = jnp.where((row & 15) < 4, corner, -1)
    source = jnp.where(row < 128, column, corner)
    chosen = (lax.broadcasted_iota(jnp.int32, (rows, 768), 1) == source).astype(BF)
    return jnp.dot(chosen, block.reshape(768, 256), preferred_element_type=F32)


def pack_kernel(
    one, two, weight, row, face, outer, corner_face, corner_outer, same_one, same_two, taps, sem
):
    copy = pltpu.make_async_copy(weight.at[pl.ds(0, 9)], taps, sem)
    copy.start()
    same_one[...], same_two[...] = one[...], two[...]
    edge = 11 * (1 - lax.axis_index("ha"))
    for n, block in enumerate((one, two)):
        cells = border_cells(block[...], 160)
        hi, lo = cells[0:64].reshape(4, 16, 256), cells[64:128].reshape(4, 16, 256)
        face[n], outer[n] = by_core(lo, hi).astype(BF), by_core(hi, lo).astype(BF)
        hi, lo = cells[128:144], cells[144:160]
        corner_face[n], corner_outer[n] = by_core(lo, hi).astype(BF), by_core(hi, lo).astype(BF)
        for f in range(4):
            row[n, f] = block[f, edge]
    copy.wait()


def pad_block(put, block, row, left, right, corner_left, corner_right):
    ha, wa = lax.axis_index("ha"), lax.axis_index("xh") * 2 + lax.axis_index("core")
    is_top, is_low = (ha == 1).astype(F32), (ha == 0).astype(F32)
    rest = jnp.zeros((2, 256), F32)
    for f in range(4):
        edge = row(f).astype(F32)
        put(f, 0, edge * is_top)
        put(f, 13, edge * is_low)
        for r in range(12):
            put(f, r + 1, block(f, r))
        for n, side, corner, has in (
            (14, left, corner_left, (wa > 0).astype(F32)),
            (15, right, corner_right, (wa < 3).astype(F32)),
        ):
            cells, end = side(f).astype(F32)[0:12], corner(f).astype(F32)[0:1]
            cells = jnp.concatenate([end * is_top, cells, end * is_low, rest], axis=0)
            put(f, n, cells * has)


def build_shifted(put, padded):
    col = lax.broadcasted_iota(jnp.int32, (16, 256), 0)
    for f in range(4):
        lefts, rights = padded[f, 14].astype(F32), padded[f, 15].astype(F32)
        for r in range(14):
            cells, lo, hi = padded[f, r].astype(F32), lefts[r : r + 1], rights[r : r + 1]
            put(f, r, 1, padded[f, r])
            put(f, r, 0, jnp.where(col == 0, lo, pltpu.roll(cells, 1, 0)).astype(BF))
            put(f, r, 2, jnp.where(col == 15, hi, pltpu.roll(cells, 15, 0)).astype(BF))


def keep_in(padded):
    def put(f, n, cells):
        padded[f, n] = cells.astype(BF)

    return put


def put_back(wide):
    def put(f, r, which, cells):
        wide[f, r, :, (2 - which) * 256 : (3 - which) * 256] = cells

    return put


def weight_copies(weight, held, sem, first=0):
    return [
        pltpu.make_async_copy(
            weight.at[pl.ds(a * 9, 9)], held.at[pl.ds((a - first) * 9, 9)], sem.at[a]
        )
        for a in range(first, 3)
    ]


def conv_sum(wide, tap, total):
    for a in (2, 1, 0):
        frames = a + 2
        for b in range(3):
            window = wide[2 - a : 4, 2 - b : 14 - b].reshape(frames * 192, 768)
            part = None
            for e in range(3):
                one = lax.dot_general(
                    window[:, e * 256 : (e + 1) * 256],
                    tap((a * 3 + b) * 3 + e),
                    NT,
                    preferred_element_type=F32,
                )
                part = one if part is None else part + one
            if a == 2 and b == 0:
                total[...] = part
            else:
                total[0 : frames * 192] += part


def channel_order():
    lane = lax.broadcasted_iota(jnp.int32, (256, 256), 1)
    goal, kept = x_place() ^ ((lane >> 5) & 3), lax.axis_index("core") ^ (lane >> 7)
    source = ((goal & 1) << 7) + ((goal >> 1) << 6) + (kept << 5) + (lane & 31)
    return (lax.broadcasted_iota(jnp.int32, (256, 256), 0) == source).astype(BF)


def film_kernel(
    step, inputs, hidden, table, weight, act_out, inp_out, slope, taps,
    film, block, sem, block_sem, tap_sem,
):
    start = step[0]
    whole = pl.multiple_of(start // 8 * 8, 8)
    film_copy = pltpu.make_async_copy(table.at[pl.ds(whole, 8)], film, sem)
    film_copy.start()
    block_copy = pltpu.make_async_copy(hidden, block, block_sem)
    block_copy.start()
    copies = weight_copies(weight, taps, tap_sem, 1)
    for copy in copies:
        copy.start()
    order = channel_order()
    sort = lambda v: jnp.dot(v, order, preferred_element_type=F32).astype(BF)
    inp_out[...] = sort(inputs[...].reshape(768, 256)).reshape(4, 12, 16, 256)
    block_copy.wait()
    film_copy.wait()
    line = film[pl.ds(start - whole, 1), :]
    scale, shift = 1.0 + line[:, 0:256], line[:, 256:512]
    shifted = block[...].reshape(768, 256).astype(F32) * scale + shift
    sigma = jax.nn.sigmoid(shifted)
    act_out[...] = sort((shifted * sigma).astype(BF))
    slope[...] = scale * sigma * (1.0 + shifted * (1.0 - sigma))
    for copy in copies:
        copy.wait()


def pad_kernel(block, row, face, outer, corner_face, corner_outer, act, out):
    near_cells, far_cells = face[0].astype(F32), outer[0].astype(F32)
    near_ends, far_ends = corner_face[0].astype(F32), corner_outer[0].astype(F32)
    pad_block(
        keep_in(out),
        lambda f, r: block[f, r],
        lambda f: row[0, f],
        lambda f: by_core(near_cells[f], far_cells[f]),
        lambda f: by_core(far_cells[f], near_cells[f]),
        lambda f: by_core(near_ends[f : f + 1], far_ends[f : f + 1]),
        lambda f: by_core(far_ends[f : f + 1], near_ends[f : f + 1]),
    )
    for f in range(4):
        for n in range(12):
            cells = act[f * 192 + n * 16 : f * 192 + n * 16 + 16, 128:256]
            out[f, 16 + n % 6, :, n // 6 * 128 : n // 6 * 128 + 128] = cells


def first_kernel(padded, slope, taps, more, wide, hid_out, total):
    build_shifted(put_back(wide), padded)
    conv_sum(wide, lambda t: taps[t] if t < 9 else more[t - 9], total)
    hid_out[...] = (total[...] * slope[...]).astype(BF).reshape(4, 12, 16, 256)


def input_conv_kernel(
    hid, block, border, cols, after, weight, out, held, total, sem, wide, padded, near_block
):
    del after
    copies = weight_copies(weight, held, sem)
    copies.append(pltpu.make_async_copy(block, near_block, sem.at[3]))
    for copy in copies:
        copy.start()
    faces, outers = border[8].astype(F32), border[9].astype(F32)
    pad_block(
        keep_in(padded),
        lambda f, r: hid[f, r],
        lambda f: border[f],
        lambda f: by_core(cols[0, f].astype(F32), border[4 + f].astype(F32)),
        lambda f: by_core(border[4 + f].astype(F32), cols[1, f].astype(F32)),
        lambda f: by_core(faces[f : f + 1], outers[f : f + 1]),
        lambda f: by_core(outers[f : f + 1], faces[f : f + 1]),
    )
    build_shifted(put_back(wide), padded)
    for copy in copies:
        copy.wait()
    conv_sum(wide, lambda t: held[t], total)
    grad = near_block[...].reshape(768, 256).astype(F32) + total[...]
    out[...] = grad.astype(BF).reshape(4, 12, 16, 256)


def second_own_kernel(wide, act, got, after, keep, one, two, three, pair_wide, pair_act):
    del after
    build_shifted(put_back(pair_wide), got)
    for f in range(4):
        for n in range(12):
            cells = got[f, 16 + n % 6, :, n // 6 * 128 : n // 6 * 128 + 128]
            pair_act[f * 192 + n * 16 : f * 192 + n * 16 + 16, :] = cells
    for a in range(3):
        rows = (a + 2) * 192
        for b in range(3):
            total = None
            for left, right in ((act[0:rows, 0:128], wide), (pair_act[0:rows], pair_wide)):
                window = right[2 - a : 4, 2 - b : 14 - b].reshape(rows, 768)
                part = lax.dot_general(left, window, TN, preferred_element_type=F32)
                total = part if total is None else total + part
            for d, out in enumerate((keep, one, two, three)):
                out[a * 3 + b] = total[d * 32 : d * 32 + 32].astype(out.dtype)


def second_x_kernel(got1, got2, got3, own, keep, one, two, three, held):
    y = lax.axis_index("y")

    def tap(t):
        ab, lanes = t // 3, slice(t % 3 * 256, t % 3 * 256 + 256)
        total = own[ab, :, lanes]
        for got in (got1, got2, got3):
            total = total + got[ab, :, lanes].astype(F32)
        return total

    for g in range(7):
        parts = [tap(t) if t < 27 else jnp.zeros((32, 256), F32) for t in range(4 * g, 4 * g + 4)]
        held[...] = jnp.concatenate(parts, axis=0).T.reshape(8, 4, 8, 128)
        for d, out in enumerate((keep, one, two, three)):
            out[g * 64 : g * 64 + 64] = held[:, y ^ d].reshape(64, 128).astype(out.dtype)
    for out in (one, two, three):
        out[448:592] = jnp.zeros((144, 128), BF)


def border_at(n, h):
    slot = n * 2 + h
    return slot // 4, slice(slot % 4 * 16, slot % 4 * 16 + 16)


def border_rows(n, h):
    return slice(448 + (n * 2 + h) * 16, 464 + (n * 2 + h) * 16)


def first_grad_kernel(
    hid, inp, row, face, outer, corner_face, corner_outer, after,
    own, pair, wide, padded, side,
):
    del after
    order = channel_order()
    for at, ref in ((0, row), (4, face), (8, outer), (12, corner_face), (13, corner_outer)):
        size = 4 if at < 12 else 1
        cells = jnp.dot(ref[1].reshape(size * 16, 256), order, preferred_element_type=F32)
        side[at : at + size] = cells.reshape(size, 16, 256)

    def put(f, r, which, cells):
        at = which * 128
        wide[f, r, :, at : at + 128] = cells[:, 0:128]
        wide[f, r, :, at + 384 : at + 512] = cells[:, 128:256]

    pad_block(
        keep_in(padded),
        lambda f, r: inp[f, r],
        lambda f: side[f],
        lambda f: by_core(side[4 + f], side[8 + f]),
        lambda f: by_core(side[8 + f], side[4 + f]),
        lambda f: by_core(side[12, f : f + 1], side[13, f : f + 1]),
        lambda f: by_core(side[13, f : f + 1], side[12, f : f + 1]),
    )
    build_shifted(put, padded)
    cells = border_cells(hid[...], 128)
    for n in range(8):
        for h in range(2):
            q, rows = border_at(n, h)
            pair[q, 27, rows] = cells[n * 16 : n * 16 + 16, h * 128 : h * 128 + 128]
    for a in range(3):
        rows = (a + 2) * 192
        left = hid[2 - a : 4].reshape(rows, 256)
        for b in range(3):
            window = wide[0 : a + 2, b : b + 12].reshape(rows, 768)
            grad = lax.dot_general(left, window, TN, preferred_element_type=F32)
            grad = grad.reshape(8, 4, 8, 768)
            for q in range(4):
                piece = grad[:, q].reshape(64, 768)
                for e in range(3):
                    t = (a * 3 + b) * 3 + e
                    own[q, t] = piece[:, e * 128 : e * 128 + 128]
                    pair[q, t] = piece[:, e * 128 + 384 : e * 128 + 512]


def first_sum_kernel(own, pair, after, keep, one, two, three, cols):
    del after
    y = lax.axis_index("y")
    for d, out in enumerate((keep, one, two, three)):
        q = y ^ d
        out[...] = (own[q] + pair[q, 0:27]).astype(out.dtype)
    for n in range(8):
        for h in range(2):
            q, rows = border_at(n, h)
            cols[n // 4, n % 4, :, h * 128 : h * 128 + 128] = pair[q, 27, rows].astype(BF)


def first_y_kernel(got1, got2, got3, own, hid, cols, after, keep, one, two, three):
    del after

    def tap(t):
        total = own[t]
        for got in (got1, got2, got3):
            total = total + got[t].astype(F32)
        return total

    for g in range(7):
        taps = [tap(t) if t < 27 else jnp.zeros((64, 128), F32) for t in range(4 * g, 4 * g + 4)]
        for d, out in enumerate((keep, one, two, three)):
            piece = jnp.concatenate([v[:, d * 32 : d * 32 + 32] for v in taps], axis=1)
            out[g * 64 : g * 64 + 64] = piece.astype(out.dtype)

    edge = 11 * (1 - lax.axis_index("ha"))
    faces, outers = [], []
    for f in range(4):
        hi, lo = cols[0, f].astype(F32), cols[1, f].astype(F32)
        face, outer = by_core(hi, lo), by_core(lo, hi)
        row, across = hid[f, edge], outer.astype(BF)
        for h in range(2):
            lanes = slice(h * 128, h * 128 + 128)
            one[border_rows(f, h)] = row[:, lanes]
            two[border_rows(f, h)] = across[:, lanes]
        faces.append(jnp.where(edge == 0, face[0:1], face[11:12]))
        outers.append(jnp.where(edge == 0, outer[0:1], outer[11:12]))
    rest = [jnp.zeros((8, 128), F32)]
    for out, rows, cells in ((one, slice(576, 592), faces), (three, slice(448, 464), outers)):
        halves = [c[:, 0:128] for c in cells] + [c[:, 128:256] for c in cells]
        out[rows] = jnp.concatenate(halves + rest, axis=0).astype(BF)


def last_kernel(own_two, a2, a1, a3, own_one, b2, b1, b3, out, keep, border, held):
    for f in range(4):
        for h in range(2):
            lanes = slice(h * 128, h * 128 + 128)
            border[f, :, lanes] = b1[border_rows(f, h)]
            border[4 + f, :, lanes] = b2[border_rows(f, h)]
    for n, corners in ((8, b1[576:592]), (9, b3[448:464])):
        corners = corners.astype(F32)
        for h in range(2):
            cells = corners[h * 4 : h * 4 + 4]
            cells = jnp.concatenate([cells, jnp.zeros((12, 128), F32)], axis=0)
            border[n, :, h * 128 : h * 128 + 128] = cells.astype(BF)
    for n, (own, got) in enumerate(((own_two, (a1, a2, a3)), (own_one, (b1, b2, b3)))):
        total = own[...]
        for ref in got:
            total = total + ref[0:448].astype(F32)
        held[n] = total.reshape(7, 8, 8, 128)

    def plane(z):
        return jnp.concatenate([held[n, :, z].reshape(56, 128) for n in range(2)], axis=0)

    for q in range(8):
        out[q] = plane(q).astype(BF)
    keep[...] = plane(lax.axis_index("z"))


def final_kernel(factor, got, own, after, one, two):
    del after
    z = lax.axis_index("z")
    total = own[...]
    for d in range(1, 8):
        total = total + got[(z + d) & 7].astype(F32)
    total = (total * factor).reshape(2, 7, 8, 128)
    for out, which in ((two, 0), (one, 1)):
        for t in range(27):
            out[t] = total[which, t // 4, :, t % 4 * 32 : t % 4 * 32 + 32]


def shards(activations, saved_hidden, cotangent, conv_one, conv_two, film_table, timesteps):
    inputs, hidden, block = activations[0], saved_hidden[0], cotangent[0]
    taps_one = conv_one.transpose(1, 2, 3, 0, 4).reshape(27, 256, 256)
    taps_two = conv_two.transpose(1, 2, 3, 0, 4).reshape(27, 256, 256)
    wide = near((4, 14, 16, 768), BF)
    def ring(parts, axis):
        return [send(parts[d - 1], ring_pairs(**{axis: d})) for d in (2, 1, 3)]

    *packed, held_block, held_inputs, held_two = call(
        pack_kernel,
        "pack_first",
        (block, inputs, taps_two),
        "pph",
        [near((2, 4, 16, 256), BF)] * 3
        + [near((2, 16, 256), BF)] * 2
        + [near((4, 12, 16, 256), BF)] * 2
        + [near((9, 256, 256), BF)],
        [pltpu.SemaphoreType.DMA],
    )
    ways = ((1, 0), (0, 1), (0, 3), (1, 1), (1, 3))
    sides = [send(p, block_pairs(*way)) for p, way in zip(packed, ways)]
    act, inp, slope, more_two = call(
        film_kernel,
        "film",
        (timesteps, held_inputs, hidden, film_table, taps_two),
        "svhhh",
        [
            near((768, 256), BF),
            near((4, 12, 16, 256), BF),
            near((768, 256), F32),
            near((18, 256, 256), BF),
        ],
        [
            pltpu.VMEM((8, 512), F32),
            pltpu.VMEM((4, 12, 16, 256), BF),
            pltpu.SemaphoreType.DMA,
            pltpu.SemaphoreType.DMA,
            pltpu.SemaphoreType.DMA((3,)),
        ],
    )
    (padded,) = call(
        pad_kernel,
        "pad_cotangent",
        (held_block, *sides, act),
        "vvvvvvv",
        [near((4, 22, 16, 256), BF)],
    )
    pair_padded = send(padded, core_pairs())
    wide_cot, grad_hidden = call(
        first_kernel,
        "conv_two_back",
        (padded, slope, held_two, more_two),
        "vvvv",
        [wide, near((4, 12, 16, 256), BF)],
        [pltpu.VMEM((768, 256), F32)],
    )

    own_one, pair_one = call(
        first_grad_kernel,
        "grad_one",
        (grad_hidden, inp, *sides, pair_padded),
        "vv" + "v" * 6,
        [near((4, 27, 64, 128), F32), near((4, 28, 64, 128), F32)],
        [
            pltpu.VMEM((4, 14, 16, 768), BF),
            pltpu.VMEM((4, 16, 16, 256), BF),
            pltpu.VMEM((14, 16, 256), F32),
        ],
    )
    got_pair_one = send(pair_one, core_pairs())
    own_two, *parts = call(
        second_own_kernel,
        "grad_two",
        (wide_cot, act, pair_padded, pair_one),
        "vvvv",
        [near((9, 32, 768), F32)] + [near((9, 32, 768), BF)] * 3,
        [pltpu.VMEM((4, 14, 16, 768), BF), pltpu.VMEM((768, 128), BF)],
    )
    got_two = ring(parts, "dx")
    own_one, *parts_one, cols = call(
        first_sum_kernel,
        "grad_one_sum",
        (own_one, got_pair_one, parts[0]),
        "vvv",
        [near((27, 64, 128), F32)]
        + [near((27, 64, 128), BF)] * 3
        + [near((2, 4, 16, 256), BF)],
    )
    got_one = ring(parts_one, "dy")

    own_two, *parts = call(
        second_x_kernel,
        "grad_two_x",
        (*got_two, own_two),
        "vvvv",
        [near((448, 128), F32)] + [near((592, 128), BF)] * 3,
        [pltpu.VMEM((8, 4, 8, 128), F32)],
    )
    got_two = ring(parts, "dy")
    own_one, *parts_one = call(
        first_y_kernel,
        "grad_one_y",
        (*got_one, own_one, grad_hidden, cols, parts[0]),
        "v" * 7,
        [near((448, 128), F32), near((592, 128), BF), near((576, 128), BF), near((464, 128), BF)],
    )
    got_one = ring(parts_one, "dx")

    out, own, border = call(
        last_kernel,
        "last_stage",
        (own_two, *got_two, own_one, *got_one),
        "v" * 8,
        [far((8, 112, 128), BF), near((112, 128), F32), near((10, 16, 256), BF)],
        [pltpu.VMEM((2, 7, 8, 8, 128), F32)],
    )
    planes = lax.all_to_all(out, "z", 0, 0, tiled=True)

    (grad_input,) = call(
        input_conv_kernel,
        "conv_one_back",
        (grad_hidden, block, border, cols, own, taps_one),
        "vhvvvh",
        [(jax.ShapeDtypeStruct((4, 12, 16, 256), BF), "v")],
        [
            pltpu.VMEM((27, 256, 256), BF),
            pltpu.VMEM((768, 256), F32),
            pltpu.SemaphoreType.DMA((4,)),
            pltpu.VMEM((4, 14, 16, 768), BF),
            pltpu.VMEM((4, 16, 16, 256), BF),
            pltpu.VMEM((4, 12, 16, 256), BF),
        ],
    )

    factor = float(256 * 768) ** (-0.5)
    result = jax.ShapeDtypeStruct((27, 8, 32), F32), "v"
    grad_one, grad_two = call(
        functools.partial(final_kernel, factor), "final_sum", (planes, own, grad_input), "vvh", [result, result]
    )
    shape = lambda g: g.transpose(2, 0, 1).reshape(32, 3, 3, 3, 8)
    return grad_input[None], shape(grad_one), shape(grad_two)


def solution(mesh):
    fine = Mesh(mesh.devices.reshape(SIZES), AX)
    clip = ("z", "y")
    placed = P(clip, None, "ha", ("xh", "core"), None)
    weight = P(("ha", "xh", "core"), None, None, None, clip)
    return jax.shard_map(
        shards,
        mesh=fine,
        in_specs=(placed, placed, placed, P(), P(), P(), P(clip)),
        out_specs=(placed, weight, weight),
        check_vma=False,
    )
```

```python
import functools

import jax
import jax.numpy as jnp
from jax import lax
from jax.experimental import pallas as pl
from jax.experimental.pallas import tpu as pltpu
from jax.sharding import Mesh
from jax.sharding import PartitionSpec as P

BF = jnp.bfloat16
F32 = jnp.float32
AX = ("z", "y", "ha", "xh", "core")
SIZES = (8, 4, 2, 2, 2)
VM = pl.BlockSpec(memory_space=pltpu.VMEM)
HB = pl.BlockSpec(memory_space=pl.ANY)
SM = pl.BlockSpec(memory_space=pltpu.SMEM)
NT = (((1,), (1,)), ((), ()))
TN = (((0,), (0,)), ((), ()))


def core_pairs():
    return [(i, i ^ 1) for i in range(256)]


def block_pairs(dh, dw):
    return [(i, i ^ (dh * 4 + dw)) for i in range(256)]


def ring_pairs(dx=0, dy=0):
    pairs = []
    for i in range(256):
        core, xh, ha, y, z = i % 2, i // 2 % 2, i // 4 % 2, i // 8 % 4, i // 32
        x, y = (xh * 2 + ha) ^ dx, y ^ dy
        pairs.append((i, ((z * 4 + y) * 2 + x % 2) * 4 + x // 2 * 2 + core))
    return pairs


def send(value, pairs):
    return lax.ppermute(value, AX, pairs)


def call(kernel, name, args, spaces, outs, scratch=(), limit=16):
    where = {"v": pltpu.VMEM, "p": pltpu.HBM, "h": pltpu.HBM}
    args = [
        pltpu.with_memory_space_constraint(a, where[s]) if s in where else a
        for a, s in zip(args, spaces)
    ]
    specs = {"v": VM, "p": VM, "h": HB, "s": SM}
    return pl.pallas_call(
        kernel,
        out_shape=tuple(o for o, _ in outs),
        in_specs=[specs[s] for s in spaces],
        out_specs=tuple(specs[s] for _, s in outs),
        scratch_shapes=list(scratch),
        compiler_params=pltpu.CompilerParams(vmem_limit_bytes=limit * 2**20),
        name=name,
    )(*args)


def near(shape, dtype):
    return pltpu.VMEM(shape, dtype), "v"


def far(shape, dtype):
    return pltpu.HBM(shape, dtype), "p"


def x_place():
    return lax.axis_index("xh") * 2 + lax.axis_index("ha")


def by_core(when_one, when_zero):
    return jnp.where(lax.axis_index("core") == 1, when_one, when_zero)


def border_cells(block, rows):
    edge = 11 * (1 - lax.axis_index("ha"))
    row = lax.broadcasted_iota(jnp.int32, (rows, 1), 0)
    column = jnp.where(row < 64, 15, 0) + (row >> 4 & 3) * 192 + (row & 15) * 16
    column = jnp.where((row & 15) < 12, column, -1)
    corner = jnp.where(row < 144, 15, 0) + (row & 15) * 192 + edge * 16
    corner = jnp.where((row & 15) < 4, corner, -1)
    source = jnp.where(row < 128, column, corner)
    chosen = (lax.broadcasted_iota(jnp.int32, (rows, 768), 1) == source).astype(BF)
    return jnp.dot(chosen, block.reshape(768, 256), preferred_element_type=F32)


def pack_kernel(one, two, row, face, outer, corner_face, corner_outer, same_one, same_two):
    same_one[...], same_two[...] = one[...], two[...]
    edge = 11 * (1 - lax.axis_index("ha"))
    for n, block in enumerate((one, two)):
        cells = border_cells(block[...], 160)
        hi, lo = cells[0:64].reshape(4, 16, 256), cells[64:128].reshape(4, 16, 256)
        face[n], outer[n] = by_core(lo, hi).astype(BF), by_core(hi, lo).astype(BF)
        hi, lo = cells[128:144], cells[144:160]
        corner_face[n], corner_outer[n] = by_core(lo, hi).astype(BF), by_core(hi, lo).astype(BF)
        for f in range(4):
            row[n, f] = block[f, edge]


def pad_block(put, block, row, left, right, corner_left, corner_right):
    ha, wa = lax.axis_index("ha"), lax.axis_index("xh") * 2 + lax.axis_index("core")
    is_top, is_low = (ha == 1).astype(F32), (ha == 0).astype(F32)
    rest = jnp.zeros((2, 256), F32)
    for f in range(4):
        edge = row(f).astype(F32)
        put(f, 0, edge * is_top)
        put(f, 13, edge * is_low)
        for r in range(12):
            put(f, r + 1, block(f, r))
        for n, side, corner, has in (
            (14, left, corner_left, (wa > 0).astype(F32)),
            (15, right, corner_right, (wa < 3).astype(F32)),
        ):
            cells, end = side(f).astype(F32)[0:12], corner(f).astype(F32)[0:1]
            cells = jnp.concatenate([end * is_top, cells, end * is_low, rest], axis=0)
            put(f, n, cells * has)


def build_shifted(put, padded):
    col = lax.broadcasted_iota(jnp.int32, (16, 256), 0)
    for f in range(4):
        lefts, rights = padded[f, 14].astype(F32), padded[f, 15].astype(F32)
        for r in range(14):
            cells, lo, hi = padded[f, r].astype(F32), lefts[r : r + 1], rights[r : r + 1]
            put(f, r, 1, padded[f, r])
            put(f, r, 0, jnp.where(col == 0, lo, pltpu.roll(cells, 1, 0)).astype(BF))
            put(f, r, 2, jnp.where(col == 15, hi, pltpu.roll(cells, 15, 0)).astype(BF))


def keep_in(padded):
    def put(f, n, cells):
        padded[f, n] = cells.astype(BF)

    return put


def put_back(wide):
    def put(f, r, which, cells):
        wide[f, r, :, (2 - which) * 256 : (3 - which) * 256] = cells

    return put


def weight_copies(weight, held, sem):
    return [
        pltpu.make_async_copy(weight.at[pl.ds(a * 9, 9)], held.at[pl.ds(a * 9, 9)], sem.at[a])
        for a in range(3)
    ]


def conv_sum(wide, tap, total):
    for a in (2, 1, 0):
        frames = a + 2
        for b in range(3):
            window = wide[2 - a : 4, 2 - b : 14 - b].reshape(frames * 192, 768)
            part = None
            for e in range(3):
                one = lax.dot_general(
                    window[:, e * 256 : (e + 1) * 256],
                    tap((a * 3 + b) * 3 + e),
                    NT,
                    preferred_element_type=F32,
                )
                part = one if part is None else part + one
            if a == 2 and b == 0:
                total[...] = part
            else:
                total[0 : frames * 192] += part


def channel_order():
    lane = lax.broadcasted_iota(jnp.int32, (256, 256), 1)
    goal, kept = x_place() ^ ((lane >> 5) & 3), lax.axis_index("core") ^ (lane >> 7)
    source = ((goal & 1) << 7) + ((goal >> 1) << 6) + (kept << 5) + (lane & 31)
    return (lax.broadcasted_iota(jnp.int32, (256, 256), 0) == source).astype(BF)


def film_kernel(
    step, inputs, hidden, table, weight, act_out, inp_out, slope, taps,
    film, block, sem, block_sem, tap_sem,
):
    start = step[0]
    whole = pl.multiple_of(start // 8 * 8, 8)
    film_copy = pltpu.make_async_copy(table.at[pl.ds(whole, 8)], film, sem)
    film_copy.start()
    block_copy = pltpu.make_async_copy(hidden, block, block_sem)
    block_copy.start()
    copies = weight_copies(weight, taps, tap_sem)
    for copy in copies:
        copy.start()
    order = channel_order()
    sort = lambda v: jnp.dot(v, order, preferred_element_type=F32).astype(BF)
    inp_out[...] = sort(inputs[...].reshape(768, 256)).reshape(4, 12, 16, 256)
    block_copy.wait()
    film_copy.wait()
    line = film[pl.ds(start - whole, 1), :]
    scale, shift = 1.0 + line[:, 0:256], line[:, 256:512]
    shifted = block[...].reshape(768, 256).astype(F32) * scale + shift
    sigma = jax.nn.sigmoid(shifted)
    act_out[...] = sort((shifted * sigma).astype(BF))
    slope[...] = scale * sigma * (1.0 + shifted * (1.0 - sigma))
    for copy in copies:
        copy.wait()


def pad_kernel(block, row, face, outer, corner_face, corner_outer, act, out):
    near_cells, far_cells = face[0].astype(F32), outer[0].astype(F32)
    near_ends, far_ends = corner_face[0].astype(F32), corner_outer[0].astype(F32)
    pad_block(
        keep_in(out),
        lambda f, r: block[f, r],
        lambda f: row[0, f],
        lambda f: by_core(near_cells[f], far_cells[f]),
        lambda f: by_core(far_cells[f], near_cells[f]),
        lambda f: by_core(near_ends[f : f + 1], far_ends[f : f + 1]),
        lambda f: by_core(far_ends[f : f + 1], near_ends[f : f + 1]),
    )
    for f in range(4):
        for n in range(12):
            cells = act[f * 192 + n * 16 : f * 192 + n * 16 + 16, 128:256]
            out[f, 16 + n % 6, :, n // 6 * 128 : n // 6 * 128 + 128] = cells


def first_kernel(padded, slope, taps, wide, hid_out, total):
    build_shifted(put_back(wide), padded)
    conv_sum(wide, lambda t: taps[t], total)
    hid_out[...] = (total[...] * slope[...]).astype(BF).reshape(4, 12, 16, 256)


def input_conv_kernel(
    hid, block, border, cols, after, weight, out, held, total, sem, wide, padded, near_block
):
    del after
    copies = weight_copies(weight, held, sem)
    copies.append(pltpu.make_async_copy(block, near_block, sem.at[3]))
    for copy in copies:
        copy.start()
    faces, outers = border[8].astype(F32), border[9].astype(F32)
    pad_block(
        keep_in(padded),
        lambda f, r: hid[f, r],
        lambda f: border[f],
        lambda f: by_core(cols[0, f].astype(F32), border[4 + f].astype(F32)),
        lambda f: by_core(border[4 + f].astype(F32), cols[1, f].astype(F32)),
        lambda f: by_core(faces[f : f + 1], outers[f : f + 1]),
        lambda f: by_core(outers[f : f + 1], faces[f : f + 1]),
    )
    build_shifted(put_back(wide), padded)
    for copy in copies:
        copy.wait()
    conv_sum(wide, lambda t: held[t], total)
    grad = near_block[...].reshape(768, 256).astype(F32) + total[...]
    out[...] = grad.astype(BF).reshape(4, 12, 16, 256)


def second_own_kernel(wide, act, got, after, keep, one, two, three, pair_wide, pair_act):
    del after
    build_shifted(put_back(pair_wide), got)
    for f in range(4):
        for n in range(12):
            cells = got[f, 16 + n % 6, :, n // 6 * 128 : n // 6 * 128 + 128]
            pair_act[f * 192 + n * 16 : f * 192 + n * 16 + 16, :] = cells
    for a in range(3):
        rows = (a + 2) * 192
        for b in range(3):
            total = None
            for left, right in ((act[0:rows, 0:128], wide), (pair_act[0:rows], pair_wide)):
                window = right[2 - a : 4, 2 - b : 14 - b].reshape(rows, 768)
                part = lax.dot_general(left, window, TN, preferred_element_type=F32)
                total = part if total is None else total + part
            for d, out in enumerate((keep, one, two, three)):
                out[a * 3 + b] = total[d * 32 : d * 32 + 32].astype(out.dtype)


def second_x_kernel(got1, got2, got3, own, keep, one, two, three, held):
    y = lax.axis_index("y")

    def tap(t):
        ab, lanes = t // 3, slice(t % 3 * 256, t % 3 * 256 + 256)
        total = own[ab, :, lanes]
        for got in (got1, got2, got3):
            total = total + got[ab, :, lanes].astype(F32)
        return total

    for g in range(7):
        parts = [tap(t) if t < 27 else jnp.zeros((32, 256), F32) for t in range(4 * g, 4 * g + 4)]
        held[...] = jnp.concatenate(parts, axis=0).T.reshape(8, 4, 8, 128)
        for d, out in enumerate((keep, one, two, three)):
            out[g * 64 : g * 64 + 64] = held[:, y ^ d].reshape(64, 128).astype(out.dtype)
    for out in (one, two, three):
        out[448:592] = jnp.zeros((144, 128), BF)


def border_at(n, h):
    slot = n * 2 + h
    return slot // 4, slice(slot % 4 * 16, slot % 4 * 16 + 16)


def border_rows(n, h):
    return slice(448 + (n * 2 + h) * 16, 464 + (n * 2 + h) * 16)


def first_grad_kernel(
    hid, inp, row, face, outer, corner_face, corner_outer, after,
    own, pair, wide, padded, side,
):
    del after
    order = channel_order()
    for at, ref in ((0, row), (4, face), (8, outer), (12, corner_face), (13, corner_outer)):
        size = 4 if at < 12 else 1
        cells = jnp.dot(ref[1].reshape(size * 16, 256), order, preferred_element_type=F32)
        side[at : at + size] = cells.reshape(size, 16, 256)

    def put(f, r, which, cells):
        at = which * 128
        wide[f, r, :, at : at + 128] = cells[:, 0:128]
        wide[f, r, :, at + 384 : at + 512] = cells[:, 128:256]

    pad_block(
        keep_in(padded),
        lambda f, r: inp[f, r],
        lambda f: side[f],
        lambda f: by_core(side[4 + f], side[8 + f]),
        lambda f: by_core(side[8 + f], side[4 + f]),
        lambda f: by_core(side[12, f : f + 1], side[13, f : f + 1]),
        lambda f: by_core(side[13, f : f + 1], side[12, f : f + 1]),
    )
    build_shifted(put, padded)
    cells = border_cells(hid[...], 128)
    for n in range(8):
        for h in range(2):
            q, rows = border_at(n, h)
            pair[q, 27, rows] = cells[n * 16 : n * 16 + 16, h * 128 : h * 128 + 128]
    for a in range(3):
        rows = (a + 2) * 192
        left = hid[2 - a : 4].reshape(rows, 256)
        for b in range(3):
            window = wide[0 : a + 2, b : b + 12].reshape(rows, 768)
            grad = lax.dot_general(left, window, TN, preferred_element_type=F32)
            grad = grad.reshape(8, 4, 8, 768)
            for q in range(4):
                piece = grad[:, q].reshape(64, 768)
                for e in range(3):
                    t = (a * 3 + b) * 3 + e
                    own[q, t] = piece[:, e * 128 : e * 128 + 128]
                    pair[q, t] = piece[:, e * 128 + 384 : e * 128 + 512]


def first_sum_kernel(own, pair, after, keep, one, two, three, cols):
    del after
    y = lax.axis_index("y")
    for d, out in enumerate((keep, one, two, three)):
        q = y ^ d
        out[...] = (own[q] + pair[q, 0:27]).astype(out.dtype)
    for n in range(8):
        for h in range(2):
            q, rows = border_at(n, h)
            cols[n // 4, n % 4, :, h * 128 : h * 128 + 128] = pair[q, 27, rows].astype(BF)


def first_y_kernel(got1, got2, got3, own, hid, cols, after, keep, one, two, three):
    del after

    def tap(t):
        total = own[t]
        for got in (got1, got2, got3):
            total = total + got[t].astype(F32)
        return total

    for g in range(7):
        taps = [tap(t) if t < 27 else jnp.zeros((64, 128), F32) for t in range(4 * g, 4 * g + 4)]
        for d, out in enumerate((keep, one, two, three)):
            piece = jnp.concatenate([v[:, d * 32 : d * 32 + 32] for v in taps], axis=1)
            out[g * 64 : g * 64 + 64] = piece.astype(out.dtype)

    edge = 11 * (1 - lax.axis_index("ha"))
    faces, outers = [], []
    for f in range(4):
        hi, lo = cols[0, f].astype(F32), cols[1, f].astype(F32)
        face, outer = by_core(hi, lo), by_core(lo, hi)
        row, across = hid[f, edge], outer.astype(BF)
        for h in range(2):
            lanes = slice(h * 128, h * 128 + 128)
            one[border_rows(f, h)] = row[:, lanes]
            two[border_rows(f, h)] = across[:, lanes]
        faces.append(jnp.where(edge == 0, face[0:1], face[11:12]))
        outers.append(jnp.where(edge == 0, outer[0:1], outer[11:12]))
    rest = [jnp.zeros((8, 128), F32)]
    for out, rows, cells in ((one, slice(576, 592), faces), (three, slice(448, 464), outers)):
        halves = [c[:, 0:128] for c in cells] + [c[:, 128:256] for c in cells]
        out[rows] = jnp.concatenate(halves + rest, axis=0).astype(BF)


def last_kernel(own_two, a1, a2, a3, own_one, b1, b2, b3, out, keep, border, held):
    for f in range(4):
        for h in range(2):
            lanes = slice(h * 128, h * 128 + 128)
            border[f, :, lanes] = b1[border_rows(f, h)]
            border[4 + f, :, lanes] = b2[border_rows(f, h)]
    for n, corners in ((8, b1[576:592]), (9, b3[448:464])):
        corners = corners.astype(F32)
        for h in range(2):
            cells = corners[h * 4 : h * 4 + 4]
            cells = jnp.concatenate([cells, jnp.zeros((12, 128), F32)], axis=0)
            border[n, :, h * 128 : h * 128 + 128] = cells.astype(BF)
    for n, (own, got) in enumerate(((own_two, (a1, a2, a3)), (own_one, (b1, b2, b3)))):
        total = own[...]
        for ref in got:
            total = total + ref[0:448].astype(F32)
        held[n] = total.reshape(7, 8, 8, 128)

    def plane(z):
        return jnp.concatenate([held[n, :, z].reshape(56, 128) for n in range(2)], axis=0)

    for q in range(8):
        out[q] = plane(q).astype(BF)
    keep[...] = plane(lax.axis_index("z"))


def final_kernel(factor, got, own, after, one, two):
    del after
    z = lax.axis_index("z")
    total = own[...]
    for d in range(1, 8):
        total = total + got[(z + d) & 7].astype(F32)
    total = (total * factor).reshape(2, 7, 8, 128)
    for out, which in ((two, 0), (one, 1)):
        for t in range(27):
            out[t] = total[which, t // 4, :, t % 4 * 32 : t % 4 * 32 + 32]


def shards(activations, saved_hidden, cotangent, conv_one, conv_two, film_table, timesteps):
    inputs, hidden, block = activations[0], saved_hidden[0], cotangent[0]
    taps_one = conv_one.transpose(1, 2, 3, 0, 4).reshape(27, 256, 256)
    taps_two = conv_two.transpose(1, 2, 3, 0, 4).reshape(27, 256, 256)
    wide = near((4, 14, 16, 768), BF)
    def ring(parts, axis):
        return [send(parts[d - 1], ring_pairs(**{axis: d})) for d in (1, 2, 3)]

    *packed, held_block, held_inputs = call(
        pack_kernel,
        "pack_first",
        (block, inputs),
        "pp",
        [near((2, 4, 16, 256), BF)] * 3
        + [near((2, 16, 256), BF)] * 2
        + [near((4, 12, 16, 256), BF)] * 2,
    )
    ways = ((1, 0), (0, 1), (0, 3), (1, 1), (1, 3))
    sides = [send(p, block_pairs(*way)) for p, way in zip(packed, ways)]
    act, inp, slope, held_two = call(
        film_kernel,
        "film",
        (timesteps, held_inputs, hidden, film_table, taps_two),
        "svhhh",
        [
            near((768, 256), BF),
            near((4, 12, 16, 256), BF),
            near((768, 256), F32),
            near((27, 256, 256), BF),
        ],
        [
            pltpu.VMEM((8, 512), F32),
            pltpu.VMEM((4, 12, 16, 256), BF),
            pltpu.SemaphoreType.DMA,
            pltpu.SemaphoreType.DMA,
            pltpu.SemaphoreType.DMA((3,)),
        ],
    )
    (padded,) = call(
        pad_kernel,
        "pad_cotangent",
        (held_block, *sides, act),
        "vvvvvvv",
        [near((4, 22, 16, 256), BF)],
    )
    pair_padded = send(padded, core_pairs())
    wide_cot, grad_hidden = call(
        first_kernel,
        "conv_two_back",
        (padded, slope, held_two),
        "vvv",
        [wide, near((4, 12, 16, 256), BF)],
        [pltpu.VMEM((768, 256), F32)],
    )

    own_one, pair_one = call(
        first_grad_kernel,
        "grad_one",
        (grad_hidden, inp, *sides, pair_padded),
        "vv" + "v" * 6,
        [near((4, 27, 64, 128), F32), near((4, 28, 64, 128), F32)],
        [
            pltpu.VMEM((4, 14, 16, 768), BF),
            pltpu.VMEM((4, 16, 16, 256), BF),
            pltpu.VMEM((14, 16, 256), F32),
        ],
    )
    got_pair_one = send(pair_one, core_pairs())
    own_two, *parts = call(
        second_own_kernel,
        "grad_two",
        (wide_cot, act, pair_padded, pair_one),
        "vvvv",
        [near((9, 32, 768), F32)] + [near((9, 32, 768), BF)] * 3,
        [pltpu.VMEM((4, 14, 16, 768), BF), pltpu.VMEM((768, 128), BF)],
    )
    got_two = ring(parts, "dx")
    own_one, *parts_one, cols = call(
        first_sum_kernel,
        "grad_one_sum",
        (own_one, got_pair_one, parts[0]),
        "vvv",
        [near((27, 64, 128), F32)]
        + [near((27, 64, 128), BF)] * 3
        + [near((2, 4, 16, 256), BF)],
    )
    got_one = ring(parts_one, "dy")

    own_two, *parts = call(
        second_x_kernel,
        "grad_two_x",
        (*got_two, own_two),
        "vvvv",
        [near((448, 128), F32)] + [near((592, 128), BF)] * 3,
        [pltpu.VMEM((8, 4, 8, 128), F32)],
    )
    got_two = ring(parts, "dy")
    own_one, *parts_one = call(
        first_y_kernel,
        "grad_one_y",
        (*got_one, own_one, grad_hidden, cols, parts[0]),
        "v" * 7,
        [near((448, 128), F32), near((592, 128), BF), near((576, 128), BF), near((464, 128), BF)],
    )
    got_one = ring(parts_one, "dx")

    out, own, border = call(
        last_kernel,
        "last_stage",
        (own_two, *got_two, own_one, *got_one),
        "v" * 8,
        [far((8, 112, 128), BF), near((112, 128), F32), near((10, 16, 256), BF)],
        [pltpu.VMEM((2, 7, 8, 8, 128), F32)],
    )
    planes = lax.all_to_all(out, "z", 0, 0, tiled=True)

    (grad_input,) = call(
        input_conv_kernel,
        "conv_one_back",
        (grad_hidden, block, border, cols, own, taps_one),
        "vhvvvh",
        [(jax.ShapeDtypeStruct((4, 12, 16, 256), BF), "v")],
        [
            pltpu.VMEM((27, 256, 256), BF),
            pltpu.VMEM((768, 256), F32),
            pltpu.SemaphoreType.DMA((4,)),
            pltpu.VMEM((4, 14, 16, 768), BF),
            pltpu.VMEM((4, 16, 16, 256), BF),
            pltpu.VMEM((4, 12, 16, 256), BF),
        ],
    )

    factor = float(256 * 768) ** (-0.5)
    result = jax.ShapeDtypeStruct((27, 8, 32), F32), "v"
    grad_one, grad_two = call(
        functools.partial(final_kernel, factor), "final_sum", (planes, own, grad_input), "vvh", [result, result]
    )
    shape = lambda g: g.transpose(2, 0, 1).reshape(32, 3, 3, 3, 8)
    return grad_input[None], shape(grad_one), shape(grad_two)


def solution(mesh):
    fine = Mesh(mesh.devices.reshape(SIZES), AX)
    clip = ("z", "y")
    placed = P(clip, None, "ha", ("xh", "core"), None)
    weight = P(("ha", "xh", "core"), None, None, None, clip)
    return jax.shard_map(
        shards,
        mesh=fine,
        in_specs=(placed, placed, placed, P(), P(), P(), P(clip)),
        out_specs=(placed, weight, weight),
        check_vma=False,
    )
```

```python
import functools

import jax
import jax.numpy as jnp
from jax import lax
from jax.experimental import pallas as pl
from jax.experimental.pallas import tpu as pltpu
from jax.sharding import Mesh
from jax.sharding import PartitionSpec as P

BF = jnp.bfloat16
F32 = jnp.float32
AX = ("z", "y", "ha", "xh", "core")
SIZES = (8, 4, 2, 2, 2)
VM = pl.BlockSpec(memory_space=pltpu.VMEM)
HB = pl.BlockSpec(memory_space=pl.ANY)
SM = pl.BlockSpec(memory_space=pltpu.SMEM)
NT = (((1,), (1,)), ((), ()))
TN = (((0,), (0,)), ((), ()))


def core_pairs():
    return [(i, i ^ 1) for i in range(256)]


def block_pairs(dh, dw):
    return [(i, i ^ (dh * 4 + dw)) for i in range(256)]


def ring_pairs(dx=0, dy=0):
    pairs = []
    for i in range(256):
        core, xh, ha, y, z = i % 2, i // 2 % 2, i // 4 % 2, i // 8 % 4, i // 32
        x, y = (xh * 2 + ha) ^ dx, y ^ dy
        pairs.append((i, ((z * 4 + y) * 2 + x % 2) * 4 + x // 2 * 2 + core))
    return pairs


def send(value, pairs):
    return lax.ppermute(value, AX, pairs)


def call(kernel, name, args, spaces, outs, scratch=(), limit=16):
    where = {"v": pltpu.VMEM, "p": pltpu.HBM, "h": pltpu.HBM}
    args = [
        pltpu.with_memory_space_constraint(a, where[s]) if s in where else a
        for a, s in zip(args, spaces)
    ]
    specs = {"v": VM, "p": VM, "h": HB, "s": SM}
    return pl.pallas_call(
        kernel,
        out_shape=tuple(o for o, _ in outs),
        in_specs=[specs[s] for s in spaces],
        out_specs=tuple(specs[s] for _, s in outs),
        scratch_shapes=list(scratch),
        compiler_params=pltpu.CompilerParams(vmem_limit_bytes=limit * 2**20),
        name=name,
    )(*args)


def near(shape, dtype):
    return pltpu.VMEM(shape, dtype), "v"


def far(shape, dtype):
    return pltpu.HBM(shape, dtype), "p"


def x_place():
    return lax.axis_index("xh") * 2 + lax.axis_index("ha")


def by_core(when_one, when_zero):
    return jnp.where(lax.axis_index("core") == 1, when_one, when_zero)


def border_cells(block, rows):
    edge = 11 * (1 - lax.axis_index("ha"))
    row = lax.broadcasted_iota(jnp.int32, (rows, 1), 0)
    column = jnp.where(row < 64, 15, 0) + (row >> 4 & 3) * 192 + (row & 15) * 16
    column = jnp.where((row & 15) < 12, column, -1)
    corner = jnp.where(row < 144, 15, 0) + (row & 15) * 192 + edge * 16
    corner = jnp.where((row & 15) < 4, corner, -1)
    source = jnp.where(row < 128, column, corner)
    chosen = (lax.broadcasted_iota(jnp.int32, (rows, 768), 1) == source).astype(BF)
    return jnp.dot(chosen, block.reshape(768, 256), preferred_element_type=F32)


def pack_kernel(one, two, row, face, outer, corner_face, corner_outer, same_one, same_two):
    same_one[...], same_two[...] = one[...], two[...]
    edge = 11 * (1 - lax.axis_index("ha"))
    for n, block in enumerate((one, two)):
        cells = border_cells(block[...], 160)
        hi, lo = cells[0:64].reshape(4, 16, 256), cells[64:128].reshape(4, 16, 256)
        face[n], outer[n] = by_core(lo, hi).astype(BF), by_core(hi, lo).astype(BF)
        hi, lo = cells[128:144], cells[144:160]
        corner_face[n], corner_outer[n] = by_core(lo, hi).astype(BF), by_core(hi, lo).astype(BF)
        for f in range(4):
            row[n, f] = block[f, edge]


def pad_block(put, block, row, left, right, corner_left, corner_right):
    ha, wa = lax.axis_index("ha"), lax.axis_index("xh") * 2 + lax.axis_index("core")
    is_top, is_low = (ha == 1).astype(F32), (ha == 0).astype(F32)
    rest = jnp.zeros((2, 256), F32)
    for f in range(4):
        edge = row(f).astype(F32)
        put(f, 0, edge * is_top)
        put(f, 13, edge * is_low)
        for r in range(12):
            put(f, r + 1, block(f, r))
        for n, side, corner, has in (
            (14, left, corner_left, (wa > 0).astype(F32)),
            (15, right, corner_right, (wa < 3).astype(F32)),
        ):
            cells, end = side(f).astype(F32)[0:12], corner(f).astype(F32)[0:1]
            cells = jnp.concatenate([end * is_top, cells, end * is_low, rest], axis=0)
            put(f, n, cells * has)


def build_shifted(put, padded):
    col = lax.broadcasted_iota(jnp.int32, (16, 256), 0)
    for f in range(4):
        lefts, rights = padded[f, 14].astype(F32), padded[f, 15].astype(F32)
        for r in range(14):
            cells, lo, hi = padded[f, r].astype(F32), lefts[r : r + 1], rights[r : r + 1]
            put(f, r, 1, padded[f, r])
            put(f, r, 0, jnp.where(col == 0, lo, pltpu.roll(cells, 1, 0)).astype(BF))
            put(f, r, 2, jnp.where(col == 15, hi, pltpu.roll(cells, 15, 0)).astype(BF))


def keep_in(padded):
    def put(f, n, cells):
        padded[f, n] = cells.astype(BF)

    return put


def put_back(wide):
    def put(f, r, which, cells):
        wide[f, r, :, (2 - which) * 256 : (3 - which) * 256] = cells

    return put


def weight_copies(weight, held, sem):
    return [
        pltpu.make_async_copy(weight.at[pl.ds(a * 9, 9)], held.at[pl.ds(a * 9, 9)], sem.at[a])
        for a in range(3)
    ]


def conv_sum(wide, tap, total):
    for a in (2, 1, 0):
        frames = a + 2
        for b in range(3):
            window = wide[2 - a : 4, 2 - b : 14 - b].reshape(frames * 192, 768)
            part = None
            for e in range(3):
                one = lax.dot_general(
                    window[:, e * 256 : (e + 1) * 256],
                    tap((a * 3 + b) * 3 + e),
                    NT,
                    preferred_element_type=F32,
                )
                part = one if part is None else part + one
            if a == 2 and b == 0:
                total[...] = part
            else:
                total[0 : frames * 192] += part


def channel_order():
    lane = lax.broadcasted_iota(jnp.int32, (256, 256), 1)
    goal, kept = x_place() ^ ((lane >> 5) & 3), lax.axis_index("core") ^ (lane >> 7)
    source = ((goal & 1) << 7) + ((goal >> 1) << 6) + (kept << 5) + (lane & 31)
    return (lax.broadcasted_iota(jnp.int32, (256, 256), 0) == source).astype(BF)


def film_kernel(
    step, inputs, hidden, table, weight, act_out, inp_out, slope, taps,
    film, block, sem, block_sem, tap_sem,
):
    start = step[0]
    whole = pl.multiple_of(start // 8 * 8, 8)
    film_copy = pltpu.make_async_copy(table.at[pl.ds(whole, 8)], film, sem)
    film_copy.start()
    block_copy = pltpu.make_async_copy(hidden, block, block_sem)
    block_copy.start()
    copies = weight_copies(weight, taps, tap_sem)
    for copy in copies:
        copy.start()
    order = channel_order()
    sort = lambda v: jnp.dot(v, order, preferred_element_type=F32).astype(BF)
    inp_out[...] = sort(inputs[...].reshape(768, 256)).reshape(4, 12, 16, 256)
    block_copy.wait()
    film_copy.wait()
    line = film[pl.ds(start - whole, 1), :]
    scale, shift = 1.0 + line[:, 0:256], line[:, 256:512]
    shifted = block[...].reshape(768, 256).astype(F32) * scale + shift
    sigma = jax.nn.sigmoid(shifted)
    act_out[...] = sort((shifted * sigma).astype(BF))
    slope[...] = scale * sigma * (1.0 + shifted * (1.0 - sigma))
    for copy in copies:
        copy.wait()


def pad_kernel(block, row, face, outer, corner_face, corner_outer, act, out):
    near_cells, far_cells = face[0].astype(F32), outer[0].astype(F32)
    near_ends, far_ends = corner_face[0].astype(F32), corner_outer[0].astype(F32)
    pad_block(
        keep_in(out),
        lambda f, r: block[f, r],
        lambda f: row[0, f],
        lambda f: by_core(near_cells[f], far_cells[f]),
        lambda f: by_core(far_cells[f], near_cells[f]),
        lambda f: by_core(near_ends[f : f + 1], far_ends[f : f + 1]),
        lambda f: by_core(far_ends[f : f + 1], near_ends[f : f + 1]),
    )
    for f in range(4):
        for n in range(12):
            cells = act[f * 192 + n * 16 : f * 192 + n * 16 + 16, 128:256]
            out[f, 16 + n % 6, :, n // 6 * 128 : n // 6 * 128 + 128] = cells


def first_kernel(padded, slope, taps, wide, hid_out, total):
    build_shifted(put_back(wide), padded)
    conv_sum(wide, lambda t: taps[t], total)
    hid_out[...] = (total[...] * slope[...]).astype(BF).reshape(4, 12, 16, 256)


def input_conv_kernel(
    hid, block, border, cols, after, weight, out, held, total, sem, wide, padded, near_block
):
    del after
    copies = weight_copies(weight, held, sem)
    copies.append(pltpu.make_async_copy(block, near_block, sem.at[3]))
    for copy in copies:
        copy.start()
    faces, outers = border[8].astype(F32), border[9].astype(F32)
    pad_block(
        keep_in(padded),
        lambda f, r: hid[f, r],
        lambda f: border[f],
        lambda f: by_core(cols[0, f].astype(F32), border[4 + f].astype(F32)),
        lambda f: by_core(border[4 + f].astype(F32), cols[1, f].astype(F32)),
        lambda f: by_core(faces[f : f + 1], outers[f : f + 1]),
        lambda f: by_core(outers[f : f + 1], faces[f : f + 1]),
    )
    build_shifted(put_back(wide), padded)
    for copy in copies:
        copy.wait()
    conv_sum(wide, lambda t: held[t], total)
    grad = near_block[...].reshape(768, 256).astype(F32) + total[...]
    out[...] = grad.astype(BF).reshape(4, 12, 16, 256)


def second_own_kernel(wide, act, got, after, keep, one, two, three, pair_wide, pair_act):
    del after
    build_shifted(put_back(pair_wide), got)
    for f in range(4):
        for n in range(12):
            cells = got[f, 16 + n % 6, :, n // 6 * 128 : n // 6 * 128 + 128]
            pair_act[f * 192 + n * 16 : f * 192 + n * 16 + 16, :] = cells
    for a in range(3):
        rows = (a + 2) * 192
        for b in range(3):
            total = None
            for left, right in ((act[0:rows, 0:128], wide), (pair_act[0:rows], pair_wide)):
                window = right[2 - a : 4, 2 - b : 14 - b].reshape(rows, 768)
                part = lax.dot_general(left, window, TN, preferred_element_type=F32)
                total = part if total is None else total + part
            for d, out in enumerate((keep, one, two, three)):
                out[a * 3 + b] = total[d * 32 : d * 32 + 32].astype(out.dtype)


def second_x_kernel(got1, got2, got3, own, keep, one, two, three, held):
    y = lax.axis_index("y")

    def tap(t):
        ab, lanes = t // 3, slice(t % 3 * 256, t % 3 * 256 + 256)
        total = own[ab, :, lanes]
        for got in (got1, got2, got3):
            total = total + got[ab, :, lanes].astype(F32)
        return total

    for g in range(7):
        parts = [tap(t) if t < 27 else jnp.zeros((32, 256), F32) for t in range(4 * g, 4 * g + 4)]
        held[...] = jnp.concatenate(parts, axis=0).T.reshape(8, 4, 8, 128)
        for d, out in enumerate((keep, one, two, three)):
            out[g * 64 : g * 64 + 64] = held[:, y ^ d].reshape(64, 128).astype(out.dtype)
    for out in (one, two, three):
        out[448:592] = jnp.zeros((144, 128), BF)


def border_at(n, h):
    slot = n * 2 + h
    return slot // 4, slice(slot % 4 * 16, slot % 4 * 16 + 16)


def border_rows(n, h):
    return slice(448 + (n * 2 + h) * 16, 464 + (n * 2 + h) * 16)


def first_grad_kernel(
    hid, inp, row, face, outer, corner_face, corner_outer, after,
    own, pair, wide, padded, side,
):
    del after
    order = channel_order()
    for at, ref in ((0, row), (4, face), (8, outer), (12, corner_face), (13, corner_outer)):
        size = 4 if at < 12 else 1
        cells = jnp.dot(ref[1].reshape(size * 16, 256), order, preferred_element_type=F32)
        side[at : at + size] = cells.reshape(size, 16, 256)

    def put(f, r, which, cells):
        at = which * 128
        wide[f, r, :, at : at + 128] = cells[:, 0:128]
        wide[f, r, :, at + 384 : at + 512] = cells[:, 128:256]

    pad_block(
        keep_in(padded),
        lambda f, r: inp[f, r],
        lambda f: side[f],
        lambda f: by_core(side[4 + f], side[8 + f]),
        lambda f: by_core(side[8 + f], side[4 + f]),
        lambda f: by_core(side[12, f : f + 1], side[13, f : f + 1]),
        lambda f: by_core(side[13, f : f + 1], side[12, f : f + 1]),
    )
    build_shifted(put, padded)
    cells = border_cells(hid[...], 128)
    for n in range(8):
        for h in range(2):
            q, rows = border_at(n, h)
            pair[q, 27, rows] = cells[n * 16 : n * 16 + 16, h * 128 : h * 128 + 128]
    for a in range(3):
        rows = (a + 2) * 192
        left = hid[2 - a : 4].reshape(rows, 256)
        for b in range(3):
            window = wide[0 : a + 2, b : b + 12].reshape(rows, 768)
            grad = lax.dot_general(left, window, TN, preferred_element_type=F32)
            grad = grad.reshape(8, 4, 8, 768)
            for q in range(4):
                piece = grad[:, q].reshape(64, 768)
                for e in range(3):
                    t = (a * 3 + b) * 3 + e
                    own[q, t] = piece[:, e * 128 : e * 128 + 128]
                    pair[q, t] = piece[:, e * 128 + 384 : e * 128 + 512]


def first_sum_kernel(own, pair, after, keep, one, two, three, cols):
    del after
    y = lax.axis_index("y")
    for d, out in enumerate((keep, one, two, three)):
        q = y ^ d
        out[...] = (own[q] + pair[q, 0:27]).astype(out.dtype)
    for n in range(8):
        for h in range(2):
            q, rows = border_at(n, h)
            cols[n // 4, n % 4, :, h * 128 : h * 128 + 128] = pair[q, 27, rows].astype(BF)


def first_y_kernel(got1, got2, got3, own, hid, cols, after, keep, one, two, three):
    del after

    def tap(t):
        total = own[t]
        for got in (got1, got2, got3):
            total = total + got[t].astype(F32)
        return total

    for g in range(7):
        taps = [tap(t) if t < 27 else jnp.zeros((64, 128), F32) for t in range(4 * g, 4 * g + 4)]
        for d, out in enumerate((keep, one, two, three)):
            piece = jnp.concatenate([v[:, d * 32 : d * 32 + 32] for v in taps], axis=1)
            out[g * 64 : g * 64 + 64] = piece.astype(out.dtype)

    edge = 11 * (1 - lax.axis_index("ha"))
    faces, outers = [], []
    for f in range(4):
        hi, lo = cols[0, f].astype(F32), cols[1, f].astype(F32)
        face, outer = by_core(hi, lo), by_core(lo, hi)
        row, across = hid[f, edge], outer.astype(BF)
        for h in range(2):
            lanes = slice(h * 128, h * 128 + 128)
            one[border_rows(f, h)] = row[:, lanes]
            two[border_rows(f, h)] = across[:, lanes]
        faces.append(jnp.where(edge == 0, face[0:1], face[11:12]))
        outers.append(jnp.where(edge == 0, outer[0:1], outer[11:12]))
    rest = [jnp.zeros((8, 128), F32)]
    for out, rows, cells in ((one, slice(576, 592), faces), (three, slice(448, 464), outers)):
        halves = [c[:, 0:128] for c in cells] + [c[:, 128:256] for c in cells]
        out[rows] = jnp.concatenate(halves + rest, axis=0).astype(BF)


def last_kernel(own_two, a2, a1, a3, own_one, b2, b1, b3, out, keep, border, held):
    for f in range(4):
        for h in range(2):
            lanes = slice(h * 128, h * 128 + 128)
            border[f, :, lanes] = b1[border_rows(f, h)]
            border[4 + f, :, lanes] = b2[border_rows(f, h)]
    for n, corners in ((8, b1[576:592]), (9, b3[448:464])):
        corners = corners.astype(F32)
        for h in range(2):
            cells = corners[h * 4 : h * 4 + 4]
            cells = jnp.concatenate([cells, jnp.zeros((12, 128), F32)], axis=0)
            border[n, :, h * 128 : h * 128 + 128] = cells.astype(BF)
    for n, (own, got) in enumerate(((own_two, (a1, a2, a3)), (own_one, (b1, b2, b3)))):
        total = own[...]
        for ref in got:
            total = total + ref[0:448].astype(F32)
        held[n] = total.reshape(7, 8, 8, 128)

    def plane(z):
        return jnp.concatenate([held[n, :, z].reshape(56, 128) for n in range(2)], axis=0)

    for q in range(8):
        out[q] = plane(q).astype(BF)
    keep[...] = plane(lax.axis_index("z"))


def final_kernel(factor, got, own, after, one, two):
    del after
    z = lax.axis_index("z")
    total = own[...]
    for d in range(1, 8):
        total = total + got[(z + d) & 7].astype(F32)
    total = (total * factor).reshape(2, 7, 8, 128)
    for out, which in ((two, 0), (one, 1)):
        for t in range(27):
            out[t] = total[which, t // 4, :, t % 4 * 32 : t % 4 * 32 + 32]


def shards(activations, saved_hidden, cotangent, conv_one, conv_two, film_table, timesteps):
    inputs, hidden, block = activations[0], saved_hidden[0], cotangent[0]
    taps_one = conv_one.transpose(1, 2, 3, 0, 4).reshape(27, 256, 256)
    taps_two = conv_two.transpose(1, 2, 3, 0, 4).reshape(27, 256, 256)
    wide = near((4, 14, 16, 768), BF)
    def ring(parts, axis):
        return [send(parts[d - 1], ring_pairs(**{axis: d})) for d in (2, 1, 3)]

    *packed, held_block, held_inputs = call(
        pack_kernel,
        "pack_first",
        (block, inputs),
        "pp",
        [near((2, 4, 16, 256), BF)] * 3
        + [near((2, 16, 256), BF)] * 2
        + [near((4, 12, 16, 256), BF)] * 2,
    )
    ways = ((1, 0), (0, 1), (0, 3), (1, 1), (1, 3))
    sides = [send(p, block_pairs(*way)) for p, way in zip(packed, ways)]
    act, inp, slope, held_two = call(
        film_kernel,
        "film",
        (timesteps, held_inputs, hidden, film_table, taps_two),
        "svhhh",
        [
            near((768, 256), BF),
            near((4, 12, 16, 256), BF),
            near((768, 256), F32),
            near((27, 256, 256), BF),
        ],
        [
            pltpu.VMEM((8, 512), F32),
            pltpu.VMEM((4, 12, 16, 256), BF),
            pltpu.SemaphoreType.DMA,
            pltpu.SemaphoreType.DMA,
            pltpu.SemaphoreType.DMA((3,)),
        ],
    )
    (padded,) = call(
        pad_kernel,
        "pad_cotangent",
        (held_block, *sides, act),
        "vvvvvvv",
        [near((4, 22, 16, 256), BF)],
    )
    pair_padded = send(padded, core_pairs())
    wide_cot, grad_hidden = call(
        first_kernel,
        "conv_two_back",
        (padded, slope, held_two),
        "vvv",
        [wide, near((4, 12, 16, 256), BF)],
        [pltpu.VMEM((768, 256), F32)],
    )

    own_one, pair_one = call(
        first_grad_kernel,
        "grad_one",
        (grad_hidden, inp, *sides, pair_padded),
        "vv" + "v" * 6,
        [near((4, 27, 64, 128), F32), near((4, 28, 64, 128), F32)],
        [
            pltpu.VMEM((4, 14, 16, 768), BF),
            pltpu.VMEM((4, 16, 16, 256), BF),
            pltpu.VMEM((14, 16, 256), F32),
        ],
    )
    got_pair_one = send(pair_one, core_pairs())
    own_two, *parts = call(
        second_own_kernel,
        "grad_two",
        (wide_cot, act, pair_padded, pair_one),
        "vvvv",
        [near((9, 32, 768), F32)] + [near((9, 32, 768), BF)] * 3,
        [pltpu.VMEM((4, 14, 16, 768), BF), pltpu.VMEM((768, 128), BF)],
    )
    got_two = ring(parts, "dx")
    own_one, *parts_one, cols = call(
        first_sum_kernel,
        "grad_one_sum",
        (own_one, got_pair_one, parts[0]),
        "vvv",
        [near((27, 64, 128), F32)]
        + [near((27, 64, 128), BF)] * 3
        + [near((2, 4, 16, 256), BF)],
    )
    got_one = ring(parts_one, "dy")

    own_two, *parts = call(
        second_x_kernel,
        "grad_two_x",
        (*got_two, own_two),
        "vvvv",
        [near((448, 128), F32)] + [near((592, 128), BF)] * 3,
        [pltpu.VMEM((8, 4, 8, 128), F32)],
    )
    got_two = ring(parts, "dy")
    own_one, *parts_one = call(
        first_y_kernel,
        "grad_one_y",
        (*got_one, own_one, grad_hidden, cols, parts[0]),
        "v" * 7,
        [near((448, 128), F32), near((592, 128), BF), near((576, 128), BF), near((464, 128), BF)],
    )
    got_one = ring(parts_one, "dx")

    out, own, border = call(
        last_kernel,
        "last_stage",
        (own_two, *got_two, own_one, *got_one),
        "v" * 8,
        [far((8, 112, 128), BF), near((112, 128), F32), near((10, 16, 256), BF)],
        [pltpu.VMEM((2, 7, 8, 8, 128), F32)],
    )
    planes = lax.all_to_all(out, "z", 0, 0, tiled=True)

    (grad_input,) = call(
        input_conv_kernel,
        "conv_one_back",
        (grad_hidden, block, border, cols, own, taps_one),
        "vhvvvh",
        [(jax.ShapeDtypeStruct((4, 12, 16, 256), BF), "v")],
        [
            pltpu.VMEM((27, 256, 256), BF),
            pltpu.VMEM((768, 256), F32),
            pltpu.SemaphoreType.DMA((4,)),
            pltpu.VMEM((4, 14, 16, 768), BF),
            pltpu.VMEM((4, 16, 16, 256), BF),
            pltpu.VMEM((4, 12, 16, 256), BF),
        ],
    )

    factor = float(256 * 768) ** (-0.5)
    result = jax.ShapeDtypeStruct((27, 8, 32), F32), "v"
    grad_one, grad_two = call(
        functools.partial(final_kernel, factor), "final_sum", (planes, own, grad_input), "vvh", [result, result]
    )
    shape = lambda g: g.transpose(2, 0, 1).reshape(32, 3, 3, 3, 8)
    return grad_input[None], shape(grad_one), shape(grad_two)


def solution(mesh):
    fine = Mesh(mesh.devices.reshape(SIZES), AX)
    clip = ("z", "y")
    placed = P(clip, None, "ha", ("xh", "core"), None)
    weight = P(("ha", "xh", "core"), None, None, None, clip)
    return jax.shard_map(
        shards,
        mesh=fine,
        in_specs=(placed, placed, placed, P(), P(), P(), P(clip)),
        out_specs=(placed, weight, weight),
        check_vma=False,
    )
```

```python
import functools

import jax
import jax.numpy as jnp
from jax import lax
from jax.experimental import pallas as pl
from jax.experimental.pallas import tpu as pltpu
from jax.sharding import Mesh
from jax.sharding import PartitionSpec as P

BF = jnp.bfloat16
F32 = jnp.float32
AX = ("z", "y", "ha", "xh", "core")
SIZES = (8, 4, 2, 2, 2)
VM = pl.BlockSpec(memory_space=pltpu.VMEM)
HB = pl.BlockSpec(memory_space=pl.ANY)
SM = pl.BlockSpec(memory_space=pltpu.SMEM)
NT = (((1,), (1,)), ((), ()))
TN = (((0,), (0,)), ((), ()))


def core_pairs():
    return [(i, i ^ 1) for i in range(256)]


def block_pairs(dh, dw):
    return [(i, i ^ (dh * 4 + dw)) for i in range(256)]


def ring_pairs(dx=0, dy=0):
    pairs = []
    for i in range(256):
        core, xh, ha, y, z = i % 2, i // 2 % 2, i // 4 % 2, i // 8 % 4, i // 32
        x, y = (xh * 2 + ha) ^ dx, y ^ dy
        pairs.append((i, ((z * 4 + y) * 2 + x % 2) * 4 + x // 2 * 2 + core))
    return pairs


def send(value, pairs):
    return lax.ppermute(value, AX, pairs)


def call(kernel, name, args, spaces, outs, scratch=(), limit=16):
    where = {"v": pltpu.VMEM, "p": pltpu.HBM, "h": pltpu.HBM}
    args = [
        pltpu.with_memory_space_constraint(a, where[s]) if s in where else a
        for a, s in zip(args, spaces)
    ]
    specs = {"v": VM, "p": VM, "h": HB, "s": SM}
    return pl.pallas_call(
        kernel,
        out_shape=tuple(o for o, _ in outs),
        in_specs=[specs[s] for s in spaces],
        out_specs=tuple(specs[s] for _, s in outs),
        scratch_shapes=list(scratch),
        compiler_params=pltpu.CompilerParams(vmem_limit_bytes=limit * 2**20),
        name=name,
    )(*args)


def near(shape, dtype):
    return pltpu.VMEM(shape, dtype), "v"


def far(shape, dtype):
    return pltpu.HBM(shape, dtype), "p"


def x_place():
    return lax.axis_index("xh") * 2 + lax.axis_index("ha")


def by_core(when_one, when_zero):
    return jnp.where(lax.axis_index("core") == 1, when_one, when_zero)


def border_cells(block, rows):
    edge = 11 * (1 - lax.axis_index("ha"))
    row = lax.broadcasted_iota(jnp.int32, (rows, 1), 0)
    column = jnp.where(row < 64, 15, 0) + (row >> 4 & 3) * 192 + (row & 15) * 16
    column = jnp.where((row & 15) < 12, column, -1)
    corner = jnp.where(row < 144, 15, 0) + (row & 15) * 192 + edge * 16
    corner = jnp.where((row & 15) < 4, corner, -1)
    source = jnp.where(row < 128, column, corner)
    chosen = (lax.broadcasted_iota(jnp.int32, (rows, 768), 1) == source).astype(BF)
    return jnp.dot(chosen, block.reshape(768, 256), preferred_element_type=F32)


def pack_kernel(one, two, row, face, outer, corner_face, corner_outer, same_one, same_two):
    same_one[...], same_two[...] = one[...], two[...]
    edge = 11 * (1 - lax.axis_index("ha"))
    for n, block in enumerate((one, two)):
        cells = border_cells(block[...], 160)
        hi, lo = cells[0:64].reshape(4, 16, 256), cells[64:128].reshape(4, 16, 256)
        face[n], outer[n] = by_core(lo, hi).astype(BF), by_core(hi, lo).astype(BF)
        hi, lo = cells[128:144], cells[144:160]
        corner_face[n], corner_outer[n] = by_core(lo, hi).astype(BF), by_core(hi, lo).astype(BF)
        for f in range(4):
            row[n, f] = block[f, edge]


def pad_block(put, block, row, left, right, corner_left, corner_right):
    ha, wa = lax.axis_index("ha"), lax.axis_index("xh") * 2 + lax.axis_index("core")
    is_top, is_low = (ha == 1).astype(F32), (ha == 0).astype(F32)
    rest = jnp.zeros((2, 256), F32)
    for f in range(4):
        edge = row(f).astype(F32)
        put(f, 0, edge * is_top)
        put(f, 13, edge * is_low)
        for r in range(12):
            put(f, r + 1, block(f, r))
        for n, side, corner, has in (
            (14, left, corner_left, (wa > 0).astype(F32)),
            (15, right, corner_right, (wa < 3).astype(F32)),
        ):
            cells, end = side(f).astype(F32)[0:12], corner(f).astype(F32)[0:1]
            cells = jnp.concatenate([end * is_top, cells, end * is_low, rest], axis=0)
            put(f, n, cells * has)


def build_shifted(put, padded):
    col = lax.broadcasted_iota(jnp.int32, (16, 256), 0)
    for f in range(4):
        lefts, rights = padded[f, 14].astype(F32), padded[f, 15].astype(F32)
        for r in range(14):
            cells, lo, hi = padded[f, r].astype(F32), lefts[r : r + 1], rights[r : r + 1]
            put(f, r, 1, padded[f, r])
            put(f, r, 0, jnp.where(col == 0, lo, pltpu.roll(cells, 1, 0)).astype(BF))
            put(f, r, 2, jnp.where(col == 15, hi, pltpu.roll(cells, 15, 0)).astype(BF))


def keep_in(padded):
    def put(f, n, cells):
        padded[f, n] = cells.astype(BF)

    return put


def put_back(wide):
    def put(f, r, which, cells):
        wide[f, r, :, (2 - which) * 256 : (3 - which) * 256] = cells

    return put


def weight_copies(weight, held, sem):
    return [
        pltpu.make_async_copy(weight.at[pl.ds(a * 9, 9)], held.at[pl.ds(a * 9, 9)], sem.at[a])
        for a in range(3)
    ]


def conv_sum(wide, tap, total):
    for a in (2, 1, 0):
        frames = a + 2
        for b in range(3):
            window = wide[2 - a : 4, 2 - b : 14 - b].reshape(frames * 192, 768)
            part = None
            for e in range(3):
                one = lax.dot_general(
                    window[:, e * 256 : (e + 1) * 256],
                    tap((a * 3 + b) * 3 + e),
                    NT,
                    preferred_element_type=F32,
                )
                part = one if part is None else part + one
            if a == 2 and b == 0:
                total[...] = part
            else:
                total[0 : frames * 192] += part


def channel_order():
    lane = lax.broadcasted_iota(jnp.int32, (256, 256), 1)
    goal, kept = x_place() ^ ((lane >> 5) & 3), lax.axis_index("core") ^ (lane >> 7)
    source = ((goal & 1) << 7) + ((goal >> 1) << 6) + (kept << 5) + (lane & 31)
    return (lax.broadcasted_iota(jnp.int32, (256, 256), 0) == source).astype(BF)


def film_kernel(
    step, inputs, hidden, table, weight, act_out, inp_out, slope, taps,
    film, block, sem, block_sem, tap_sem,
):
    start = step[0]
    whole = pl.multiple_of(start // 8 * 8, 8)
    film_copy = pltpu.make_async_copy(table.at[pl.ds(whole, 8)], film, sem)
    film_copy.start()
    block_copy = pltpu.make_async_copy(hidden, block, block_sem)
    block_copy.start()
    copies = weight_copies(weight, taps, tap_sem)
    for copy in copies:
        copy.start()
    order = channel_order()
    sort = lambda v: jnp.dot(v, order, preferred_element_type=F32).astype(BF)
    inp_out[...] = sort(inputs[...].reshape(768, 256)).reshape(4, 12, 16, 256)
    block_copy.wait()
    film_copy.wait()
    line = film[pl.ds(start - whole, 1), :]
    scale, shift = 1.0 + line[:, 0:256], line[:, 256:512]
    shifted = block[...].reshape(768, 256).astype(F32) * scale + shift
    sigma = jax.nn.sigmoid(shifted)
    act_out[...] = sort((shifted * sigma).astype(BF))
    slope[...] = scale * sigma * (1.0 + shifted * (1.0 - sigma))
    for copy in copies:
        copy.wait()


def pad_kernel(block, row, face, outer, corner_face, corner_outer, act, out):
    near_cells, far_cells = face[0].astype(F32), outer[0].astype(F32)
    near_ends, far_ends = corner_face[0].astype(F32), corner_outer[0].astype(F32)
    pad_block(
        keep_in(out),
        lambda f, r: block[f, r],
        lambda f: row[0, f],
        lambda f: by_core(near_cells[f], far_cells[f]),
        lambda f: by_core(far_cells[f], near_cells[f]),
        lambda f: by_core(near_ends[f : f + 1], far_ends[f : f + 1]),
        lambda f: by_core(far_ends[f : f + 1], near_ends[f : f + 1]),
    )
    for f in range(4):
        for n in range(12):
            cells = act[f * 192 + n * 16 : f * 192 + n * 16 + 16, 128:256]
            out[f, 16 + n % 6, :, n // 6 * 128 : n // 6 * 128 + 128] = cells


def first_kernel(padded, slope, taps, wide, hid_out, total):
    build_shifted(put_back(wide), padded)
    conv_sum(wide, lambda t: taps[t], total)
    hid_out[...] = (total[...] * slope[...]).astype(BF).reshape(4, 12, 16, 256)


def input_conv_kernel(
    hid, block, border, cols, after, weight, out, held, total, sem, wide, padded, near_block
):
    del after
    copies = weight_copies(weight, held, sem)
    copies.append(pltpu.make_async_copy(block, near_block, sem.at[3]))
    for copy in copies:
        copy.start()
    faces, outers = border[8].astype(F32), border[9].astype(F32)
    pad_block(
        keep_in(padded),
        lambda f, r: hid[f, r],
        lambda f: border[f],
        lambda f: by_core(cols[0, f].astype(F32), border[4 + f].astype(F32)),
        lambda f: by_core(border[4 + f].astype(F32), cols[1, f].astype(F32)),
        lambda f: by_core(faces[f : f + 1], outers[f : f + 1]),
        lambda f: by_core(outers[f : f + 1], faces[f : f + 1]),
    )
    build_shifted(put_back(wide), padded)
    for copy in copies:
        copy.wait()
    conv_sum(wide, lambda t: held[t], total)
    grad = near_block[...].reshape(768, 256).astype(F32) + total[...]
    out[...] = grad.astype(BF).reshape(4, 12, 16, 256)


def second_own_kernel(wide, act, got, after, keep, one, two, three, pair_wide, pair_act):
    del after
    build_shifted(put_back(pair_wide), got)
    for f in range(4):
        for n in range(12):
            cells = got[f, 16 + n % 6, :, n // 6 * 128 : n // 6 * 128 + 128]
            pair_act[f * 192 + n * 16 : f * 192 + n * 16 + 16, :] = cells
    for a in range(3):
        rows = (a + 2) * 192
        for b in range(3):
            total = None
            for left, right in ((act[0:rows, 0:128], wide), (pair_act[0:rows], pair_wide)):
                window = right[2 - a : 4, 2 - b : 14 - b].reshape(rows, 768)
                part = lax.dot_general(left, window, TN, preferred_element_type=F32)
                total = part if total is None else total + part
            for d, out in enumerate((keep, one, two, three)):
                out[a * 3 + b] = total[d * 32 : d * 32 + 32].astype(out.dtype)


def second_x_kernel(got1, got2, got3, own, keep, one, two, three, held):
    y = lax.axis_index("y")

    def tap(t):
        ab, lanes = t // 3, slice(t % 3 * 256, t % 3 * 256 + 256)
        total = own[ab, :, lanes]
        for got in (got1, got2, got3):
            total = total + got[ab, :, lanes].astype(F32)
        return total

    for g in range(7):
        parts = [tap(t) if t < 27 else jnp.zeros((32, 256), F32) for t in range(4 * g, 4 * g + 4)]
        held[...] = jnp.concatenate(parts, axis=0).T.reshape(8, 4, 8, 128)
        for d, out in enumerate((keep, one, two, three)):
            out[g * 64 : g * 64 + 64] = held[:, y ^ d].reshape(64, 128).astype(out.dtype)
    for out, rows in ((one, 144), (two, 144), (three, 16)):
        out[448 : 448 + rows] = jnp.zeros((rows, 128), BF)


def border_at(n, h):
    slot = n * 2 + h
    return slot // 4, slice(slot % 4 * 16, slot % 4 * 16 + 16)


def border_rows(n, h):
    return slice(448 + (n * 2 + h) * 16, 464 + (n * 2 + h) * 16)


def first_grad_kernel(
    hid, inp, row, face, outer, corner_face, corner_outer, after,
    own, pair, wide, padded, side,
):
    del after
    order = channel_order()
    for at, ref in ((0, row), (4, face), (8, outer), (12, corner_face), (13, corner_outer)):
        size = 4 if at < 12 else 1
        cells = jnp.dot(ref[1].reshape(size * 16, 256), order, preferred_element_type=F32)
        side[at : at + size] = cells.reshape(size, 16, 256)

    def put(f, r, which, cells):
        at = which * 128
        wide[f, r, :, at : at + 128] = cells[:, 0:128]
        wide[f, r, :, at + 384 : at + 512] = cells[:, 128:256]

    pad_block(
        keep_in(padded),
        lambda f, r: inp[f, r],
        lambda f: side[f],
        lambda f: by_core(side[4 + f], side[8 + f]),
        lambda f: by_core(side[8 + f], side[4 + f]),
        lambda f: by_core(side[12, f : f + 1], side[13, f : f + 1]),
        lambda f: by_core(side[13, f : f + 1], side[12, f : f + 1]),
    )
    build_shifted(put, padded)
    cells = border_cells(hid[...], 128)
    for n in range(8):
        for h in range(2):
            q, rows = border_at(n, h)
            pair[q, 27, rows] = cells[n * 16 : n * 16 + 16, h * 128 : h * 128 + 128]
    for a in range(3):
        rows = (a + 2) * 192
        left = hid[2 - a : 4].reshape(rows, 256)
        for b in range(3):
            window = wide[0 : a + 2, b : b + 12].reshape(rows, 768)
            grad = lax.dot_general(left, window, TN, preferred_element_type=F32)
            grad = grad.reshape(8, 4, 8, 768)
            for q in range(4):
                piece = grad[:, q].reshape(64, 768)
                for e in range(3):
                    t = (a * 3 + b) * 3 + e
                    own[q, t] = piece[:, e * 128 : e * 128 + 128]
                    pair[q, t] = piece[:, e * 128 + 384 : e * 128 + 512]


def first_sum_kernel(own, pair, after, keep, one, two, three, cols):
    del after
    y = lax.axis_index("y")
    for d, out in enumerate((keep, one, two, three)):
        q = y ^ d
        out[...] = (own[q] + pair[q, 0:27]).astype(out.dtype)
    for n in range(8):
        for h in range(2):
            q, rows = border_at(n, h)
            cols[n // 4, n % 4, :, h * 128 : h * 128 + 128] = pair[q, 27, rows].astype(BF)


def first_y_kernel(got1, got2, got3, own, hid, cols, after, keep, one, two, three):
    del after

    def tap(t):
        total = own[t]
        for got in (got1, got2, got3):
            total = total + got[t].astype(F32)
        return total

    for g in range(7):
        taps = [tap(t) if t < 27 else jnp.zeros((64, 128), F32) for t in range(4 * g, 4 * g + 4)]
        for d, out in enumerate((keep, one, two, three)):
            piece = jnp.concatenate([v[:, d * 32 : d * 32 + 32] for v in taps], axis=1)
            out[g * 64 : g * 64 + 64] = piece.astype(out.dtype)

    edge = 11 * (1 - lax.axis_index("ha"))
    faces, outers = [], []
    for f in range(4):
        hi, lo = cols[0, f].astype(F32), cols[1, f].astype(F32)
        face, outer = by_core(hi, lo), by_core(lo, hi)
        row, across = hid[f, edge], outer.astype(BF)
        for h in range(2):
            lanes = slice(h * 128, h * 128 + 128)
            one[border_rows(f, h)] = row[:, lanes]
            two[border_rows(f, h)] = across[:, lanes]
        faces.append(jnp.where(edge == 0, face[0:1], face[11:12]))
        outers.append(jnp.where(edge == 0, outer[0:1], outer[11:12]))
    rest = [jnp.zeros((8, 128), F32)]
    for out, rows, cells in ((one, slice(576, 592), faces), (three, slice(448, 464), outers)):
        halves = [c[:, 0:128] for c in cells] + [c[:, 128:256] for c in cells]
        out[rows] = jnp.concatenate(halves + rest, axis=0).astype(BF)


def last_kernel(own_two, a2, a1, a3, own_one, b2, b1, b3, out, keep, border, held):
    for f in range(4):
        for h in range(2):
            lanes = slice(h * 128, h * 128 + 128)
            border[f, :, lanes] = b1[border_rows(f, h)]
            border[4 + f, :, lanes] = b2[border_rows(f, h)]
    for n, corners in ((8, b1[576:592]), (9, b3[448:464])):
        corners = corners.astype(F32)
        for h in range(2):
            cells = corners[h * 4 : h * 4 + 4]
            cells = jnp.concatenate([cells, jnp.zeros((12, 128), F32)], axis=0)
            border[n, :, h * 128 : h * 128 + 128] = cells.astype(BF)
    for n, (own, got) in enumerate(((own_two, (a1, a2, a3)), (own_one, (b1, b2, b3)))):
        total = own[...]
        for ref in got:
            total = total + ref[0:448].astype(F32)
        held[n] = total.reshape(7, 8, 8, 128)

    def plane(z):
        return jnp.concatenate([held[n, :, z].reshape(56, 128) for n in range(2)], axis=0)

    for q in range(8):
        out[q] = plane(q).astype(BF)
    keep[...] = plane(lax.axis_index("z"))


def final_kernel(factor, got, own, after, one, two):
    del after
    z = lax.axis_index("z")
    total = own[...]
    for d in range(1, 8):
        total = total + got[(z + d) & 7].astype(F32)
    total = (total * factor).reshape(2, 7, 8, 128)
    for out, which in ((two, 0), (one, 1)):
        for t in range(27):
            out[t] = total[which, t // 4, :, t % 4 * 32 : t % 4 * 32 + 32]


def shards(activations, saved_hidden, cotangent, conv_one, conv_two, film_table, timesteps):
    inputs, hidden, block = activations[0], saved_hidden[0], cotangent[0]
    taps_one = conv_one.transpose(1, 2, 3, 0, 4).reshape(27, 256, 256)
    taps_two = conv_two.transpose(1, 2, 3, 0, 4).reshape(27, 256, 256)
    wide = near((4, 14, 16, 768), BF)
    def ring(parts, axis):
        return [send(parts[d - 1], ring_pairs(**{axis: d})) for d in (2, 1, 3)]

    *packed, held_block, held_inputs = call(
        pack_kernel,
        "pack_first",
        (block, inputs),
        "pp",
        [near((2, 4, 16, 256), BF)] * 3
        + [near((2, 16, 256), BF)] * 2
        + [near((4, 12, 16, 256), BF)] * 2,
    )
    ways = ((1, 0), (0, 1), (0, 3), (1, 1), (1, 3))
    sides = [send(p, block_pairs(*way)) for p, way in zip(packed, ways)]
    act, inp, slope, held_two = call(
        film_kernel,
        "film",
        (timesteps, held_inputs, hidden, film_table, taps_two),
        "svhhh",
        [
            near((768, 256), BF),
            near((4, 12, 16, 256), BF),
            near((768, 256), F32),
            near((27, 256, 256), BF),
        ],
        [
            pltpu.VMEM((8, 512), F32),
            pltpu.VMEM((4, 12, 16, 256), BF),
            pltpu.SemaphoreType.DMA,
            pltpu.SemaphoreType.DMA,
            pltpu.SemaphoreType.DMA((3,)),
        ],
    )
    (padded,) = call(
        pad_kernel,
        "pad_cotangent",
        (held_block, *sides, act),
        "vvvvvvv",
        [near((4, 22, 16, 256), BF)],
    )
    pair_padded = send(padded, core_pairs())
    wide_cot, grad_hidden = call(
        first_kernel,
        "conv_two_back",
        (padded, slope, held_two),
        "vvv",
        [wide, near((4, 12, 16, 256), BF)],
        [pltpu.VMEM((768, 256), F32)],
    )

    own_one, pair_one = call(
        first_grad_kernel,
        "grad_one",
        (grad_hidden, inp, *sides, pair_padded),
        "vv" + "v" * 6,
        [near((4, 27, 64, 128), F32), near((4, 28, 64, 128), F32)],
        [
            pltpu.VMEM((4, 14, 16, 768), BF),
            pltpu.VMEM((4, 16, 16, 256), BF),
            pltpu.VMEM((14, 16, 256), F32),
        ],
    )
    got_pair_one = send(pair_one, core_pairs())
    own_two, *parts = call(
        second_own_kernel,
        "grad_two",
        (wide_cot, act, pair_padded, pair_one),
        "vvvv",
        [near((9, 32, 768), F32)] + [near((9, 32, 768), BF)] * 3,
        [pltpu.VMEM((4, 14, 16, 768), BF), pltpu.VMEM((768, 128), BF)],
    )
    got_two = ring(parts, "dx")
    own_one, *parts_one, cols = call(
        first_sum_kernel,
        "grad_one_sum",
        (own_one, got_pair_one, parts[0]),
        "vvv",
        [near((27, 64, 128), F32)]
        + [near((27, 64, 128), BF)] * 3
        + [near((2, 4, 16, 256), BF)],
    )
    got_one = ring(parts_one, "dy")

    own_two, *parts = call(
        second_x_kernel,
        "grad_two_x",
        (*got_two, own_two),
        "vvvv",
        [near((448, 128), F32), near((592, 128), BF), near((592, 128), BF), near((464, 128), BF)],
        [pltpu.VMEM((8, 4, 8, 128), F32)],
    )
    got_two = ring(parts, "dy")
    own_one, *parts_one = call(
        first_y_kernel,
        "grad_one_y",
        (*got_one, own_one, grad_hidden, cols, parts[0]),
        "v" * 7,
        [near((448, 128), F32), near((592, 128), BF), near((576, 128), BF), near((464, 128), BF)],
    )
    got_one = ring(parts_one, "dx")

    out, own, border = call(
        last_kernel,
        "last_stage",
        (own_two, *got_two, own_one, *got_one),
        "v" * 8,
        [far((8, 112, 128), BF), near((112, 128), F32), near((10, 16, 256), BF)],
        [pltpu.VMEM((2, 7, 8, 8, 128), F32)],
    )
    planes = lax.all_to_all(out, "z", 0, 0, tiled=True)

    (grad_input,) = call(
        input_conv_kernel,
        "conv_one_back",
        (grad_hidden, block, border, cols, own, taps_one),
        "vhvvvh",
        [(jax.ShapeDtypeStruct((4, 12, 16, 256), BF), "v")],
        [
            pltpu.VMEM((27, 256, 256), BF),
            pltpu.VMEM((768, 256), F32),
            pltpu.SemaphoreType.DMA((4,)),
            pltpu.VMEM((4, 14, 16, 768), BF),
            pltpu.VMEM((4, 16, 16, 256), BF),
            pltpu.VMEM((4, 12, 16, 256), BF),
        ],
    )

    factor = float(256 * 768) ** (-0.5)
    result = jax.ShapeDtypeStruct((27, 8, 32), F32), "v"
    grad_one, grad_two = call(
        functools.partial(final_kernel, factor), "final_sum", (planes, own, grad_input), "vvh", [result, result]
    )
    shape = lambda g: g.transpose(2, 0, 1).reshape(32, 3, 3, 3, 8)
    return grad_input[None], shape(grad_one), shape(grad_two)


def solution(mesh):
    fine = Mesh(mesh.devices.reshape(SIZES), AX)
    clip = ("z", "y")
    placed = P(clip, None, "ha", ("xh", "core"), None)
    weight = P(("ha", "xh", "core"), None, None, None, clip)
    return jax.shard_map(
        shards,
        mesh=fine,
        in_specs=(placed, placed, placed, P(), P(), P(), P(clip)),
        out_specs=(placed, weight, weight),
        check_vma=False,
    )
```
